32 devices in a mesh: batch: 8 (over z, x), tm: 4 (over y, core).
Axes of the slice: x: 2, y: 2, z: 4, core: 2. Of those that a mesh axis runs over, the one named last changes fastest.
Arguments:
- input_small: bfloat16 [16, 4, 7, 7, 512], P('batch', 'tm'), may hold values from -15 to 15
- input_large: bfloat16 [16, 4, 10, 10, 512], P('batch', 'tm'), may hold values from -15 to 15
- spatial_one: bfloat16 [9, 512, 1152], P(None, ('batch', 'tm')), may hold values from -0.09375 to 0.09375
- temporal_one: bfloat16 [3, 1152, 512], P(None, None, ('batch', 'tm')), may hold values from -0.109375 to 0.109375
- spatial_two: bfloat16 [9, 512, 1152], P(None, ('batch', 'tm')), may hold values from -0.09375 to 0.09375
- temporal_two: bfloat16 [3, 1152, 512], P(None, None, ('batch', 'tm')), may hold values from -0.109375 to 0.109375
- mid_gain: float32 [2, 1152], replicated, may hold values from 0.1 to 1.9
- mid_shift: float32 [2, 1152], replicated, may hold values from -3 to 3
- out_gain: float32 [2, 512], replicated, may hold values from 0.1 to 1.9
- out_shift: float32 [2, 512], replicated, may hold values from -3 to 3
- cotangent_small: bfloat16 [16, 4, 7, 7, 512], P('batch', 'tm'), may hold values from -6 to 6
- cotangent_large: bfloat16 [16, 4, 10, 10, 512], P('batch', 'tm'), may hold values from -6 to 6
Outputs:
- output_small: bfloat16 [16, 4, 7, 7, 512], P('batch', 'tm')
- output_large: bfloat16 [16, 4, 10, 10, 512], P('batch', 'tm')
- grad_small: float32 [16, 4, 7, 7, 512], P('batch', 'tm')
- grad_large: float32 [16, 4, 10, 10, 512], P('batch', 'tm')
- grad_spatial_one: float32 [9, 512, 1152], P(None, ('batch', 'tm'))
- grad_temporal_one: float32 [3, 1152, 512], P(None, None, ('batch', 'tm'))
- grad_spatial_two: float32 [9, 512, 1152], P(None, ('batch', 'tm'))
- grad_temporal_two: float32 [3, 1152, 512], P(None, None, ('batch', 'tm'))
- grad_mid_gain: float32 [2, 1152], replicated
- grad_mid_shift: float32 [2, 1152], replicated
- grad_out_gain: float32 [2, 512], replicated
- grad_out_shift: float32 [2, 512], replicated
The draws below stay inside these ranges and needn't reach their ends.
All inputs are finite; a program needn't handle non-finite values.
Results may differ from the reference program's by a relative error of at most 0.025.
Values may be sent and summed in bfloat16 or wider, within the bound.
No kernel may reach another device: no remote copies, remote signals or barrier semaphores. Data moves between devices by JAX's collectives and lax.ppermute only.
A program may use at most 320 MiB of HBM per device.

```python
import jax
import jax.numpy as jnp
from jax import lax

C = 512
MID = 1152
FRAMES = 4
SIDE_A = 7
SIDE_B = 10
CLIPS_A = 16
CLIPS_B = 16


def shape_clips(key, base):
    clips = base.shape[0]
    frames = base.shape[1]
    offset = 0.5 * jnp.clip(jax.random.normal(key, (clips, 1, 1, 1, base.shape[4]), jnp.float32), -2.0, 2.0)
    along = jnp.arange(clips, dtype=jnp.float32) / max(clips - 1, 1)
    timing = jnp.arange(frames, dtype=jnp.float32) / max(frames - 1, 1)
    scale = (3.0 ** along)[:, None, None, None, None] * (3.0 ** (timing - 1.0))[None, :, None, None, None]
    return scale * (base + offset)


def draw_input_small(key, part):
    key = jax.random.fold_in(key, 11)
    base_key, shift_key = jax.random.split(key)
    shape = (CLIPS_A, FRAMES, SIDE_A, SIDE_A, C)
    base = jnp.clip(jax.random.normal(base_key, shape, jnp.float32), -4.0, 4.0)
    return shape_clips(shift_key, base).astype(jnp.bfloat16)


def draw_input_large(key, part):
    key = jax.random.fold_in(key, 23)
    base_key, shift_key = jax.random.split(key)
    shape = (CLIPS_B, FRAMES, SIDE_B, SIDE_B, C)
    base = jnp.clip(jax.random.normal(base_key, shape, jnp.float32), -4.0, 4.0)
    return shape_clips(shift_key, base).astype(jnp.bfloat16)


def levels(own_key, dims, pieces, smallest, high):
    level = 1.0
    for axis_at, blocks in pieces:
        steps = jax.random.uniform(jax.random.fold_in(jax.random.fold_in(own_key, 6), axis_at), (blocks,), jnp.float32, smallest / len(pieces), high / len(pieces))
        level = level * jnp.repeat(jnp.exp(steps), dims[axis_at] // blocks).reshape((-1,) + (1,) * (len(dims) - 1 - axis_at))
    return level


def centred(rng, shape, scale, limit, cuts=(), kind=jnp.bfloat16):
    drawn = jax.random.normal(rng, shape, jnp.float32) * scale
    if len(cuts) > 0:
        drawn = levels(rng, shape, cuts, -0.22, 0.18) * drawn
    return jnp.clip(drawn, min=-limit, max=limit).astype(kind)


def setup_inputs(seed: int = 0) -> dict:
    arg_keys = jax.random.split(jax.random.key(seed), 13)
    return {
        "input_small": draw_input_small(jax.random.fold_in(arg_keys[12], 71), 0),
        "input_large": draw_input_large(jax.random.fold_in(arg_keys[12], 71), 0),
        "spatial_one": centred(arg_keys[2], (9, C, MID), (9 * C) ** -0.5, 0.09375, ((1, 32),)),
        "temporal_one": centred(arg_keys[3], (3, MID, C), (3 * MID) ** -0.5, 0.109375, ((2, 32),)),
        "spatial_two": centred(arg_keys[4], (9, C, MID), (9 * C) ** -0.5, 0.09375, ((1, 32),)),
        "temporal_two": centred(arg_keys[5], (3, MID, C), (3 * MID) ** -0.5, 0.109375, ((2, 32),)),
        "mid_gain": jnp.clip(1.0 + 0.18 * jax.random.normal(arg_keys[6], (2, MID), jnp.float32), 0.1, 1.9),
        "mid_shift": centred(arg_keys[7], (2, MID), 0.5, 3.0, (), jnp.float32),
        "out_gain": jnp.clip(1.0 + 0.18 * jax.random.normal(arg_keys[8], (2, C), jnp.float32), 0.1, 1.9),
        "out_shift": centred(arg_keys[9], (2, C), 0.5, 3.0, (), jnp.float32),
        "cotangent_small": centred(arg_keys[10], (CLIPS_A, FRAMES, SIDE_A, SIDE_A, C), 1.0, 6.0, ((0, 8), (1, 4))),
        "cotangent_large": centred(arg_keys[11], (CLIPS_B, FRAMES, SIDE_B, SIDE_B, C), 1.0, 6.0, ((0, 8), (1, 4))),
    }


EPS = 1e-05
HIGH = lax.Precision.HIGHEST

@jax.custom_vjp
def low(v):
    return lax.optimization_barrier(v.astype(jnp.bfloat16)).astype(jnp.float32)

@jax.custom_vjp
def low_back(v):
    return v

def low_keep(v):
    return (low(v), None)

def low_pass(kept, grad):
    return (grad,)

def back_keep(v):
    return (v, None)

def back_low(kept, grad):
    return (low(grad),)
low.defvjp(low_keep, low_pass)
low_back.defvjp(back_keep, back_low)

def spatial(value, kernel):
    height = value.shape[2]
    width = value.shape[3]
    padded = jnp.pad(value, ((0, 0), (0, 0), (1, 1), (1, 1), (0, 0)))
    total = jnp.zeros(value.shape[:4] + (kernel.shape[2],), jnp.float32)
    for i in range(3):
        for j in range(3):
            total = total + jnp.einsum('nfhwc,cm->nfhwm', padded[:, :, i:i + height, j:j + width], kernel[3 * i + j], precision=HIGH)
    return total

def temporal(value, kernel):
    frames = value.shape[1]
    padded = jnp.pad(value, ((0, 0), (1, 1), (0, 0), (0, 0), (0, 0)))
    total = jnp.zeros(value.shape[:4] + (kernel.shape[2],), jnp.float32)
    for k in range(3):
        total = total + jnp.einsum('nfhwm,mc->nfhwc', padded[:, k:k + frames], kernel[k], precision=HIGH)
    return total

def normalize(parts, gain, shift):
    counted = sum((p.size // p.shape[-1] for p in parts))
    totals = sum((lax.optimization_barrier(jnp.sum(p, axis=(0, 1, 2, 3))) for p in parts))
    squares = sum((lax.optimization_barrier(jnp.sum(p * p, axis=(0, 1, 2, 3))) for p in parts))
    average = totals / counted
    spread = squares / counted - average * average
    inverse = lax.rsqrt(spread + EPS)
    return [gain * ((p - average) * inverse) + shift for p in parts]

def forward(input_small, input_large, spatial_one, temporal_one, spatial_two, temporal_two, mid_gain, mid_shift, out_gain, out_shift):
    inputs = [input_small, input_large]
    first = [low_back(spatial(v, spatial_one)) for v in inputs]
    act_one = [low_back(low(jax.nn.silu(h))) for h in normalize(first, mid_gain[0], mid_shift[0])]
    time_one = [low_back(low(temporal(v, temporal_one))) for v in act_one]
    middle = [low(jax.nn.silu(h)) for h in normalize(time_one, out_gain[0], out_shift[0])]
    second = [low_back(spatial(v, spatial_two)) for v in middle]
    act_two = [low_back(low(jax.nn.silu(h))) for h in normalize(second, mid_gain[1], mid_shift[1])]
    time_two = [low_back(low(temporal(v, temporal_two))) for v in act_two]
    branch = normalize(time_two, out_gain[1], out_shift[1])
    return (jax.nn.silu(inputs[0] + branch[0]), jax.nn.silu(inputs[1] + branch[1]))

def reference(input_small, input_large, spatial_one, temporal_one, spatial_two, temporal_two, mid_gain, mid_shift, out_gain, out_shift, cotangent_small, cotangent_large):
    floats = [input_small, input_large, spatial_one, temporal_one, spatial_two, temporal_two, mid_gain, mid_shift, out_gain, out_shift]
    floats = [v.astype(jnp.float32) for v in floats]
    outputs, pullback = jax.vjp(forward, *floats)
    grads = pullback((cotangent_small.astype(jnp.float32), cotangent_large.astype(jnp.float32)))
    return (outputs[0].astype(jnp.bfloat16), outputs[1].astype(jnp.bfloat16), grads[0], grads[1], grads[2], grads[3], grads[4], grads[5], grads[6], grads[7], grads[8], grads[9])
```

```python
import jax
import jax.numpy as jnp
from jax import lax
from jax.sharding import PartitionSpec as P

EPS = 1e-05
F32 = jnp.float32
BF16 = jnp.bfloat16


def swap(value, axis, bit):
    n = lax.axis_size(axis)
    return lax.ppermute(value, axis, [(i, i ^ bit) for i in range(n)])


def batch_sum(value):
    n = lax.axis_size("batch")
    copies = jnp.broadcast_to(value[None], (n,) + value.shape)
    return jnp.sum(lax.all_to_all(copies, "batch", 0, 0, tiled=True), axis=0)


def tm_bits():
    t = lax.axis_index("tm")
    return t % 2, t // 2


def pair(first, second, bit):
    return jnp.where(bit == 0, jnp.stack([first, second]), jnp.stack([second, first]))


def halves(value, bit):
    h = value.shape[0] // 2
    mine = lax.dynamic_slice_in_dim(value, bit * h, h, 0)
    other = lax.dynamic_slice_in_dim(value, (1 - bit) * h, h, 0)
    return mine, other


def gather_tm(value):
    core, y = tm_bits()
    both = pair(value, swap(value, "tm", 2), y)
    all4 = pair(both, swap(both, "tm", 1), core)
    return jnp.swapaxes(all4, 0, 1).reshape((4,) + value.shape)


def sum_tm(value):
    core, y = tm_bits()
    mine, other = halves(value, core)
    mine = (mine + swap(other.astype(BF16), "tm", 1).astype(F32)).astype(BF16)
    mine = (mine.astype(F32) + swap(mine, "tm", 2).astype(F32)).astype(BF16)
    return pair(mine, swap(mine, "tm", 1), core).reshape(value.shape)


def scatter_tm(value):
    core, y = tm_bits()
    v = value.reshape((2, 2) + value.shape[1:])
    v = jnp.swapaxes(v, 0, 1)
    mine = lax.dynamic_index_in_dim(v, core, 0, keepdims=False)
    other = lax.dynamic_index_in_dim(v, 1 - core, 0, keepdims=False)
    mine = mine + swap(other.astype(BF16), "tm", 1).astype(F32)
    own = lax.dynamic_index_in_dim(mine, y, 0, keepdims=False)
    away = lax.dynamic_index_in_dim(mine, 1 - y, 0, keepdims=False)
    return own + swap(away.astype(BF16), "tm", 2).astype(F32)


DN = ("HWNC", "HWIO", "HWNC")


def conv(x, k):
    return lax.conv_general_dilated(
        x, k, (1, 1), "SAME", dimension_numbers=DN, preferred_element_type=F32
    )


def conv_weight_grad(x, g):
    return lax.conv_general_dilated(
        x, g, (1, 1), ((1, 1), (1, 1)), dimension_numbers=("HWNC"[:2] + "CN", "HWIO", "HWNC"),
        preferred_element_type=F32,
    )


class Shapes:
    def __init__(self, small, large):
        self.hs, self.hl = small, large
        self.ns, self.nl = small * small, large * large

    def split(self, rows):
        c = rows.shape[-1]
        n = rows.shape[0] // (self.ns + self.nl)
        cut = self.ns * n
        return (
            rows[:cut].reshape(self.hs, self.hs, n, c),
            rows[cut:].reshape(self.hl, self.hl, n, c),
        )

    @staticmethod
    def join(parts):
        return jnp.concatenate([p.reshape(-1, p.shape[-1]) for p in parts])


def conv_forward(shapes, rows, kernel):
    return shapes.join([conv(p, kernel) for p in shapes.split(rows)])


def conv_backward_input(shapes, rows, kernel):
    flipped = jnp.swapaxes(jnp.flip(kernel, (0, 1)), 2, 3)
    return shapes.join([conv(p, flipped) for p in shapes.split(rows)])


def conv_backward_kernel(shapes, rows, grads):
    out = 0.0
    for x, g in zip(shapes.split(rows), shapes.split(grads)):
        out = out + lax.conv_general_dilated(
            x, g, (1, 1), ((1, 1), (1, 1)), dimension_numbers=("HWCN", "HWIO", "HWNC"),
            preferred_element_type=F32,
        )
    return out


def frames_shifted(rows, frames, by):
    c = rows.shape[-1]
    v = rows.reshape(-1, frames, c)
    if by == 1:
        v = jnp.concatenate([v[:, 1:], jnp.zeros_like(v[:, :1])], axis=1)
    elif by == -1:
        v = jnp.concatenate([jnp.zeros_like(v[:, :1]), v[:, :-1]], axis=1)
    return v.reshape(-1, c)


def sums(a, b):
    return jnp.stack([jnp.sum(a, axis=0), jnp.sum(b, axis=0)])


def stats_of(rows, counted):
    s = batch_sum(sums(rows, rows * rows)) / counted
    mean = s[0]
    return mean, lax.rsqrt(s[1] - mean * mean + EPS)


def slope(v):
    sig = jax.nn.sigmoid(v)
    return sig * (1.0 + v * (1.0 - sig))


def norm_back(e, xhat, gain, inverse, counted):
    s = batch_sum(sums(e * xhat, e))
    dgain, dshift = s[0], s[1]
    dv = gain * inverse * (e - (dshift + xhat * dgain) / counted)
    return dv, dgain, dshift


def fetch_kernels(spatial, temporal):
    both = jnp.concatenate([spatial, jnp.swapaxes(temporal, 1, 2)], axis=0)
    n = lax.axis_size("tm")
    k, r, m = both.shape
    moved = lax.all_to_all(both, "tm", split_axis=2, concat_axis=1, tiled=True)
    whole = lax.all_gather(moved, "batch", axis=0)
    whole = jnp.swapaxes(whole, 0, 1).reshape(k, -1, m // n)
    return whole[:9], whole[9:]


def return_kernels(grad_s, grad_t):
    both = jnp.concatenate([grad_s, grad_t], axis=0).astype(BF16)
    k, c, m = both.shape
    nb, nt = lax.axis_size("batch"), lax.axis_size("tm")
    own = c // (nb * nt)
    pieces = jnp.swapaxes(both.reshape(k, nb * nt, own, m), 0, 1)
    moved = lax.all_to_all(pieces, ("batch", "tm"), 0, 0, tiled=True)
    moved = moved.reshape(nb, nt, k, own, m)
    summed = jnp.sum(moved.astype(F32), axis=0)
    summed = jnp.moveaxis(summed, 0, 2).reshape(k, own, nt * m)
    return summed[:9], jnp.swapaxes(summed[9:], 1, 2)


def body(
    input_small, input_large, spatial_one, temporal_one, spatial_two, temporal_two,
    mid_gain, mid_shift, out_gain, out_shift, cotangent_small, cotangent_large,
):
    clips = input_small.shape[0]
    frames = lax.axis_size("tm")
    shapes = Shapes(input_small.shape[2], input_large.shape[2])
    places = shapes.ns + shapes.nl
    counted = float(places * clips * frames * lax.axis_size("batch"))
    t = lax.axis_index("tm")

    def to_rows(small, large):
        out = []
        for v in (small, large):
            v = v[:, 0].reshape(clips, -1, v.shape[-1])
            out.append(jnp.swapaxes(v, 0, 1).reshape(-1, v.shape[-1]))
        return jnp.concatenate(out)

    def from_rows(rows):
        v = jnp.swapaxes(rows.reshape(places, clips, -1), 0, 1)
        s = v[:, : shapes.ns].reshape(clips, 1, shapes.hs, shapes.hs, -1)
        l = v[:, shapes.ns :].reshape(clips, 1, shapes.hl, shapes.hl, -1)
        return s, l

    def whole_rows(rows):
        g = gather_tm(rows)
        return jnp.moveaxis(g, 0, 1).reshape(-1, rows.shape[-1])

    def frame_pieces(rows):
        return jnp.moveaxis(rows.reshape(-1, frames, rows.shape[-1]), 1, 0)

    k_sa, k_ta = fetch_kernels(spatial_one, temporal_one)
    k_sb, k_tb = fetch_kernels(spatial_two, temporal_two)
    mid = k_sa.shape[2]
    chans = k_sa.shape[1]
    k_sa = k_sa.reshape(3, 3, chans, mid)
    k_sb = k_sb.reshape(3, 3, chans, mid)

    def mine(v):
        return lax.dynamic_slice_in_dim(v, t * mid, mid, 0)

    x = whole_rows(to_rows(input_small, input_large))
    cot = whole_rows(to_rows(cotangent_small, cotangent_large))

    def temporal(a, k):
        y = lax.dot_general(a, k.reshape(3 * chans, mid), (((1,), (1,)), ((), ())), preferred_element_type=F32)
        return (
            frames_shifted(y[:, :chans], frames, -1)
            + y[:, chans : 2 * chans]
            + frames_shifted(y[:, 2 * chans :], frames, 1)
        )

    def temporal_back(a, g, k):
        wide = jnp.concatenate(
            [frames_shifted(g, frames, 1), g, frames_shifted(g, frames, -1)], axis=1
        )
        da = lax.dot_general(wide, k.reshape(3 * chans, mid), (((1,), (0,)), ((), ())), preferred_element_type=F32)
        dk = lax.dot_general(wide, a, (((0,), (0,)), ((), ())), preferred_element_type=F32)
        return da.astype(BF16), dk.reshape(3, chans, mid)

    def forward_half(x, ks, kt, gm, sm, go, so):
        s1 = conv_forward(shapes, x, ks)
        m1, r1 = stats_of(s1, counted)
        xh1 = (s1 - m1) * r1
        p1 = gm * xh1 + sm
        a1 = jax.nn.silu(p1).astype(BF16)
        t1 = sum_tm(temporal(a1, kt)).astype(F32)
        m2, r2 = stats_of(t1, counted)
        xh2 = (t1 - m2) * r2
        p2 = go * xh2 + so
        return (xh1, p1, r1, a1), (xh2, p2, r2)

    gm0, gm1, sm0, sm1 = mine(mid_gain[0]), mine(mid_gain[1]), mine(mid_shift[0]), mine(mid_shift[1])
    (xh1, p1, r1, a1), (xh2, p2, r2) = forward_half(x, k_sa, k_ta, gm0, sm0, out_gain[0], out_shift[0])
    b1 = jax.nn.silu(p2).astype(BF16)
    (xh3, p3, r3, a2), (xh4, p4, r4) = forward_half(b1, k_sb, k_tb, gm1, sm1, out_gain[1], out_shift[1])
    pre = x.astype(F32) + p4
    dpre = cot.astype(F32) * slope(pre)
    own_pre = lax.dynamic_index_in_dim(frame_pieces(pre), t, 0, keepdims=False)
    own_dpre = lax.dynamic_index_in_dim(frame_pieces(dpre), t, 0, keepdims=False)
    out_s, out_l = from_rows(jax.nn.silu(own_pre).astype(BF16))

    dt2, dg4, ds4 = norm_back(dpre, xh4, out_gain[1], r4, counted)
    da2, dk_tb = temporal_back(a2, dt2.astype(BF16), k_tb)
    e3 = da2.astype(F32) * slope(p3)
    ds2, dg3, ds3 = norm_back(e3, xh3, gm1, r3, counted)
    ds2 = ds2.astype(BF16)
    dk_sb = conv_backward_kernel(shapes, b1, ds2).reshape(9, chans, mid)
    grad_sb, grad_tb = return_kernels(dk_sb, dk_tb)
    db1 = sum_tm(conv_backward_input(shapes, ds2, k_sb)).astype(F32)
    e2 = db1 * slope(p2)
    dt1, dg2, ds2_ = norm_back(e2, xh2, out_gain[0], r2, counted)
    da1, dk_ta = temporal_back(a1, dt1.astype(BF16), k_ta)
    e1 = da1.astype(F32) * slope(p1)
    ds1, dg1, ds1_ = norm_back(e1, xh1, gm0, r1, counted)
    ds1 = ds1.astype(BF16)
    dk_sa = conv_backward_kernel(shapes, x, ds1).reshape(9, chans, mid)
    grad_sa, grad_ta = return_kernels(dk_sa, dk_ta)
    din = scatter_tm(frame_pieces(conv_backward_input(shapes, ds1, k_sa)))
    grad_s, grad_l = from_rows(own_dpre + din)

    mids = lax.all_gather(jnp.stack([dg1, dg3, ds1_, ds3]), "tm", axis=1, tiled=True)
    return (
        out_s, out_l, grad_s, grad_l, grad_sa, grad_ta, grad_sb, grad_tb,
        mids[:2], mids[2:], jnp.stack([dg2, dg4]), jnp.stack([ds2_, ds4]),
    )


def solution(mesh):
    act = P("batch", "tm", None, None, None)
    rows = P(None, ("batch", "tm"), None)
    cols = P(None, None, ("batch", "tm"))
    return jax.shard_map(
        body,
        mesh=mesh,
        in_specs=(act, act, rows, cols, rows, cols, P(), P(), P(), P(), act, act),
        out_specs=(act, act, act, act, rows, cols, rows, cols, P(), P(), P(), P()),
        check_vma=False,
    )
```

```python
import functools

import jax
import jax.numpy as jnp
from jax import lax
from jax.experimental import pallas as pl
from jax.experimental.pallas import tpu as pltpu
from jax.sharding import PartitionSpec as P

EPS = 1e-05
F32 = jnp.float32
BF16 = jnp.bfloat16
VMEM_LIMIT = 40 * 1024 * 1024


def swap(value, axis, bit):
    n = lax.axis_size(axis)
    return lax.ppermute(value, axis, [(i, i ^ bit) for i in range(n)])


def shared(copies):
    return lax.all_to_all(copies, "batch", 0, 0, tiled=True)


def tm_bits():
    t = lax.axis_index("tm")
    return t % 2, t // 2


def pair(first, second, bit):
    return jnp.where(bit == 0, jnp.stack([first, second]), jnp.stack([second, first]))


def gather_tm(value):
    core, y = tm_bits()
    both = pair(value, swap(value, "tm", 2), y)
    all4 = pair(both, swap(both, "tm", 1), core)
    return jnp.swapaxes(all4, 0, 1).reshape((4,) + value.shape)


def sum_tm(mine, other):
    mine = (mine.astype(F32) + swap(other, "tm", 1).astype(F32)).astype(BF16)
    mine = (mine.astype(F32) + swap(mine, "tm", 2).astype(F32)).astype(BF16)
    return mine, swap(mine, "tm", 1)


def scatter_tm(value):
    core, y = tm_bits()
    v = value.reshape((2, 2) + value.shape[1:])
    v = jnp.swapaxes(v, 0, 1)
    mine = lax.dynamic_index_in_dim(v, core, 0, keepdims=False)
    other = lax.dynamic_index_in_dim(v, 1 - core, 0, keepdims=False)
    mine = mine + swap(other.astype(BF16), "tm", 1).astype(F32)
    own = lax.dynamic_index_in_dim(mine, y, 0, keepdims=False)
    away = lax.dynamic_index_in_dim(mine, 1 - y, 0, keepdims=False)
    return own + swap(away.astype(BF16), "tm", 2).astype(F32)


def n_tiles(offsets):
    return 2 * offsets + -(-offsets // 4)


def tiled(x):
    k, p, _ = x.shape
    q = -(-k // 4)
    main = x[:, :, :1024].reshape(k, p, 4, 2, 128)
    main = jnp.transpose(main, (2, 0, 3, 1, 4)).reshape(4, 2 * k, p, 128)
    rest = jnp.pad(x[:, :, 1024:], ((0, 4 * q - k), (0, 0), (0, 0))).reshape(q, 4, p, 4, 32)
    rest = jnp.transpose(rest, (3, 0, 2, 1, 4)).reshape(4, q, p, 128)
    return jnp.concatenate([main, rest], axis=1)


def untiled(y, k):
    p = y.shape[2]
    q = -(-k // 4)
    main = jnp.transpose(y[:, : 2 * k].reshape(4, k, 2, p, 128), (1, 3, 0, 2, 4)).reshape(k, p, 1024)
    rest = y[:, 2 * k :].reshape(4, q, p, 4, 32)
    rest = jnp.transpose(rest, (1, 3, 2, 0, 4)).reshape(4 * q, p, 128)[:k]
    return jnp.concatenate([main, rest], axis=2)


def pack(spatials, temporals):
    p = (spatials + [t.swapaxes(1, 2) for t in temporals])[0].shape[1]
    if p % 16:
        return jnp.concatenate(
            [tiled(v) for v in spatials] + [tiled(jnp.swapaxes(v, 1, 2)) for v in temporals], axis=1
        )
    ns = len(spatials)
    total = ns * n_tiles(9) + len(temporals) * n_tiles(3)

    def body(*refs):
        out_ref = refs[-1]
        at = 0
        for n, ref in enumerate(refs[:-1]):
            k = ref.shape[0]
            rows = []
            for o in range(k):
                v = ref[o].astype(F32)
                rows.append(v if n < ns else v.T)
            for t in range(4):
                for o in range(k):
                    for h in range(2):
                        lane = 256 * t + 128 * h
                        out_ref[t, at + 2 * o + h] = rows[o][:, lane : lane + 128].astype(BF16)
                for q in range(-(-k // 4)):
                    group = lax.broadcasted_iota(jnp.int32, (p, 128), 1) // 32
                    tile = jnp.zeros((p, 128), F32)
                    for r in range(4):
                        if 4 * q + r < k:
                            moved = pltpu.roll(rows[4 * q + r][:, 1024:], (32 * (r - t)) % 128, 1)
                            tile = jnp.where(group == r, moved, tile)
                    out_ref[t, at + 2 * k + q] = tile.astype(BF16)
            at += n_tiles(k)

    return call(body, "pack", [struct((4, total, p, 128), BF16)], [], *spatials, *temporals)[0]


def spread_tm(packed):
    t = lax.axis_index("tm")
    got = []
    for s in range(4):
        piece = lax.dynamic_index_in_dim(packed, t ^ s, 0, keepdims=False)
        got.append(swap(piece, "tm", s) if s else piece)
    got = jnp.stack(got)
    return jnp.stack([lax.dynamic_index_in_dim(got, t ^ s, 0, keepdims=False) for s in range(4)])


def blocks(whole):
    nb, nt, tiles, p, _ = whole.shape
    if p % 16 == 0:
        return whole.reshape(nb * nt, tiles, p, 128)
    v = jnp.moveaxis(whole.reshape(2, nb * nt // 2, tiles, p, 128), 2, 1)
    return v.reshape(2, tiles, nb * nt // 2 * p, 128)


def gather_batch(moved):
    return blocks(lax.all_gather(moved, "batch", axis=0))


def owners(grads, nb, nt):
    nblk, tiles, p, _ = grads.shape
    if nblk == nb * nt:
        return grads.reshape(nb, nt, tiles, p, 128)
    own = nblk * p // (nb * nt)
    v = grads.reshape(nblk, tiles, nb * nt // nblk, own, 128)
    return jnp.moveaxis(v, 2, 1).reshape(nb, nt, tiles, own, 128)


def unpack(parts, spatials, temporals):
    n, _, total, p, _ = parts.shape
    ks = [9] * spatials + [3] * temporals
    if p % 16:
        summed = jnp.sum(parts.astype(F32), axis=0)
        out, at = [], 0
        for m, k in enumerate(ks):
            v = untiled(summed[:, at : at + n_tiles(k)], k)
            out.append(v if m < spatials else jnp.swapaxes(v, 1, 2))
            at += n_tiles(k)
        return out

    def body(in_ref, *outs):
        group = lax.broadcasted_iota(jnp.int32, (p, 128), 1) // 32

        def tile(t, i):
            v = in_ref[0, t, i].astype(F32)
            for m in range(1, n):
                v = v + in_ref[m, t, i].astype(F32)
            return v

        at = 0
        for m, (k, out_ref) in enumerate(zip(ks, outs)):
            rest = [[tile(t, at + 2 * k + q) for t in range(4)] for q in range(-(-k // 4))]
            for o in range(k):
                pieces = [tile(t, at + 2 * o + h) for t in range(4) for h in range(2)]
                last = jnp.zeros((p, 128), F32)
                for t in range(4):
                    moved = pltpu.roll(rest[o // 4][t], (32 * (t - o % 4)) % 128, 1)
                    last = jnp.where(group == t, moved, last)
                whole = jnp.concatenate(pieces + [last], axis=1)
                out_ref[o] = whole if m < spatials else whole.T
            at += n_tiles(k)

    outs = [struct((9, p, 1152) if m < spatials else (3, 1152, p), F32) for m in range(len(ks))]
    return call(body, "unpack", outs, [], parts)


def channels(v, t):
    main = lax.dynamic_slice_in_dim(v, 256 * t, 256, v.ndim - 1)
    rest = lax.dynamic_slice_in_dim(v, 1024 + 32 * t, 32, v.ndim - 1)
    return jnp.concatenate([main] + [rest] * 4, axis=-1)


def all_channels(v):
    main = jnp.moveaxis(v[..., :256], 0, -2)
    rest = jnp.moveaxis(v[..., 256:288], 0, -2)
    lead = main.shape[:-2]
    return jnp.concatenate([main.reshape(lead + (-1,)), rest.reshape(lead + (-1,))], axis=-1)


class Sizes:
    def __init__(self, hs, hl, group, frames, nb, counted):
        self.hs, self.hl, self.group, self.frames, self.nb = hs, hl, group, frames, nb
        self.ns, self.nl = hs * hs, hl * hl
        self.cut = self.ns * group
        self.rows = (self.ns + self.nl) * group
        self.counted = counted


def call(body, name, outs, scratch, *args, flops=0):
    smem = pl.BlockSpec(memory_space=pltpu.SMEM)
    vmem = pl.BlockSpec(memory_space=pltpu.VMEM)
    moved = sum(a.size * a.dtype.itemsize for a in args) + sum(
        o.size * o.dtype.itemsize for o in outs
    )
    return pl.pallas_call(
        body,
        out_shape=outs,
        in_specs=[smem if a.dtype == jnp.int32 else vmem for a in args],
        out_specs=[vmem] * len(outs),
        scratch_shapes=scratch,
        name=name,
        compiler_params=pltpu.CompilerParams(vmem_limit_bytes=VMEM_LIMIT),
        cost_estimate=pl.CostEstimate(flops=flops, bytes_accessed=moved, transcendentals=0),
    )(*args)


def struct(shape, dtype):
    return jax.ShapeDtypeStruct(shape, dtype)


def moments(ar_ref, counted):
    s = jnp.sum(ar_ref[...], axis=0)
    mean = s[0:1] / counted
    return mean, lax.rsqrt(s[1:2] / counted - mean * mean + EPS)


def put_sums(out_ref, first, second):
    both = jnp.concatenate(
        [jnp.sum(first, axis=0, keepdims=True), jnp.sum(second, axis=0, keepdims=True)], axis=0
    )
    out_ref[...] = jnp.broadcast_to(both[None], out_ref.shape)


def sigmoid(v):
    return 1.0 / (1.0 + jnp.exp(-v))


def slope(v):
    sig = sigmoid(v)
    return sig * (1.0 + v * (1.0 - sig))


def ordered(core_ref, mine_ref, other_ref):
    first = core_ref[0] == 0
    mine, other = mine_ref[...].astype(F32), other_ref[...].astype(F32)
    return jnp.concatenate([jnp.where(first, mine, other), jnp.where(first, other, mine)], axis=1)


def fill(sz, rows, small_ref, large_ref):
    c = rows.shape[1]
    for ref, h, v in (
        (small_ref, sz.hs, rows[: sz.cut]),
        (large_ref, sz.hl, rows[sz.cut :]),
    ):
        ref[...] = jnp.zeros(ref.shape, F32)
        ref[1 : h + 1, 1 : h + 1] = v.reshape(h, h, sz.group, c)


def window(sz, small_ref, large_ref, i, j, lanes):
    c = lanes.stop - lanes.start
    s = small_ref[i : i + sz.hs, j : j + sz.hs, :, lanes].reshape(sz.cut, c)
    l = large_ref[i : i + sz.hl, j : j + sz.hl, :, lanes].reshape(sz.rows - sz.cut, c)
    return jnp.concatenate([s, l], axis=0)


def tile(k_ref, n, half=None):
    nblk, _, p, lanes = k_ref.shape
    if half is None:
        return k_ref[:, n].reshape(nblk * p, lanes)
    return k_ref[pl.ds(half * (nblk // 2), nblk // 2), n].reshape(nblk // 2 * p, lanes)


def tiles(k_ref, ns, half=None):
    return jnp.concatenate([tile(k_ref, n, half) for n in ns], axis=1)


def lane_group(v):
    return lax.broadcasted_iota(jnp.int32, (1, v.shape[1]), 1) // 32


def folded(v):
    v = v + pltpu.roll(v, 32, 1)
    return v + pltpu.roll(v, 64, 1)


def picked(first, rest):
    out = first
    for r, v in enumerate(rest):
        out = jnp.where(lane_group(first) == r + 1, v, out)
    return out


def conv_rows(sz, xb, small, large, ysmall, ylarge, k_ref, base):
    c = xb.shape[1]
    every = slice(0, c)
    main = None
    for i in range(3):
        left = jnp.concatenate(
            [window(sz, small, large, i, j, every).astype(BF16) for j in range(3)], axis=1
        )
        right = jnp.concatenate(
            [tiles(k_ref, (base + 6 * i + 2 * j, base + 6 * i + 2 * j + 1)) for j in range(3)], axis=0
        )
        d = jnp.dot(left, right, preferred_element_type=F32)
        main = d if main is None else main + d
    y = jnp.dot(xb, tiles(k_ref, (base + 18, base + 19, base + 20)), preferred_element_type=F32)
    fill(sz, y, ysmall, ylarge)
    rest = window(sz, ysmall, ylarge, 2, 2, slice(256, 384))
    rest = jnp.where(lane_group(rest) == 0, rest, 0.0)
    for q in range(2):
        at = [window(sz, ysmall, ylarge, (4 * q + r) // 3, (4 * q + r) % 3, slice(128 * q, 128 * q + 128)) for r in range(4)]
        rest = rest + picked(at[0], at[1:])
    return jnp.concatenate([main, folded(rest)], axis=1)


def maps(sz, c):
    def one(h):
        return pltpu.VMEM((h + 2, h + 2, sz.group, c), F32)

    return [one(sz.hs), one(sz.hl)]


def first_conv(sz, x, k, base):
    c = x.shape[1]

    def body(x_ref, k_ref, s_ref, sums_ref, small, large, ysmall, ylarge):
        fill(sz, x_ref[...].astype(F32), small, large)
        total = conv_rows(sz, x_ref[...], small, large, ysmall, ylarge, k_ref, base)
        s_ref[...] = total
        put_sums(sums_ref, total, total * total)

    outs = [struct((sz.rows, 384), F32), struct((sz.nb, 2, 384), F32)]
    return call(body, "conv_one", outs, maps(sz, c) + maps(sz, 384), x, k, flops=18 * sz.rows * c * 288)


def second_conv(sz, core, mine, other, ar, gain, shift, k, base):
    c = gain.shape[1]

    def body(core_ref, mine_ref, other_ref, ar_ref, g_ref, h_ref, k_ref, b_ref, s_ref, sums_ref,
             small, large, ysmall, ylarge):
        mean, inv = moments(ar_ref, sz.counted)
        p = g_ref[...] * ((ordered(core_ref, mine_ref, other_ref) - mean) * inv) + h_ref[...]
        b = (p * sigmoid(p)).astype(BF16)
        b_ref[...] = b
        fill(sz, b.astype(F32), small, large)
        total = conv_rows(sz, b, small, large, ysmall, ylarge, k_ref, base)
        s_ref[...] = total
        put_sums(sums_ref, total, total * total)

    outs = [struct((sz.rows, c), BF16), struct((sz.rows, 384), F32), struct((sz.nb, 2, 384), F32)]
    return call(body, "conv_two", outs, maps(sz, c) + maps(sz, 384), core, mine, other, ar, gain, shift, k,
                flops=18 * sz.rows * c * 288)


def frame_shift(sz, v, by):
    if by == 0:
        return v
    c = v.shape[1]
    v = v.reshape(-1, sz.group, c)
    frame = lax.broadcasted_iota(jnp.int32, (1, sz.group, c), 1) % sz.frames
    moved = pltpu.roll(v, (-by) % sz.group, 1)
    inside = (frame + by >= 0) & (frame + by < sz.frames)
    return jnp.where(inside, moved, 0.0).reshape(-1, c)


def norm_temporal(sz, core, s, ar, gain, shift, k, base):
    half = k.shape[0] * k.shape[2] // 2

    def body(core_ref, s_ref, ar_ref, g_ref, h_ref, k_ref, wide_ref, other_ref, mine_ref):
        mean, inv = moments(ar_ref, sz.counted)
        p = g_ref[...] * ((s_ref[...] - mean) * inv) + h_ref[...]
        a = (p * sigmoid(p)).astype(BF16).astype(F32)
        moved = [frame_shift(sz, a, by) for by in (-1, 0, 1)]
        rest = picked(moved[0][:, 256:], [moved[1][:, 256:], moved[2][:, 256:], jnp.zeros_like(a[:, 256:])])
        wide = jnp.concatenate([m[:, :256] for m in moved] + [rest], axis=1).astype(BF16)
        wide_ref[...] = wide
        for out_ref, h in ((other_ref, 1 - core_ref[0]), (mine_ref, core_ref[0])):
            right = tiles(k_ref, range(base, base + 7), h)
            t = lax.dot_general(wide, right, (((1,), (1,)), ((), ())), preferred_element_type=F32)
            out_ref[...] = t.astype(out_ref.dtype)

    outs = [struct((sz.rows, 896), BF16), struct((sz.rows, half), BF16), struct((sz.rows, half), F32)]
    return call(body, "norm_temporal", outs, [], core, s, ar, gain, shift, k,
                flops=6 * sz.rows * 2 * half * 288)


def half_sums(sz, core, mine, other):
    half = mine.shape[1]

    def body(core_ref, mine_ref, other_ref, sums_ref):
        t = ordered(core_ref, mine_ref, other_ref)
        put_sums(sums_ref, t, t * t)

    return call(body, "half_sums", [struct((sz.nb, 2, 2 * half), F32)], [], core, mine, other)[0]


def output_slope(sz, core, mine, other, ar, gain, shift, x, cot):
    c = x.shape[1]

    def body(core_ref, mine_ref, other_ref, ar_ref, g_ref, h_ref, x_ref, cot_ref, out_ref, d_ref, sums_ref):
        mean, inv = moments(ar_ref, sz.counted)
        xhat = (ordered(core_ref, mine_ref, other_ref) - mean) * inv
        pre = x_ref[...].astype(F32) + (g_ref[...] * xhat + h_ref[...])
        sig = sigmoid(pre)
        out_ref[...] = (pre * sig).astype(BF16)
        d = cot_ref[...].astype(F32) * (sig * (1.0 + pre * (1.0 - sig)))
        d_ref[...] = d
        put_sums(sums_ref, d * xhat, d)

    outs = [struct((sz.rows, c), BF16), struct((sz.rows, c), F32), struct((sz.nb, 2, c), F32)]
    return call(body, "output_slope", outs, [], core, mine, other, ar, gain, shift, x, cot)


def middle_slope(sz, core, d_mine, d_other, mine, other, ar, gain, shift):
    c = gain.shape[1]

    def body(core_ref, dm_ref, do_ref, mine_ref, other_ref, ar_ref, g_ref, h_ref, e_ref, sums_ref):
        mean, inv = moments(ar_ref, sz.counted)
        xhat = (ordered(core_ref, mine_ref, other_ref) - mean) * inv
        e = ordered(core_ref, dm_ref, do_ref) * slope(g_ref[...] * xhat + h_ref[...])
        e_ref[...] = e
        put_sums(sums_ref, e * xhat, e)

    outs = [struct((sz.rows, c), F32), struct((sz.nb, 2, c), F32)]
    return call(body, "middle_slope", outs, [], core, d_mine, d_other, mine, other, ar, gain, shift)


def temporal_back(sz, core, e, mine, other, ar, back, gain, s, ar_s, gain_s, shift_s, k, base):
    c = e.shape[1]

    def body(core_ref, e_ref, mine_ref, other_ref, ar_ref, back_ref, g_ref, s_ref, ars_ref, gs_ref, hs_ref,
             k_ref, dt_ref, es_ref, sums_ref, got_ref):
        mean, inv = moments(ar_ref, sz.counted)
        got = jnp.sum(back_ref[...], axis=0)
        got_ref[...] = got
        xhat = (ordered(core_ref, mine_ref, other_ref) - mean) * inv
        d = g_ref[...] * inv * (e_ref[...] - (got[1:2] + xhat * got[0:1]) / sz.counted)
        d = d.astype(BF16)
        dt_ref[...] = d
        d = d.astype(F32)
        left = jnp.concatenate([frame_shift(sz, d, by).astype(BF16) for by in (1, 0, -1)], axis=1)
        right = jnp.concatenate(
            [tiles(k_ref, (base + 2 * n, base + 2 * n + 1)) for n in range(3)], axis=0
        )
        main = jnp.dot(left, right, preferred_element_type=F32)
        y = jnp.dot(dt_ref[...], tile(k_ref, base + 6), preferred_element_type=F32)
        rest = picked(frame_shift(sz, y, 1), [y, frame_shift(sz, y, -1), jnp.zeros_like(y)])
        da = jnp.concatenate([main, folded(rest)], axis=1).astype(BF16).astype(F32)
        mean_s, inv_s = moments(ars_ref, sz.counted)
        xhat_s = (s_ref[...] - mean_s) * inv_s
        es = da * slope(gs_ref[...] * xhat_s + hs_ref[...])
        es_ref[...] = es
        put_sums(sums_ref, es * xhat_s, es)

    outs = [
        struct((sz.rows, c), BF16),
        struct((sz.rows, 384), F32),
        struct((sz.nb, 2, 384), F32),
        struct((2, c), F32),
    ]
    return call(body, "temporal_back", outs, [], core, e, mine, other, ar, back, gain, s, ar_s, gain_s,
                shift_s, k, flops=6 * sz.rows * c * 288)


def norm_back_rows(sz, e_ref, s_ref, ar_ref, back_ref, g_ref):
    mean, inv = moments(ar_ref, sz.counted)
    got = jnp.sum(back_ref[...], axis=0)
    xhat = (s_ref[...] - mean) * inv
    d = g_ref[...] * inv * (e_ref[...] - (got[1:2] + xhat * got[0:1]) / sz.counted)
    return d.astype(BF16).astype(F32), got


def rest_patches(sz, small, large):
    lanes = slice(256, 384)
    out = []
    for q in range(3):
        at = [window(sz, small, large, 2 - o // 3, 2 - o % 3, lanes) for o in range(4 * q, min(4 * q + 4, 9))]
        at += [jnp.zeros_like(at[0])] * (4 - len(at))
        out.append(picked(at[0], at[1:]).astype(BF16))
    return jnp.concatenate(out, axis=1)


def conv_back(sz, core, e, s, ar, back, gain, k, base):
    half = k.shape[0] * k.shape[2] // 2

    def body(core_ref, e_ref, s_ref, ar_ref, back_ref, g_ref, k_ref, other_ref, mine_ref, got_ref,
             small, large):
        d, got = norm_back_rows(sz, e_ref, s_ref, ar_ref, back_ref, g_ref)
        got_ref[...] = got
        fill(sz, d, small, large)
        rest = rest_patches(sz, small, large)
        for out_ref, h in ((other_ref, 1 - core_ref[0]), (mine_ref, core_ref[0])):
            total = None
            for i in range(3):
                left = jnp.concatenate(
                    [window(sz, small, large, 2 - i, 2 - j, slice(0, 256)).astype(BF16) for j in range(3)],
                    axis=1,
                )
                right = tiles(k_ref, range(base + 6 * i, base + 6 * i + 6), h)
                if i == 2:
                    left = jnp.concatenate([left, rest], axis=1)
                    right = jnp.concatenate(
                        [right, tiles(k_ref, range(base + 18, base + 21), h)], axis=1
                    )
                one = lax.dot_general(left, right, (((1,), (1,)), ((), ())), preferred_element_type=F32)
                total = one if total is None else total + one
            out_ref[...] = total.astype(out_ref.dtype)

    outs = [struct((sz.rows, half), BF16), struct((sz.rows, half), F32), struct((2, 384), F32)]
    return call(body, "conv_back", outs, maps(sz, 384), core, e, s, ar, back, gain, k,
                flops=18 * sz.rows * 2 * half * 288)


def put_tiles(out_ref, at, v):
    nblk, _, p, _ = out_ref.shape
    v = v.astype(BF16)
    for n in range(v.shape[1] // 128):
        out_ref[:, at + n] = v[:, 128 * n : 128 * n + 128].reshape(nblk, p, 128)


def conv_kernel_grad(sz, x, e, s, ar, back, gain, nblk, temporal=None):
    c = x.shape[1]
    total = n_tiles(9) + (n_tiles(3) if temporal else 0)

    def body(x_ref, e_ref, s_ref, ar_ref, back_ref, g_ref, *refs):
        out_ref, small, large = refs[-3:]
        d, _ = norm_back_rows(sz, e_ref, s_ref, ar_ref, back_ref, g_ref)
        fill(sz, d, small, large)
        xt = x_ref[...].T
        for o in range(9):
            right = window(sz, small, large, 2 - o // 3, 2 - o % 3, slice(0, 256)).astype(BF16)
            put_tiles(out_ref, 2 * o, jnp.dot(xt, right, preferred_element_type=F32))
        put_tiles(out_ref, 18, jnp.dot(xt, rest_patches(sz, small, large), preferred_element_type=F32))
        if temporal:
            put_tiles(out_ref, 21, jnp.dot(refs[0][...].T, refs[1][...], preferred_element_type=F32))

    outs = [struct((nblk, total, c // nblk, 128), BF16)]
    return call(body, "conv_kernel_grad", outs, maps(sz, 384), x, e, s, ar, back, gain,
                *(temporal or ()), flops=18 * sz.rows * c * 288)[0]


def temporal_kernel_grad(dt, wide, nblk):
    c = dt.shape[1]

    def body(dt_ref, wide_ref, out_ref):
        put_tiles(out_ref, 0, jnp.dot(dt_ref[...].T, wide_ref[...], preferred_element_type=F32))

    outs = [struct((nblk, n_tiles(3), c // nblk, 128), BF16)]
    return call(body, "temporal_kernel_grad", outs, [], dt, wide, flops=2 * dt.size * wide.shape[1])[0]


def body(
    input_small, input_large, spatial_one, temporal_one, spatial_two, temporal_two,
    mid_gain, mid_shift, out_gain, out_shift, cotangent_small, cotangent_large,
):
    clips = input_small.shape[0]
    frames = lax.axis_size("tm")
    nb = lax.axis_size("batch")
    hs, hl = input_small.shape[2], input_large.shape[2]
    places = hs * hs + hl * hl
    sz = Sizes(hs, hl, clips * frames, frames, nb, float(places * clips * frames * nb))
    t = lax.axis_index("tm")
    core = (t % 2).astype(jnp.int32).reshape(1)

    def to_rows(small, large):
        out = []
        for v in (small, large):
            v = v[:, 0].reshape(clips, -1, v.shape[-1])
            out.append(jnp.swapaxes(v, 0, 1).reshape(-1, v.shape[-1]))
        return jnp.concatenate(out)

    def from_rows(rows):
        v = jnp.swapaxes(rows.reshape(places, clips, -1), 0, 1)
        s = v[:, : sz.ns].reshape(clips, 1, hs, hs, -1)
        l = v[:, sz.ns :].reshape(clips, 1, hl, hl, -1)
        return s, l

    def whole_rows(rows):
        return jnp.moveaxis(gather_tm(rows), 0, 1).reshape(-1, rows.shape[-1])

    def own_frame(rows):
        v = rows.reshape(places * clips, frames, rows.shape[-1])
        return lax.dynamic_index_in_dim(v, t, 1, keepdims=False)

    chans = input_small.shape[4]
    one = gather_batch(spread_tm(pack([spatial_one], [temporal_one])))
    two = gather_batch(spread_tm(pack([spatial_two], [temporal_two])))
    nblk = two.shape[0]

    gm, sm = channels(mid_gain, t), channels(mid_shift, t)
    x = whole_rows(to_rows(input_small, input_large))
    cot = whole_rows(to_rows(cotangent_small, cotangent_large))
    x, cot = lax.optimization_barrier((x, cot))

    s1, sums = first_conv(sz, x, one, 0)
    ar1 = shared(sums)
    a1, other, own = norm_temporal(sz, core, s1, ar1, gm[0:1], sm[0:1], one, 21)
    t1m, t1o = sum_tm(own, other)
    ar2 = shared(half_sums(sz, core, t1m, t1o))
    b1, s2, sums = second_conv(sz, core, t1m, t1o, ar2, out_gain[0:1], out_shift[0:1], two, 0)
    ar3 = shared(sums)
    a2, other, own = norm_temporal(sz, core, s2, ar3, gm[1:2], sm[1:2], two, 21)
    t2m, t2o = sum_tm(own, other)
    ar4 = shared(half_sums(sz, core, t2m, t2o))
    out, dpre, sums = output_slope(sz, core, t2m, t2o, ar4, out_gain[1:2], out_shift[1:2], x, cot)
    out_s, out_l = from_rows(own_frame(out))
    own_dpre = own_frame(dpre)

    back4 = shared(sums)
    dt2, e3, sums, n4 = temporal_back(
        sz, core, dpre, t2m, t2o, ar4, back4, out_gain[1:2], s2, ar3, gm[1:2], sm[1:2], two, 21
    )
    back3 = shared(sums)
    other, own, n3 = conv_back(sz, core, e3, s2, ar3, back3, gm[1:2], two, 0)
    d1m, d1o = sum_tm(own, other)
    e3, _ = lax.optimization_barrier((e3, own))
    dk_two = conv_kernel_grad(sz, b1, e3, s2, ar3, back3, gm[1:2], nblk, (dt2, a2))
    sum_two = lax.psum_scatter(owners(dk_two, nb, frames), "batch", scatter_dimension=0)
    e2, sums = middle_slope(sz, core, d1m, d1o, t1m, t1o, ar2, out_gain[0:1], out_shift[0:1])
    back2 = shared(sums)
    dt1, e1, sums, n2 = temporal_back(
        sz, core, e2, t1m, t1o, ar2, back2, out_gain[0:1], s1, ar1, gm[0:1], sm[0:1], one, 21
    )
    back1 = shared(sums)
    dk_one = conv_kernel_grad(sz, x, e1, s1, ar1, back1, gm[0:1], nblk, (dt1, a1))
    moved = lax.all_to_all(
        owners(dk_one, nb, frames).reshape((nb * frames,) + (dk_one.shape[1], -1, 128)),
        ("batch", "tm"), 0, 0, tiled=True,
    )
    grad_sa, grad_ta = unpack(moved.reshape((nb, frames) + moved.shape[1:]), 1, 1)
    sum_two, _ = lax.optimization_barrier((sum_two, dk_one))
    grad_sb, grad_tb = unpack(spread_tm(sum_two)[None], 1, 1)
    e1, _ = lax.optimization_barrier((e1, dk_one))
    other, own, n1 = conv_back(sz, core, e1, s1, ar1, back1, gm[0:1], one, 0)
    first = core[0] == 0
    other = other.astype(F32)
    din = jnp.concatenate([jnp.where(first, own, other), jnp.where(first, other, own)], axis=1)
    din = jnp.moveaxis(din.reshape(places * clips, frames, chans), 1, 0)
    grad_s, grad_l = from_rows(own_dpre + scatter_tm(din))

    mids = all_channels(gather_tm(jnp.stack([n1, n3], axis=1).reshape(4, 384))).reshape(2, 2, -1)
    return (
        out_s, out_l, grad_s, grad_l, grad_sa, grad_ta, grad_sb, grad_tb,
        mids[0], mids[1], jnp.stack([n2[0], n4[0]]), jnp.stack([n2[1], n4[1]]),
    )


def solution(mesh):
    act = P("batch", "tm", None, None, None)
    rows = P(None, ("batch", "tm"), None)
    cols = P(None, None, ("batch", "tm"))
    return jax.shard_map(
        body,
        mesh=mesh,
        in_specs=(act, act, rows, cols, rows, cols, P(), P(), P(), P(), act, act),
        out_specs=(act, act, act, act, rows, cols, rows, cols, P(), P(), P(), P()),
        check_vma=False,
    )
```

```python
import math

import jax
import jax.numpy as jnp
from jax import lax
from jax.experimental import pallas as pl
from jax.experimental.pallas import tpu as pltpu
from jax.sharding import PartitionSpec as P

EPS = 1e-05
F32 = jnp.float32
BF16 = jnp.bfloat16
VMEM_LIMIT = 30 * 1024 * 1024


def swap(value, axis, bit):
    n = lax.axis_size(axis)
    return lax.ppermute(value, axis, [(i, i ^ bit) for i in range(n)])


def shared(copies):
    return lax.all_to_all(copies, "batch", 0, 0, tiled=True)


def tm_bits():
    t = lax.axis_index("tm")
    return t % 2, t // 2


def pair(first, second, bit):
    return jnp.where(bit == 0, jnp.stack([first, second]), jnp.stack([second, first]))


def after(value, *others):
    return lax.optimization_barrier((value,) + others)


def sum_tm(mine, other, *beside):
    mine = (mine.astype(F32) + swap(other, "tm", 1).astype(F32)).astype(BF16)
    got, *beside = after(swap(mine, "tm", 2), *beside)
    mine = (mine.astype(F32) + got.astype(F32)).astype(BF16)
    return (mine, swap(mine, "tm", 1), *beside)


def scatter_tm(mine, other):
    _, y = tm_bits()
    mine = mine + swap(other, "tm", 1).astype(F32)
    own = lax.dynamic_index_in_dim(mine, y, 0, keepdims=False)
    away = lax.dynamic_index_in_dim(mine, 1 - y, 0, keepdims=False)
    return own + swap(away.astype(BF16), "tm", 2).astype(F32)


def n_tiles(offsets):
    return 2 * offsets + -(-offsets // 4)


def tiled(x):
    k, p, _ = x.shape
    q = -(-k // 4)
    main = x[:, :, :1024].reshape(k, p, 4, 2, 128)
    main = jnp.transpose(main, (2, 0, 3, 1, 4)).reshape(4, 2 * k, p, 128)
    rest = jnp.pad(x[:, :, 1024:], ((0, 4 * q - k), (0, 0), (0, 0))).reshape(q, 4, p, 4, 32)
    rest = jnp.transpose(rest, (3, 0, 2, 1, 4)).reshape(4, q, p, 128)
    return jnp.concatenate([main, rest], axis=1)


def untiled(y, k):
    p = y.shape[2]
    q = -(-k // 4)
    main = jnp.transpose(y[:, : 2 * k].reshape(4, k, 2, p, 128), (1, 3, 0, 2, 4)).reshape(k, p, 1024)
    rest = y[:, 2 * k :].reshape(4, q, p, 4, 32)
    rest = jnp.transpose(rest, (1, 3, 2, 0, 4)).reshape(4 * q, p, 128)[:k]
    return jnp.concatenate([main, rest], axis=2)


def pack(spatials, temporals, more=0):
    temporals = [jnp.swapaxes(t, 1, 2) for t in temporals]
    p = (spatials + temporals)[0].shape[1]
    if p % 16:
        out = [tiled(v) for v in spatials] + [tiled(v) for v in temporals]
        return jnp.pad(jnp.concatenate(out, axis=1), ((0, 0), (0, more), (0, 0), (0, 0)))
    total = len(spatials) * n_tiles(9) + len(temporals) * n_tiles(3) + more

    def body(*refs):
        out_ref = refs[-1]
        at = 0
        for ref in refs[:-1]:
            k = ref.shape[0]
            rows = [ref[o].astype(F32) for o in range(k)]
            for t in range(4):
                for o in range(k):
                    for h in range(2):
                        lane = 256 * t + 128 * h
                        out_ref[t, at + 2 * o + h] = rows[o][:, lane : lane + 128].astype(BF16)
                for q in range(-(-k // 4)):
                    group = lax.broadcasted_iota(jnp.int32, (p, 128), 1) // 32
                    tile = jnp.zeros((p, 128), F32)
                    for r in range(4):
                        if 4 * q + r < k:
                            moved = pltpu.roll(rows[4 * q + r][:, 1024:], (32 * (r - t)) % 128, 1)
                            tile = jnp.where(group == r, moved, tile)
                    out_ref[t, at + 2 * k + q] = tile.astype(BF16)
            at += n_tiles(k)
        for n in range(more):
            for t in range(4):
                out_ref[t, at + n] = jnp.zeros((p, 128), BF16)

    return call(body, "pack", [struct((4, total, p, 128), BF16)], [], *spatials, *temporals)[0]


def spread_tm(packed):
    t = lax.axis_index("tm")
    got = []
    for s in range(4):
        piece = lax.dynamic_index_in_dim(packed, t ^ s, 0, keepdims=False)
        got.append(swap(piece, "tm", s) if s else piece)
    got = jnp.stack(got)
    return jnp.stack([lax.dynamic_index_in_dim(got, t ^ s, 0, keepdims=False) for s in range(4)])


def blocks(whole):
    nb, nt, tiles, p, _ = whole.shape
    if p % 16 == 0:
        return whole.reshape(nb * nt, tiles, p, 128)
    v = jnp.moveaxis(whole.reshape(2, nb * nt // 2, tiles, p, 128), 2, 1)
    return v.reshape(2, tiles, nb * nt // 2 * p, 128)


def gather_batch(moved):
    return blocks(lax.all_gather(moved, "batch", axis=0))


def fetch(v, beside_one, beside_two):
    nb = lax.axis_size("batch")
    if nb != 8 or v.shape[2] % 16:
        return [gather_batch(v)], jnp.zeros((1,), jnp.int32), beside_two(*beside_one())
    b = lax.axis_index("batch")
    z, x = b // 2, b % 2

    def turn(u, by):
        return lax.ppermute(u, "batch", [(i, (i + by) % 8) for i in range(8)])

    h = v.shape[0] // 2
    below, above, far, *first = after(turn(v, 2), turn(v, -2), swap(v, "batch", 1), *beside_one())
    opposite = [turn(below[:h], 2), turn(above[h:], -2)]
    far_below, far_above = swap(below, "batch", 1), swap(above, "batch", 1)
    far_below, far_above, *second = after(far_below, far_above, *opposite, *beside_two(*first))
    opposite, second = second[:2], second[2:]
    far_opposite = [turn(far_below[:h], 2), turn(far_above[h:], -2)]
    pieces = [v, below, above] + opposite + [far, far_below, far_above] + far_opposite
    zs = [z, z - 1, z + 1, z + 2, z + 2]
    first_rows = [0, 0, 0, 0, h]
    at = [4 * (2 * (w % 4) + x) + f for w, f in zip(zs, first_rows)]
    at += [4 * (2 * (w % 4) + 1 - x) + f for w, f in zip(zs, first_rows)]
    return pieces, jnp.stack(at).astype(jnp.int32), second


def owners(grads, nb, nt):
    nblk, tiles, p, _ = grads.shape
    if nblk == nb * nt:
        return grads.reshape(nb, nt, tiles, p, 128)
    own = nblk * p // (nb * nt)
    v = grads.reshape(nblk, tiles, nb * nt // nblk, own, 128)
    return jnp.moveaxis(v, 2, 1).reshape(nb, nt, tiles, own, 128)


def unpack(parts, spatials, temporals):
    n, _, total, p, _ = parts.shape
    ks = [9] * spatials + [3] * temporals
    if p % 16:
        summed = jnp.sum(parts.astype(F32), axis=0)
        out, at = [], 0
        for m, k in enumerate(ks):
            v = untiled(summed[:, at : at + n_tiles(k)], k)
            out.append(v if m < spatials else jnp.swapaxes(v, 1, 2))
            at += n_tiles(k)
        return out

    def body(in_ref, *outs):
        group = lax.broadcasted_iota(jnp.int32, (p, 128), 1) // 32

        def tile(t, i):
            v = in_ref[0, t, i].astype(F32)
            for m in range(1, n):
                v = v + in_ref[m, t, i].astype(F32)
            return v

        at = 0
        for k, out_ref in zip(ks, outs):
            rest = [[tile(t, at + 2 * k + q) for t in range(4)] for q in range(-(-k // 4))]
            for o in range(k):
                pieces = [tile(t, at + 2 * o + h) for t in range(4) for h in range(2)]
                last = jnp.zeros((p, 128), F32)
                for t in range(4):
                    moved = pltpu.roll(rest[o // 4][t], (32 * (t - o % 4)) % 128, 1)
                    last = jnp.where(group == t, moved, last)
                whole = jnp.concatenate(pieces + [last], axis=1)
                out_ref[o] = whole
            at += n_tiles(k)

    out = call(body, "unpack", [struct((k, p, 1152), F32) for k in ks], [], parts)
    return [v if m < spatials else jnp.swapaxes(v, 1, 2) for m, v in enumerate(out)]


def channels(v, t):
    main = lax.dynamic_slice_in_dim(v, 256 * t, 256, v.ndim - 1)
    rest = lax.dynamic_slice_in_dim(v, 1024 + 32 * t, 32, v.ndim - 1)
    return jnp.concatenate([main] + [rest] * 4, axis=-1)


def all_channels(v):
    main = jnp.moveaxis(v[..., :256], 0, -2)
    rest = jnp.moveaxis(v[..., 256:288], 0, -2)
    lead = main.shape[:-2]
    return jnp.concatenate([main.reshape(lead + (-1,)), rest.reshape(lead + (-1,))], axis=-1)


class Sizes:
    def __init__(self, hs, hl, group, frames, nb, counted):
        self.hs, self.hl, self.group, self.frames, self.nb = hs, hl, group, frames, nb
        self.ns, self.nl = hs * hs, hl * hl
        self.cut = self.ns * group
        self.rows = (self.ns + self.nl) * group
        self.counted = counted


def call(body, name, outs, scratch, *args, flops=0, anywhere=(), out_anywhere=()):
    smem = pl.BlockSpec(memory_space=pltpu.SMEM)
    vmem = pl.BlockSpec(memory_space=pltpu.VMEM)
    hbm = pl.BlockSpec(memory_space=pl.ANY)
    moved = sum(math.prod(a.shape) * a.dtype.itemsize for a in (*args, *outs))
    return pl.pallas_call(
        body,
        out_shape=outs,
        in_specs=[
            smem if a.dtype == jnp.int32 else hbm if n in anywhere else vmem for n, a in enumerate(args)
        ],
        out_specs=[hbm if n in out_anywhere else vmem for n in range(len(outs))],
        scratch_shapes=scratch,
        name=name,
        compiler_params=pltpu.CompilerParams(vmem_limit_bytes=VMEM_LIMIT),
        cost_estimate=pl.CostEstimate(flops=flops, bytes_accessed=moved, transcendentals=0),
    )(*args)


def struct(shape, dtype):
    return jax.ShapeDtypeStruct(shape, dtype)


def moments(ar_ref, counted):
    s = jnp.sum(ar_ref[...], axis=0)
    mean = s[0:1] / counted
    return mean, lax.rsqrt(s[1:2] / counted - mean * mean + EPS)


def put_sums(out_ref, first, second):
    both = jnp.concatenate(
        [jnp.sum(first, axis=0, keepdims=True), jnp.sum(second, axis=0, keepdims=True)], axis=0
    )
    out_ref[...] = jnp.broadcast_to(both[None], out_ref.shape)


def sigmoid(v):
    return 1.0 / (1.0 + jnp.exp(-v))


def slope(v):
    sig = sigmoid(v)
    return sig * (1.0 + v * (1.0 - sig))


def ordered(core_ref, mine_ref, other_ref):
    first = core_ref[0] == 0
    mine, other = mine_ref[...].astype(F32), other_ref[...].astype(F32)
    return jnp.concatenate([jnp.where(first, mine, other), jnp.where(first, other, mine)], axis=1)


def fill(sz, rows, small_ref, large_ref):
    c = rows.shape[1]
    for ref, h, v in (
        (small_ref, sz.hs, rows[: sz.cut]),
        (large_ref, sz.hl, rows[sz.cut :]),
    ):
        ref[...] = jnp.zeros(ref.shape, F32)
        ref[1 : h + 1, 1 : h + 1] = v.reshape(h, h, sz.group, c)


def window(sz, small_ref, large_ref, i, j, lanes):
    c = lanes.stop - lanes.start
    s = small_ref[i : i + sz.hs, j : j + sz.hs, :, lanes].reshape(sz.cut, c)
    l = large_ref[i : i + sz.hl, j : j + sz.hl, :, lanes].reshape(sz.rows - sz.cut, c)
    return jnp.concatenate([s, l], axis=0)


def tile(k_ref, n, half=None):
    nblk, _, p, lanes = k_ref.shape
    if half is None:
        return k_ref[:, n].reshape(nblk * p, lanes)
    return k_ref[pl.ds(half * (nblk // 2), nblk // 2), n].reshape(nblk // 2 * p, lanes)


def tiles(k_ref, ns, half=None):
    return jnp.concatenate([tile(k_ref, n, half) for n in ns], axis=1)


def lane_group(v):
    return lax.broadcasted_iota(jnp.int32, (1, v.shape[1]), 1) // 32


def folded(v):
    v = v + pltpu.roll(v, 32, 1)
    return v + pltpu.roll(v, 64, 1)


def picked(first, rest):
    out = first
    for r, v in enumerate(rest):
        out = jnp.where(lane_group(first) == r + 1, v, out)
    return out


def conv_rows(sz, xb, small, large, ysmall, ylarge, k_ref):
    c = xb.shape[1]
    every = slice(0, c)
    main = None
    base = 0
    for i in range(3):
        left = jnp.concatenate(
            [window(sz, small, large, i, j, every).astype(BF16) for j in range(3)], axis=1
        )
        right = jnp.concatenate(
            [tiles(k_ref, (base + 6 * i + 2 * j, base + 6 * i + 2 * j + 1)) for j in range(3)], axis=0
        )
        d = jnp.dot(left, right, preferred_element_type=F32)
        main = d if main is None else main + d
    y = jnp.dot(xb, tiles(k_ref, (base + 18, base + 19, base + 20)), preferred_element_type=F32)
    fill(sz, y, ysmall, ylarge)
    rest = window(sz, ysmall, ylarge, 2, 2, slice(256, 384))
    rest = jnp.where(lane_group(rest) == 0, rest, 0.0)
    for q in range(2):
        at = [window(sz, ysmall, ylarge, (4 * q + r) // 3, (4 * q + r) % 3, slice(128 * q, 128 * q + 128)) for r in range(4)]
        rest = rest + picked(at[0], at[1:])
    return jnp.concatenate([main, folded(rest)], axis=1)


def maps(sz, c):
    def one(h):
        return pltpu.VMEM((h + 2, h + 2, sz.group, c), F32)

    return [one(sz.hs), one(sz.hl)]


def lanes_of(sz, c):
    return pltpu.VMEM((c // 128, sz.rows, 128), F32)


def put_lanes(woven, v, at=0):
    for n in range(v.shape[1] // 128):
        woven[at + n] = v[:, 128 * n : 128 * n + 128]


def weave(sz, place, x, cot, x_far):
    frames, n, c = x.shape
    places = sz.rows // sz.group
    clips = sz.group // frames

    def body(place_ref, x_ref, cot_ref, far_ref, rows_ref, cot_rows_ref, xt_ref, ft_ref, woven):
        for src, dst, turned in (
            (cot_ref, cot_rows_ref, None), (x_ref, rows_ref, xt_ref), (far_ref, None, ft_ref)
        ):
            for f in range(frames):
                v = src[f].astype(F32)
                for m in range(clips):
                    rows = v[places * m : places * m + places]
                    for n in range(c // 128):
                        woven[n, pl.ds(frames * m + f, places, stride=sz.group)] = rows[:, 128 * n : 128 * n + 128]
            if dst is not None:
                for n in range(c // 128):
                    dst[:, 128 * n : 128 * n + 128] = woven[n].astype(BF16)
            if turned is not None:
                v = jnp.concatenate([woven[n] for n in range(c // 128)], axis=1).T
                turned[...] = parity_rows(sz, v, place_ref[0] == 1).astype(BF16)

    outs = [struct((sz.rows, c), BF16)] * 2 + [struct((c // 2, sz.rows), BF16)] * 2
    return call(body, "weave", outs, [lanes_of(sz, c)], place, x, cot, x_far)


def frame_of(sz, woven, frame):
    places = sz.rows // sz.group
    out = []
    for m in range(sz.group // sz.frames):
        at = pl.ds(sz.frames * m + frame, places, stride=sz.group)
        out.append(jnp.concatenate([woven[n, at] for n in range(woven.shape[0])], axis=1))
    return jnp.concatenate(out, axis=0)


def first_conv(sz, x, pieces, at):
    c = x.shape[1]
    n = len(pieces)
    nblk = sum(v.shape[0] for v in pieces)
    _, _, p, lanes = pieces[0].shape

    def body(x_ref, at_ref, *refs):
        parts, (s_ref, sums_ref, k_ref) = refs[:n], refs[n : n + 3]
        small, large, ysmall, ylarge, sems = refs[n + 3 :]
        copies = [
            pltpu.make_async_copy(v, k_ref.at[pl.ds(at_ref[m], v.shape[0])], sems.at[m])
            for m, v in enumerate(parts)
        ]
        for copy in copies:
            copy.start()
        fill(sz, x_ref[...].astype(F32), small, large)
        for copy in copies:
            copy.wait()
        total = conv_rows(sz, x_ref[...], small, large, ysmall, ylarge, k_ref)
        s_ref[...] = total
        put_sums(sums_ref, total, total * total)

    outs = [struct((sz.rows, 384), F32), struct((sz.nb, 2, 384), F32), struct((nblk, 28, p, lanes), BF16)]
    return call(body, "conv_one", outs, maps(sz, c) + maps(sz, 384) + [pltpu.SemaphoreType.DMA((n,))], x, at, *pieces,
                flops=18 * sz.rows * c * 288, anywhere=range(2, 2 + n))


def second_conv(sz, core, mine, other, ar, gain, shift, k):
    c = gain.shape[1]

    def body(core_ref, mine_ref, other_ref, ar_ref, g_ref, h_ref, k_ref, b_ref, s_ref, sums_ref,
             small, large, ysmall, ylarge):
        mean, inv = moments(ar_ref, sz.counted)
        p = g_ref[...] * ((ordered(core_ref, mine_ref, other_ref) - mean) * inv) + h_ref[...]
        b = (p * sigmoid(p)).astype(BF16)
        b_ref[...] = b
        fill(sz, b.astype(F32), small, large)
        total = conv_rows(sz, b, small, large, ysmall, ylarge, k_ref)
        s_ref[...] = total
        put_sums(sums_ref, total, total * total)

    outs = [struct((sz.rows, c), BF16), struct((sz.rows, 384), F32), struct((sz.nb, 2, 384), F32)]
    return call(body, "conv_two", outs, maps(sz, c) + maps(sz, 384),
                core, mine, other, ar, gain, shift, k, flops=18 * sz.rows * c * 288)


def frame_shift(sz, v, by):
    if by == 0:
        return v
    c = v.shape[1]
    v = v.reshape(-1, sz.group, c)
    frame = lax.broadcasted_iota(jnp.int32, (1, sz.group, c), 1) % sz.frames
    moved = pltpu.roll(v, (-by) % sz.group, 1)
    inside = (frame + by >= 0) & (frame + by < sz.frames)
    return jnp.where(inside, moved, 0.0).reshape(-1, c)


def norm_temporal(sz, core, s, ar, gain, shift, k, base):
    half = k.shape[0] * k.shape[2] // 2

    def body(core_ref, s_ref, ar_ref, g_ref, h_ref, k_ref, wide_ref, other_ref, mine_ref):
        mean, inv = moments(ar_ref, sz.counted)
        p = g_ref[...] * ((s_ref[...] - mean) * inv) + h_ref[...]
        a = (p * sigmoid(p)).astype(BF16).astype(F32)
        moved = [frame_shift(sz, a, by) for by in (-1, 0, 1)]
        rest = picked(moved[0][:, 256:], [moved[1][:, 256:], moved[2][:, 256:], jnp.zeros_like(a[:, 256:])])
        wide = jnp.concatenate([m[:, :256] for m in moved] + [rest], axis=1).astype(BF16)
        wide_ref[...] = wide
        for out_ref, h in ((other_ref, 1 - core_ref[0]), (mine_ref, core_ref[0])):
            right = tiles(k_ref, range(base, base + 7), h)
            t = lax.dot_general(wide, right, (((1,), (1,)), ((), ())), preferred_element_type=F32)
            out_ref[...] = t.astype(out_ref.dtype)

    outs = [struct((sz.rows, 896), BF16), struct((sz.rows, half), BF16), struct((sz.rows, half), F32)]
    return call(body, "norm_temporal", outs, [], core, s, ar, gain, shift, k,
                flops=6 * sz.rows * 2 * half * 288)


def half_sums(sz, core, mine, other):
    half = mine.shape[1]

    def body(core_ref, mine_ref, other_ref, sums_ref):
        t = ordered(core_ref, mine_ref, other_ref)
        put_sums(sums_ref, t, t * t)

    return call(body, "half_sums", [struct((sz.nb, 2, 2 * half), F32)], [], core, mine, other)[0]


def output_slope(sz, core, mine, other, ar, gain, shift, x, cot):
    c = x.shape[1]

    def body(core_ref, mine_ref, other_ref, ar_ref, g_ref, h_ref, x_ref, cot_ref, d_ref, sums_ref):
        mean, inv = moments(ar_ref, sz.counted)
        xhat = (ordered(core_ref, mine_ref, other_ref) - mean) * inv
        pre = x_ref[...].astype(F32) + (g_ref[...] * xhat + h_ref[...])
        d = cot_ref[...].astype(F32) * slope(pre)
        d_ref[...] = d
        put_sums(sums_ref, d * xhat, d)

    outs = [struct((sz.rows, c), F32), struct((sz.nb, 2, c), F32)]
    return call(body, "output_slope", outs, [], core, mine, other, ar, gain, shift, x, cot)


def own_output(sz, place, mine, other, ar, gain, shift, x, d):
    c = x.shape[1]
    n = sz.rows // sz.frames

    def body(place_ref, mine_ref, other_ref, ar_ref, g_ref, h_ref, x_ref, d_ref, out_ref, own_ref, woven):
        put_lanes(woven, d_ref[...])
        own_ref[...] = frame_of(sz, woven, place_ref[2])
        mean, inv = moments(ar_ref, sz.counted)
        xhat = (ordered(place_ref.at[pl.ds(1, 1)], mine_ref, other_ref) - mean) * inv
        pre = x_ref[...].astype(F32) + (g_ref[...] * xhat + h_ref[...])
        put_lanes(woven, pre * sigmoid(pre))
        out_ref[...] = frame_of(sz, woven, place_ref[2]).astype(BF16)

    outs = [struct((n, c), BF16), struct((n, c), F32)]
    return call(body, "own_output", outs, [lanes_of(sz, c)], place, mine, other, ar, gain, shift, x, d)


def temporal_back(sz, core, e, mine, other, ar, back, gain, shift, s, ar_s, gain_s, shift_s, k, base):
    c = gain.shape[1]
    given = len(e)

    def body(core_ref, *refs):
        e_refs, refs = refs[:given], refs[given:]
        (mine_ref, other_ref, ar_ref, back_ref, g_ref, h_ref, s_ref, ars_ref, gs_ref, hs_ref, k_ref,
         dt_ref, es_ref, sums_ref, got_ref) = refs
        mean, inv = moments(ar_ref, sz.counted)
        got = jnp.sum(back_ref[...], axis=0)
        got_ref[...] = got
        xhat = (ordered(core_ref, mine_ref, other_ref) - mean) * inv
        if given == 1:
            up = e_refs[0][...]
        else:
            up = ordered(core_ref, *e_refs) * slope(g_ref[...] * xhat + h_ref[...])
        d = g_ref[...] * inv * (up - (got[1:2] + xhat * got[0:1]) / sz.counted)
        d = d.astype(BF16)
        dt_ref[...] = d
        d = d.astype(F32)
        left = jnp.concatenate([frame_shift(sz, d, by).astype(BF16) for by in (1, 0, -1)], axis=1)
        right = jnp.concatenate([tiles(k_ref, (base + 2 * n, base + 2 * n + 1)) for n in range(3)], axis=0)
        main = jnp.dot(left, right, preferred_element_type=F32)
        y = jnp.dot(dt_ref[...], tile(k_ref, base + 6), preferred_element_type=F32)
        rest = picked(frame_shift(sz, y, 1), [y, frame_shift(sz, y, -1), jnp.zeros_like(y)])
        da = jnp.concatenate([main, folded(rest)], axis=1).astype(BF16).astype(F32)
        mean_s, inv_s = moments(ars_ref, sz.counted)
        xhat_s = (s_ref[...] - mean_s) * inv_s
        es = da * slope(gs_ref[...] * xhat_s + hs_ref[...])
        es_ref[...] = es
        put_sums(sums_ref, es * xhat_s, es)

    outs = [
        struct((sz.rows, c), BF16),
        struct((sz.rows, 384), F32),
        struct((sz.nb, 2, 384), F32),
        struct((2, c), F32),
    ]
    return call(body, "temporal_back", outs, [], core, *e, mine, other, ar, back, gain, shift,
                s, ar_s, gain_s, shift_s, k, flops=6 * sz.rows * c * 288)


def norm_back_rows(sz, e_ref, s_ref, ar_ref, back_ref, g_ref):
    mean, inv = moments(ar_ref, sz.counted)
    got = jnp.sum(back_ref[...], axis=0)
    xhat = (s_ref[...] - mean) * inv
    d = g_ref[...] * inv * (e_ref[...] - (got[1:2] + xhat * got[0:1]) / sz.counted)
    return d.astype(BF16).astype(F32), got


def rest_patches(sz, small, large):
    lanes = slice(256, 384)
    out = []
    for q in range(3):
        at = [window(sz, small, large, 2 - o // 3, 2 - o % 3, lanes) for o in range(4 * q, min(4 * q + 4, 9))]
        at += [jnp.zeros_like(at[0])] * (4 - len(at))
        out.append(picked(at[0], at[1:]).astype(BF16))
    return jnp.concatenate(out, axis=1)


def tall(sz):
    full = -(-sz.rows // 16) * 16
    quarter = -(-sz.rows // 64) * 16
    return full, quarter


def put_tall(sz, out_ref, d):
    full, quarter = tall(sz)
    pad = jnp.zeros((4 * quarter - sz.rows, 128), F32)
    for n in range(2):
        v = jnp.concatenate([d[:, 128 * n : 128 * n + 128], pad[: full - sz.rows]], axis=0)
        out_ref[n * full : n * full + full] = v.astype(BF16)
    rest = jnp.concatenate([d[:, 256:], pad], axis=0)
    at = [rest[quarter * g : quarter * g + quarter] for g in range(4)]
    out_ref[2 * full :] = picked(at[0], at[1:]).astype(BF16)


def get_tall(sz, ref):
    full, quarter = tall(sz)
    main = [ref[n * full : n * full + full].astype(F32)[: sz.rows] for n in range(2)]
    packed = ref[2 * full :].astype(F32)
    rest = [folded(jnp.where(lane_group(packed) == g, packed, 0.0)) for g in range(4)]
    rest = jnp.concatenate(rest, axis=0)[: sz.rows]
    return jnp.concatenate(main + [rest], axis=1)


def tall_struct(sz):
    full, quarter = tall(sz)
    return struct((2 * full + quarter, 128), BF16)


def norm_back(sz, e, s, ar, back, gain):
    def body(e_ref, s_ref, ar_ref, back_ref, g_ref, d_ref, got_ref):
        d, got = norm_back_rows(sz, e_ref, s_ref, ar_ref, back_ref, g_ref)
        got_ref[...] = got
        put_tall(sz, d_ref, d)

    outs = [tall_struct(sz), struct((2, 384), F32)]
    return call(body, "norm_back", outs, [], e, s, ar, back, gain)


def conv_back_halves(sz, core_ref, d, k_ref, small, large):
    fill(sz, d, small, large)
    rest = rest_patches(sz, small, large)
    for h in (1 - core_ref[0], core_ref[0]):
        total = None
        for i in range(3):
            left = jnp.concatenate(
                [window(sz, small, large, 2 - i, 2 - j, slice(0, 256)).astype(BF16) for j in range(3)],
                axis=1,
            )
            right = tiles(k_ref, range(6 * i, 6 * i + 6), h)
            if i == 2:
                left = jnp.concatenate([left, rest], axis=1)
                right = jnp.concatenate([right, tiles(k_ref, range(18, 21), h)], axis=1)
            one = lax.dot_general(left, right, (((1,), (1,)), ((), ())), preferred_element_type=F32)
            total = one if total is None else total + one
        yield total


def middle_back(sz, core, e, s, ar, back, gain, k, mine, other, ar_t, gain_t, shift_t, copies_of_sums):
    half = k.shape[0] * k.shape[2] // 2

    def body(core_ref, e_ref, s_ref, ar_ref, back_ref, g_ref, k_ref, mine_ref, other_ref, art_ref, gt_ref, ht_ref,
             dother_ref, dmine_ref, sums_ref, got_ref, d_ref, small, large):
        d, got = norm_back_rows(sz, e_ref, s_ref, ar_ref, back_ref, g_ref)
        got_ref[...] = got
        put_tall(sz, d_ref, d)
        mean, inv = moments(art_ref, sz.counted)
        swapped = core_ref[0] == 1
        found = []
        ends = ((dother_ref, other_ref, True), (dmine_ref, mine_ref, False))
        for (out_ref, t_ref, away), total in zip(ends, conv_back_halves(sz, core_ref, d, k_ref, small, large)):
            def part(v):
                first, second = v[:, :half], v[:, half:]
                if away:
                    first, second = second, first
                return jnp.where(swapped, second, first)

            xhat = (t_ref[...].astype(F32) - part(mean)) * part(inv)
            out_ref[...] = total.astype(out_ref.dtype)
            total = total * slope(part(gt_ref[...]) * xhat + part(ht_ref[...]))
            found.append(
                jnp.concatenate(
                    [jnp.sum(total * xhat, axis=0, keepdims=True), jnp.sum(total, axis=0, keepdims=True)], axis=0
                )
            )
        first = jnp.where(swapped, found[0], found[1])
        second = jnp.where(swapped, found[1], found[0])
        both = jnp.concatenate([first, second], axis=1)
        sums_ref[...] = jnp.broadcast_to(both[None], sums_ref.shape)

    outs = [
        struct((sz.rows, half), BF16),
        struct((sz.rows, half), F32),
        struct((copies_of_sums, 2, 2 * half), F32),
        struct((2, 384), F32),
        tall_struct(sz),
    ]
    return call(body, "middle_back", outs, maps(sz, 384), core, e, s, ar, back, gain, k,
                mine, other, ar_t, gain_t, shift_t, flops=18 * sz.rows * 2 * half * 288)


def input_back(sz, place, d, k):
    half = k.shape[0] * k.shape[2] // 2
    n = sz.rows // sz.frames

    def body(place_ref, d_ref, k_ref, other_ref, mine_ref, small, large, woven):
        rows = get_tall(sz, d_ref)
        core = place_ref[1]
        for h, total in zip((1 - core, core), conv_back_halves(sz, place_ref.at[pl.ds(1, 1)], rows, k_ref, small, large)):
            put_lanes(woven, total, h * (half // 128))
        for y in range(sz.frames // 2):
            other_ref[y] = frame_of(sz, woven, 2 * y + 1 - core).astype(BF16)
            mine_ref[y] = frame_of(sz, woven, 2 * y + core)

    outs = [struct((sz.frames // 2, n, 2 * half), BF16), struct((sz.frames // 2, n, 2 * half), F32)]
    return call(body, "input_back", outs, maps(sz, 384) + [lanes_of(sz, 2 * half)], place, d, k,
                flops=18 * sz.rows * 2 * half * 288)


def put_tiles(out_ref, at, v):
    nblk, _, p, _ = out_ref.shape
    v = v.astype(BF16)
    for n in range(v.shape[1] // 128):
        out_ref[:, at + n] = v[:, 128 * n : 128 * n + 128].reshape(nblk, p, 128)


def parity_rows(sz, v, odd):
    c, n = v.shape
    v = v.reshape(sz.nb // 2, 2, c // sz.nb, n)
    return jnp.where(odd, v[:, 1], v[:, 0]).reshape(c // 2, n)


def transposed(sz, place, x):
    c = x.shape[1]

    def body(place_ref, x_ref, keep_ref, send_ref):
        v = x_ref[...].astype(F32).T
        odd = place_ref[0] == 1
        keep_ref[...] = parity_rows(sz, v, odd).astype(BF16)
        send_ref[...] = parity_rows(sz, v, jnp.logical_not(odd)).astype(BF16)

    return call(body, "transposed", [struct((c // 2, sz.rows), BF16)] * 2, [], place, x)


def temporal_kernel_grad(sz, place, dt, wide, nblk):
    c = dt.shape[1]

    def body(place_ref, dt_ref, wide_ref, keep_ref, send_ref):
        v = jnp.dot(dt_ref[...].T, wide_ref[...], preferred_element_type=F32)
        odd = place_ref[0] == 1
        put_tiles(keep_ref, 0, parity_rows(sz, v, odd))
        put_tiles(send_ref, 0, parity_rows(sz, v, jnp.logical_not(odd)))

    outs = [struct((nblk // 2, n_tiles(3), c // nblk, 128), BF16)] * 2
    return call(body, "temporal_kernel_grad", outs, [], place, dt, wide, flops=2 * dt.size * wide.shape[1])


def kernel_grads(sz, lefts, ds, temporals):
    c = lefts[0].shape[0]
    nblk, _, p, _ = temporals[0].shape

    def body(la_ref, lb_ref, da_ref, db_ref, ta_ref, tb_ref, out_ref, sa, la, sb, lb):
        fill(sz, get_tall(sz, da_ref), sa, la)
        fill(sz, get_tall(sz, db_ref), sb, lb)

        def grad(make):
            return jnp.dot(la_ref[...], make(sa, la), preferred_element_type=F32) + jnp.dot(
                lb_ref[...], make(sb, lb), preferred_element_type=F32
            )

        for o in range(9):
            put_tiles(
                out_ref, 2 * o,
                grad(lambda s, l: window(sz, s, l, 2 - o // 3, 2 - o % 3, slice(0, 256)).astype(BF16)),
            )
        put_tiles(out_ref, 18, grad(lambda s, l: rest_patches(sz, s, l)))
        for n in range(7):
            out_ref[:, 21 + n] = (ta_ref[:, n].astype(F32) + tb_ref[:, n].astype(F32)).astype(BF16)

    outs = [struct((nblk, 28, p, 128), BF16)]
    return call(body, "kernel_grads", outs, maps(sz, 384) + maps(sz, 384), *lefts, *ds, *temporals,
                flops=2 * 18 * sz.rows * c * 288)[0]


def body(
    input_small, input_large, spatial_one, temporal_one, spatial_two, temporal_two,
    mid_gain, mid_shift, out_gain, out_shift, cotangent_small, cotangent_large,
):
    clips = input_small.shape[0]
    frames = lax.axis_size("tm")
    nb = lax.axis_size("batch")
    hs, hl = input_small.shape[2], input_large.shape[2]
    places = hs * hs + hl * hl
    sz = Sizes(hs, hl, clips * frames, frames, nb, float(places * clips * frames * nb))
    t = lax.axis_index("tm")
    core = (t % 2).astype(jnp.int32).reshape(1)

    def to_rows(small, large):
        return jnp.concatenate(
            [v[:, 0].reshape(clips, -1, v.shape[-1]) for v in (small, large)], axis=1
        ).reshape(clips * places, -1)

    def from_rows(rows):
        v = rows.reshape(clips, places, -1)
        s = v[:, : sz.ns].reshape(clips, 1, hs, hs, -1)
        l = v[:, sz.ns :].reshape(clips, 1, hl, hl, -1)
        return s, l

    b = lax.axis_index("batch")
    place = jnp.stack([b % 2, t % 2, t]).astype(jnp.int32)
    parities = [[i for i in range(nb) if i % 2 == q] for q in range(2)]

    rows = to_rows(input_small, input_large)
    cot_rows = to_rows(cotangent_small, cotangent_large)
    one = spread_tm(pack([spatial_one], [temporal_one]))

    def beside_one():
        return spread_tm(pack([spatial_two], [temporal_two])), swap(rows, "batch", 1)

    def beside_two(two, far_rows):
        acts = jnp.stack([rows, cot_rows, far_rows])
        return two, acts, swap(acts, "tm", 2)

    pieces, at, (two, acts, got) = fetch(one, beside_one, beside_two)
    both = pair(acts, got, t // 2)
    woven = pair(both, swap(both, "tm", 1), t % 2)
    woven = jnp.moveaxis(woven, 0, 1).reshape((frames,) + acts.shape)
    two = gather_batch(two)
    nblk = two.shape[0]
    x, cot, xt, xt_far = weave(sz, place, woven[:, 0], woven[:, 1], woven[:, 2])

    gm, sm = channels(mid_gain, t), channels(mid_shift, t)
    small = [gm[0:1], gm[1:2], sm[0:1], sm[1:2], out_gain[0:1], out_gain[1:2], out_shift[0:1], out_shift[1:2]]
    gm0, gm1, sm0, sm1, go0, go1, so0, so1, core, place, x = after(*small, core, place, x)

    s1, sums, one = first_conv(sz, x, pieces, at)
    ar1 = shared(sums)
    a1, other, own = norm_temporal(sz, core, s1, ar1, gm0, sm0, one, 21)
    t1m, t1o = sum_tm(own, other)
    ar2 = shared(half_sums(sz, core, t1m, t1o))
    b1, s2, sums = second_conv(sz, core, t1m, t1o, ar2, go0, so0, two)
    ar3 = shared(sums)
    a2, other, own = norm_temporal(sz, core, s2, ar3, gm1, sm1, two, 21)
    bt, bt_send = transposed(sz, place, after(b1, other)[0])
    t2m, t2o, bt, bt_far = sum_tm(own, other, bt, swap(bt_send, "batch", 1))
    ar4 = shared(half_sums(sz, core, t2m, t2o))
    dpre, sums = output_slope(sz, core, t2m, t2o, ar4, go1, so1, x, cot)
    back4 = shared(sums)
    dt2, e3, sums, n4 = temporal_back(
        sz, core, (dpre,), t2m, t2o, ar4, back4, go1, so1, s2, ar3, gm1, sm1, two, 21
    )
    back3 = shared(sums)
    other, own, sums, n3, ds2 = middle_back(
        sz, core, e3, s2, ar3, back3, gm1, two, t1m, t1o, ar2, go0, so0, nb * frames
    )
    back2 = lax.all_to_all(sums, ("batch", "tm"), 0, 0, tiled=True)
    away = after(ds2, own)[0]
    tb_grad, tb_send = temporal_kernel_grad(sz, place, after(dt2, own)[0], a2, nblk)
    own_out, own_dpre = own_output(sz, place, t2m, t2o, ar4, go1, so1, x, after(dpre, tb_send)[0])
    d1m, d1o, back2, ds2_far, tb_far, own_out, own_dpre = sum_tm(
        own, other, back2, swap(away, "batch", 1), swap(tb_send, "batch", 1), own_out, own_dpre
    )
    out_s, out_l = from_rows(own_out)
    dk_two = kernel_grads(sz, (bt, bt_far), (ds2, ds2_far), (tb_grad, tb_far))
    sum_two = lax.psum_scatter(
        owners(dk_two, nb // 2, frames), "batch", scatter_dimension=0, axis_index_groups=parities
    )
    dt1, e1, sums, n2 = temporal_back(
        sz, core, (d1m, d1o), t1m, t1o, ar2, back2, go0, so0, s1, ar1, gm0, sm0, one, 21
    )
    ta_grad, ta_send = temporal_kernel_grad(sz, place, dt1, a1, nblk)
    ta_got = swap(ta_send, "batch", 1)
    sums, ta_grad, _ = after(sums, ta_grad, dk_two)
    back1 = shared(sums)
    ds1, n1 = norm_back(sz, e1, s1, ar1, back1, gm0)
    ds1_got = swap(ds1, "batch", 1)
    other, own = input_back(sz, place, ds1, one)
    ds1_got, other, own = after(ds1_got, other, own)
    dk_one = kernel_grads(sz, (xt, xt_far), (ds1, ds1_got), (ta_grad, ta_got))
    moved = lax.all_to_all(
        owners(dk_one, nb // 2, frames).reshape((nb // 2 * frames, dk_one.shape[1], -1, 128)),
        ("batch", "tm"), 0, 0, tiled=True,
        axis_index_groups=[[i * frames + j for i in g for j in range(frames)] for g in parities],
    )
    sum_two, other, _ = after(sum_two, other, dk_one)
    grad_sb, grad_tb = unpack(spread_tm(sum_two)[None], 1, 1)
    grad_s, grad_l = from_rows(own_dpre + scatter_tm(own, other))

    n13 = jnp.stack([n1, n3], axis=1)
    n13 = pair(n13, swap(n13, "tm", 2), t // 2)
    n13 = jnp.swapaxes(pair(n13, swap(n13, "tm", 1), t % 2), 0, 1).reshape((frames, 4, 384))
    moved, grad_s, grad_l, grad_sb, grad_tb, n13 = after(moved, grad_s, grad_l, grad_sb, grad_tb, n13)
    grad_sa, grad_ta = unpack(moved.reshape((nb // 2, frames) + moved.shape[1:]), 1, 1)
    mids = all_channels(n13).reshape(2, 2, -1)
    return (
        out_s, out_l, grad_s, grad_l, grad_sa, grad_ta, grad_sb, grad_tb,
        mids[0], mids[1], jnp.stack([n2[0], n4[0]]), jnp.stack([n2[1], n4[1]]),
    )


def solution(mesh):
    act = P("batch", "tm", None, None, None)
    rows = P(None, ("batch", "tm"), None)
    cols = P(None, None, ("batch", "tm"))
    return jax.shard_map(
        body,
        mesh=mesh,
        in_specs=(act, act, rows, cols, rows, cols, P(), P(), P(), P(), act, act),
        out_specs=(act, act, act, act, rows, cols, rows, cols, P(), P(), P(), P()),
        check_vma=False,
    )
```

```python
import math

import jax
import jax.numpy as jnp
from jax import lax
from jax.experimental import pallas as pl
from jax.experimental.pallas import tpu as pltpu
from jax.sharding import PartitionSpec as P

EPS = 1e-05
F32 = jnp.float32
BF16 = jnp.bfloat16
VMEM_LIMIT = 30 * 1024 * 1024


def swap(value, axis, bit):
    n = lax.axis_size(axis)
    return lax.ppermute(value, axis, [(i, i ^ bit) for i in range(n)])


def shared(copies):
    return lax.all_to_all(copies, "batch", 0, 0, tiled=True)


def tm_bits():
    t = lax.axis_index("tm")
    return t % 2, t // 2


def pair(first, second, bit):
    return jnp.where(bit == 0, jnp.stack([first, second]), jnp.stack([second, first]))


def after(value, *others):
    return lax.optimization_barrier((value,) + others)


def sum_tm(mine, other, beside=None):
    mine = (mine.astype(F32) + swap(other, "tm", 1).astype(F32)).astype(BF16)
    got, *there = after(swap(mine, "tm", 2), *(beside(mine) if beside else ()))
    mine = (mine.astype(F32) + got.astype(F32)).astype(BF16)
    return (mine, swap(mine, "tm", 1), *there)


def scatter_tm(mine, other):
    _, y = tm_bits()
    mine = mine + swap(other, "tm", 1).astype(F32)
    own = lax.dynamic_index_in_dim(mine, y, 0, keepdims=False)
    away = lax.dynamic_index_in_dim(mine, 1 - y, 0, keepdims=False)
    return own + swap(away.astype(BF16), "tm", 2).astype(F32)


def n_tiles(offsets):
    return 2 * offsets + -(-offsets // 4)


def tiled(x):
    k, p, _ = x.shape
    q = -(-k // 4)
    main = x[:, :, :1024].reshape(k, p, 4, 2, 128)
    main = jnp.transpose(main, (2, 0, 3, 1, 4)).reshape(4, 2 * k, p, 128)
    rest = jnp.pad(x[:, :, 1024:], ((0, 4 * q - k), (0, 0), (0, 0))).reshape(q, 4, p, 4, 32)
    rest = jnp.transpose(rest, (3, 0, 2, 1, 4)).reshape(4, q, p, 128)
    return jnp.concatenate([main, rest], axis=1)


def untiled(y, k):
    p = y.shape[2]
    q = -(-k // 4)
    main = jnp.transpose(y[:, : 2 * k].reshape(4, k, 2, p, 128), (1, 3, 0, 2, 4)).reshape(k, p, 1024)
    rest = y[:, 2 * k :].reshape(4, q, p, 4, 32)
    rest = jnp.transpose(rest, (1, 3, 2, 0, 4)).reshape(4 * q, p, 128)[:k]
    return jnp.concatenate([main, rest], axis=2)


def pack(spatials, temporals, more=0):
    temporals = [jnp.swapaxes(t, 1, 2) for t in temporals]
    p = (spatials + temporals)[0].shape[1]
    if p % 16:
        out = [tiled(v) for v in spatials] + [tiled(v) for v in temporals]
        return jnp.pad(jnp.concatenate(out, axis=1), ((0, 0), (0, more), (0, 0), (0, 0)))
    total = len(spatials) * n_tiles(9) + len(temporals) * n_tiles(3) + more

    def body(*refs):
        out_ref = refs[-1]
        at = 0
        for ref in refs[:-1]:
            k = ref.shape[0]
            rows = [ref[o].astype(F32) for o in range(k)]
            for t in range(4):
                for o in range(k):
                    for h in range(2):
                        lane = 256 * t + 128 * h
                        out_ref[t, at + 2 * o + h] = rows[o][:, lane : lane + 128].astype(BF16)
                for q in range(-(-k // 4)):
                    group = lax.broadcasted_iota(jnp.int32, (p, 128), 1) // 32
                    tile = jnp.zeros((p, 128), F32)
                    for r in range(4):
                        if 4 * q + r < k:
                            moved = pltpu.roll(rows[4 * q + r][:, 1024:], (32 * (r - t)) % 128, 1)
                            tile = jnp.where(group == r, moved, tile)
                    out_ref[t, at + 2 * k + q] = tile.astype(BF16)
            at += n_tiles(k)
        for n in range(more):
            for t in range(4):
                out_ref[t, at + n] = jnp.zeros((p, 128), BF16)

    return call(body, "pack", [struct((4, total, p, 128), BF16)], [], *spatials, *temporals)[0]


def turned_tm(packed):
    t = lax.axis_index("tm")
    got = []
    for s in range(4):
        piece = lax.dynamic_index_in_dim(packed, t ^ s, 0, keepdims=False)
        got.append(swap(piece, "tm", s) if s else piece)
    return jnp.stack(got)


def spread_tm(packed):
    t = lax.axis_index("tm")
    got = turned_tm(packed)
    return jnp.stack([lax.dynamic_index_in_dim(got, t ^ s, 0, keepdims=False) for s in range(4)])


def blocks(whole):
    nb, nt, tiles, p, _ = whole.shape
    if p % 16 == 0:
        return whole.reshape(nb * nt, tiles, p, 128)
    v = jnp.moveaxis(whole.reshape(2, nb * nt // 2, tiles, p, 128), 2, 1)
    return v.reshape(2, tiles, nb * nt // 2 * p, 128)


def gather_batch(moved):
    return blocks(lax.all_gather(moved, "batch", axis=0))


def fetch(packed, ahead, beside):
    nb = lax.axis_size("batch")
    if nb != 8 or packed.shape[2] % 16:
        return [gather_batch(spread_tm(packed))], jnp.zeros((1,), jnp.int32), beside(*ahead), []
    b, t = lax.axis_index("batch"), lax.axis_index("tm")
    z, x = b // 2, b % 2

    def turn(u, by):
        return lax.ppermute(u, "batch", [(i, (i + by) % 8) for i in range(8)])

    v, *ahead = after(turned_tm(packed), *ahead)
    below, far = after(turn(v, 2), swap(v, "batch", 1))
    v, *ahead = after(v, below, *ahead)
    there = beside(*ahead[1:])
    above, far_below = after(turn(v, -2), swap(below, "batch", 1))
    opposite = [turn(after(below[:2], above)[0], 2), turn(above[2:], -2)]
    far_above = swap(above, "batch", 1)
    far_above, *there = after(far_above, *opposite, *there)
    opposite, there = there[:2], there[2:]
    far_opposite = [swap(o, "batch", 1) for o in opposite]
    pieces = [v, below, above] + opposite + [far, far_below, far_above] + far_opposite
    zs = [z, z - 1, z + 1, z + 2, z + 2]
    rows = [range(4), range(4), range(4), range(2), range(2, 4)]
    at = [4 * (2 * (w % 4) + x) + (t ^ r) for w, rs in zip(zs, rows) for r in rs]
    at += [4 * (2 * (w % 4) + 1 - x) + (t ^ r) for w, rs in zip(zs, rows) for r in rs]
    return pieces, jnp.stack(at).astype(jnp.int32), there, [far_above]


def owners(grads, nb, nt):
    nblk, tiles, p, _ = grads.shape
    if nblk == nb * nt:
        return grads.reshape(nb, nt, tiles, p, 128)
    own = nblk * p // (nb * nt)
    v = grads.reshape(nblk, tiles, nb * nt // nblk, own, 128)
    return jnp.moveaxis(v, 2, 1).reshape(nb, nt, tiles, own, 128)


def unpack(parts, spatials, temporals):
    n, _, total, p, _ = parts.shape
    ks = [9] * spatials + [3] * temporals
    if p % 16:
        summed = jnp.sum(parts.astype(F32), axis=0)
        out, at = [], 0
        for m, k in enumerate(ks):
            v = untiled(summed[:, at : at + n_tiles(k)], k)
            out.append(v if m < spatials else jnp.swapaxes(v, 1, 2))
            at += n_tiles(k)
        return out

    def body(in_ref, *outs):
        group = lax.broadcasted_iota(jnp.int32, (p, 128), 1) // 32

        def tile(t, i):
            v = in_ref[0, t, i].astype(F32)
            for m in range(1, n):
                v = v + in_ref[m, t, i].astype(F32)
            return v

        at = 0
        for k, out_ref in zip(ks, outs):
            rest = [[tile(t, at + 2 * k + q) for t in range(4)] for q in range(-(-k // 4))]
            for o in range(k):
                pieces = [tile(t, at + 2 * o + h) for t in range(4) for h in range(2)]
                last = jnp.zeros((p, 128), F32)
                for t in range(4):
                    moved = pltpu.roll(rest[o // 4][t], (32 * (t - o % 4)) % 128, 1)
                    last = jnp.where(group == t, moved, last)
                whole = jnp.concatenate(pieces + [last], axis=1)
                out_ref[o] = whole
            at += n_tiles(k)

    out = call(body, "unpack", [struct((k, p, 1152), F32) for k in ks], [], parts)
    return [v if m < spatials else jnp.swapaxes(v, 1, 2) for m, v in enumerate(out)]


def channels(v, t):
    main = lax.dynamic_slice_in_dim(v, 256 * t, 256, v.ndim - 1)
    rest = lax.dynamic_slice_in_dim(v, 1024 + 32 * t, 32, v.ndim - 1)
    return jnp.concatenate([main] + [rest] * 4, axis=-1)


def all_channels(v):
    main = jnp.moveaxis(v[..., :256], 0, -2)
    rest = jnp.moveaxis(v[..., 256:288], 0, -2)
    lead = main.shape[:-2]
    return jnp.concatenate([main.reshape(lead + (-1,)), rest.reshape(lead + (-1,))], axis=-1)


class Sizes:
    def __init__(self, hs, hl, group, frames, nb, counted):
        self.hs, self.hl, self.group, self.frames, self.nb = hs, hl, group, frames, nb
        self.ns, self.nl = hs * hs, hl * hl
        self.cut = self.ns * group
        self.rows = (self.ns + self.nl) * group
        self.counted = counted


def call(body, name, outs, scratch, *args, flops=0, anywhere=(), out_anywhere=()):
    smem = pl.BlockSpec(memory_space=pltpu.SMEM)
    vmem = pl.BlockSpec(memory_space=pltpu.VMEM)
    hbm = pl.BlockSpec(memory_space=pl.ANY)
    moved = sum(math.prod(a.shape) * a.dtype.itemsize for a in (*args, *outs))
    return pl.pallas_call(
        body,
        out_shape=outs,
        in_specs=[
            smem if a.dtype == jnp.int32 else hbm if n in anywhere else vmem for n, a in enumerate(args)
        ],
        out_specs=[hbm if n in out_anywhere else vmem for n in range(len(outs))],
        scratch_shapes=scratch,
        name=name,
        compiler_params=pltpu.CompilerParams(vmem_limit_bytes=VMEM_LIMIT),
        cost_estimate=pl.CostEstimate(flops=flops, bytes_accessed=moved, transcendentals=0),
    )(*args)


def struct(shape, dtype):
    return jax.ShapeDtypeStruct(shape, dtype)


def moments(ar_ref, counted):
    s = jnp.sum(ar_ref[...], axis=0)
    mean = s[0:1] / counted
    return mean, lax.rsqrt(s[1:2] / counted - mean * mean + EPS)


def put_sums(out_ref, first, second):
    both = jnp.concatenate(
        [jnp.sum(first, axis=0, keepdims=True), jnp.sum(second, axis=0, keepdims=True)], axis=0
    )
    out_ref[...] = jnp.broadcast_to(both[None], out_ref.shape)


def sigmoid(v):
    return 1.0 / (1.0 + jnp.exp(-v))


def slope(v):
    sig = sigmoid(v)
    return sig * (1.0 + v * (1.0 - sig))


def ordered(core_ref, mine_ref, other_ref):
    first = core_ref[0] == 0
    mine, other = mine_ref[...].astype(F32), other_ref[...].astype(F32)
    return jnp.concatenate([jnp.where(first, mine, other), jnp.where(first, other, mine)], axis=1)


def fill(sz, rows, small_ref, large_ref):
    c = rows.shape[1]
    for ref, h, v in (
        (small_ref, sz.hs, rows[: sz.cut]),
        (large_ref, sz.hl, rows[sz.cut :]),
    ):
        ref[...] = jnp.zeros(ref.shape, F32)
        ref[1 : h + 1, 1 : h + 1] = v.reshape(h, h, sz.group, c)


def window(sz, small_ref, large_ref, i, j, lanes):
    c = lanes.stop - lanes.start
    s = small_ref[i : i + sz.hs, j : j + sz.hs, :, lanes].reshape(sz.cut, c)
    l = large_ref[i : i + sz.hl, j : j + sz.hl, :, lanes].reshape(sz.rows - sz.cut, c)
    return jnp.concatenate([s, l], axis=0)


def tile(k_ref, n, half=None):
    nblk, _, p, lanes = k_ref.shape
    if half is None:
        return k_ref[:, n].reshape(nblk * p, lanes)
    return k_ref[pl.ds(half * (nblk // 2), nblk // 2), n].reshape(nblk // 2 * p, lanes)


def tiles(k_ref, ns, half=None):
    return jnp.concatenate([tile(k_ref, n, half) for n in ns], axis=1)


def lane_group(v):
    return lax.broadcasted_iota(jnp.int32, (1, v.shape[1]), 1) // 32


def folded(v):
    v = v + pltpu.roll(v, 32, 1)
    return v + pltpu.roll(v, 64, 1)


def picked(first, rest):
    out = first
    for r, v in enumerate(rest):
        out = jnp.where(lane_group(first) == r + 1, v, out)
    return out


def conv_rows(sz, xb, small, large, ysmall, ylarge, k_ref):
    c = xb.shape[1]
    every = slice(0, c)
    main = None
    base = 0
    for i in range(3):
        left = jnp.concatenate(
            [window(sz, small, large, i, j, every).astype(BF16) for j in range(3)], axis=1
        )
        right = jnp.concatenate(
            [tiles(k_ref, (base + 6 * i + 2 * j, base + 6 * i + 2 * j + 1)) for j in range(3)], axis=0
        )
        d = jnp.dot(left, right, preferred_element_type=F32)
        main = d if main is None else main + d
    y = jnp.dot(xb, tiles(k_ref, (base + 18, base + 19, base + 20)), preferred_element_type=F32)
    fill(sz, y, ysmall, ylarge)
    rest = window(sz, ysmall, ylarge, 2, 2, slice(256, 384))
    rest = jnp.where(lane_group(rest) == 0, rest, 0.0)
    for q in range(2):
        at = [window(sz, ysmall, ylarge, (4 * q + r) // 3, (4 * q + r) % 3, slice(128 * q, 128 * q + 128)) for r in range(4)]
        rest = rest + picked(at[0], at[1:])
    return jnp.concatenate([main, folded(rest)], axis=1)


def maps(sz, c):
    def one(h):
        return pltpu.VMEM((h + 2, h + 2, sz.group, c), F32)

    return [one(sz.hs), one(sz.hl)]


def wide_struct(sz, c):
    return struct((c // 2, -(-sz.rows // 128) * 128), BF16)


def put_wide(out_ref, v):
    pad = jnp.zeros((v.shape[0], out_ref.shape[1] - v.shape[1]), F32)
    out_ref[...] = jnp.concatenate([v, pad], axis=1).astype(BF16)


def lanes_of(sz, c):
    return pltpu.VMEM((c // 128, sz.rows, 128), F32)


def put_lanes(woven, v, at=0):
    for n in range(v.shape[1] // 128):
        woven[at + n] = v[:, 128 * n : 128 * n + 128]


def weave(sz, place, frames_of):
    _, n, c = frames_of[0].shape
    places = sz.rows // sz.group
    clips = sz.group // sz.frames

    def body(place_ref, *refs):
        srcs, (rows_ref, cot_rows_ref, xt_ref, ft_ref, woven) = refs[:4], refs[4:]
        for a, dst, turned in ((1, cot_rows_ref, None), (0, rows_ref, xt_ref), (2, None, ft_ref)):
            for s, src in enumerate(srcs):
                v = src[a].astype(F32)
                f = place_ref[2] ^ s
                for m in range(clips):
                    rows = v[places * m : places * m + places]
                    for n in range(c // 128):
                        woven[n, pl.ds(sz.frames * m + f, places, stride=sz.group)] = rows[:, 128 * n : 128 * n + 128]
            if dst is not None:
                for n in range(c // 128):
                    dst[:, 128 * n : 128 * n + 128] = woven[n].astype(BF16)
            if turned is not None:
                v = jnp.concatenate([woven[n] for n in range(c // 128)], axis=1).T
                put_wide(turned, parity_rows(sz, v, place_ref[0] == 1))

    outs = [struct((sz.rows, c), BF16)] * 2 + [wide_struct(sz, c)] * 2
    return call(body, "weave", outs, [lanes_of(sz, c)], place, *frames_of)


def frame_of(sz, woven, frame):
    places = sz.rows // sz.group
    out = []
    for m in range(sz.group // sz.frames):
        at = pl.ds(sz.frames * m + frame, places, stride=sz.group)
        out.append(jnp.concatenate([woven[n, at] for n in range(woven.shape[0])], axis=1))
    return jnp.concatenate(out, axis=0)


def first_conv(sz, x, pieces, at):
    c = x.shape[1]
    n = len(pieces)
    nblk = sum(v.shape[0] for v in pieces)
    _, _, p, lanes = pieces[0].shape
    whole = n == 1

    def body(x_ref, at_ref, *refs):
        parts, (s_ref, sums_ref, out_ref) = refs[:n], refs[n : n + 3]
        small, large, ysmall, ylarge, k_ref, sems = refs[n + 3 :]
        if whole:
            copies = [pltpu.make_async_copy(parts[0], k_ref, sems.at[0])]
        else:
            copies = []
            for v in parts:
                for r in range(v.shape[0]):
                    m = len(copies)
                    copies.append(pltpu.make_async_copy(v.at[r], k_ref.at[at_ref[m]], sems.at[m]))
        for copy in copies:
            copy.start()
        fill(sz, x_ref[...].astype(F32), small, large)
        for copy in copies:
            copy.wait()
        back = pltpu.make_async_copy(k_ref, out_ref, sems.at[nblk])
        back.start()
        total = conv_rows(sz, x_ref[...], small, large, ysmall, ylarge, k_ref)
        s_ref[...] = total
        put_sums(sums_ref, total, total * total)
        back.wait()

    k = struct((nblk, 28, p, lanes), BF16)
    outs = [struct((sz.rows, 384), F32), struct((sz.nb, 2, 384), F32), k]
    scratch = [pltpu.VMEM(k.shape, BF16), pltpu.SemaphoreType.DMA((nblk + 1,))]
    return call(body, "conv_one", outs, maps(sz, c) + maps(sz, 384) + scratch, x, at, *pieces,
                flops=18 * sz.rows * c * 288, anywhere=range(2, 2 + n), out_anywhere=(2,))


def second_conv(sz, core, mine, other, ar, gain, shift, k):
    c = gain.shape[1]

    def body(core_ref, mine_ref, other_ref, ar_ref, g_ref, h_ref, k_ref, b_ref, s_ref, sums_ref,
             small, large, ysmall, ylarge):
        mean, inv = moments(ar_ref, sz.counted)
        p = g_ref[...] * ((ordered(core_ref, mine_ref, other_ref) - mean) * inv) + h_ref[...]
        b = (p * sigmoid(p)).astype(BF16)
        b_ref[...] = b
        fill(sz, b.astype(F32), small, large)
        total = conv_rows(sz, b, small, large, ysmall, ylarge, k_ref)
        s_ref[...] = total
        put_sums(sums_ref, total, total * total)

    outs = [struct((sz.rows, c), BF16), struct((sz.rows, 384), F32), struct((sz.nb, 2, 384), F32)]
    return call(body, "conv_two", outs, maps(sz, c) + maps(sz, 384),
                core, mine, other, ar, gain, shift, k, flops=18 * sz.rows * c * 288)


def frame_shift(sz, v, by):
    if by == 0:
        return v
    c = v.shape[1]
    v = v.reshape(-1, sz.group, c)
    frame = lax.broadcasted_iota(jnp.int32, (1, sz.group, c), 1) % sz.frames
    moved = pltpu.roll(v, (-by) % sz.group, 1)
    inside = (frame + by >= 0) & (frame + by < sz.frames)
    return jnp.where(inside, moved, 0.0).reshape(-1, c)


def norm_temporal(sz, core, s, ar, gain, shift, k, base):
    half = k.shape[0] * k.shape[2] // 2

    def body(core_ref, s_ref, ar_ref, g_ref, h_ref, k_ref, wide_ref, other_ref, mine_ref):
        mean, inv = moments(ar_ref, sz.counted)
        p = g_ref[...] * ((s_ref[...] - mean) * inv) + h_ref[...]
        a = (p * sigmoid(p)).astype(BF16).astype(F32)
        moved = [frame_shift(sz, a, by) for by in (-1, 0, 1)]
        rest = picked(moved[0][:, 256:], [moved[1][:, 256:], moved[2][:, 256:], jnp.zeros_like(a[:, 256:])])
        wide = jnp.concatenate([m[:, :256] for m in moved] + [rest], axis=1).astype(BF16)
        wide_ref[...] = wide
        for out_ref, h in ((other_ref, 1 - core_ref[0]), (mine_ref, core_ref[0])):
            right = tiles(k_ref, range(base, base + 7), h)
            t = lax.dot_general(wide, right, (((1,), (1,)), ((), ())), preferred_element_type=F32)
            out_ref[...] = t.astype(out_ref.dtype)

    outs = [struct((sz.rows, 896), BF16), struct((sz.rows, half), BF16), struct((sz.rows, half), F32)]
    return call(body, "norm_temporal", outs, [], core, s, ar, gain, shift, k,
                flops=6 * sz.rows * 2 * half * 288)


def half_sums(sz, core, mine, other):
    half = mine.shape[1]

    def body(core_ref, mine_ref, other_ref, sums_ref):
        t = ordered(core_ref, mine_ref, other_ref)
        put_sums(sums_ref, t, t * t)

    return call(body, "half_sums", [struct((sz.nb, 2, 2 * half), F32)], [], core, mine, other)[0]


def output_slope(sz, core, mine, other, ar, gain, shift, x, cot):
    c = x.shape[1]

    def body(core_ref, mine_ref, other_ref, ar_ref, g_ref, h_ref, x_ref, cot_ref, d_ref, sums_ref):
        mean, inv = moments(ar_ref, sz.counted)
        xhat = (ordered(core_ref, mine_ref, other_ref) - mean) * inv
        pre = x_ref[...].astype(F32) + (g_ref[...] * xhat + h_ref[...])
        d = cot_ref[...].astype(F32) * slope(pre)
        d_ref[...] = d
        put_sums(sums_ref, d * xhat, d)

    outs = [struct((sz.rows, c), F32), struct((sz.nb, 2, c), F32)]
    return call(body, "output_slope", outs, [], core, mine, other, ar, gain, shift, x, cot)


def own_output(sz, place, mine, other, ar, gain, shift, x, d):
    c = x.shape[1]
    n = sz.rows // sz.frames

    def body(place_ref, mine_ref, other_ref, ar_ref, g_ref, h_ref, x_ref, d_ref, out_ref, own_ref, woven):
        put_lanes(woven, d_ref[...])
        own_ref[...] = frame_of(sz, woven, place_ref[2])
        mean, inv = moments(ar_ref, sz.counted)
        xhat = (ordered(place_ref.at[pl.ds(1, 1)], mine_ref, other_ref) - mean) * inv
        pre = x_ref[...].astype(F32) + (g_ref[...] * xhat + h_ref[...])
        put_lanes(woven, pre * sigmoid(pre))
        out_ref[...] = frame_of(sz, woven, place_ref[2]).astype(BF16)

    outs = [struct((n, c), BF16), struct((n, c), F32)]
    return call(body, "own_output", outs, [lanes_of(sz, c)], place, mine, other, ar, gain, shift, x, d)


def temporal_back(sz, core, e, mine, other, ar, back, gain, shift, s, ar_s, gain_s, shift_s, k, base):
    c = gain.shape[1]
    given = len(e)

    def body(core_ref, *refs):
        e_refs, refs = refs[:given], refs[given:]
        (mine_ref, other_ref, ar_ref, back_ref, g_ref, h_ref, s_ref, ars_ref, gs_ref, hs_ref, k_ref,
         dt_ref, es_ref, sums_ref, got_ref) = refs
        mean, inv = moments(ar_ref, sz.counted)
        got = jnp.sum(back_ref[...], axis=0)
        got_ref[...] = got
        xhat = (ordered(core_ref, mine_ref, other_ref) - mean) * inv
        if given == 1:
            up = e_refs[0][...]
        else:
            up = ordered(core_ref, *e_refs) * slope(g_ref[...] * xhat + h_ref[...])
        d = g_ref[...] * inv * (up - (got[1:2] + xhat * got[0:1]) / sz.counted)
        d = d.astype(BF16)
        dt_ref[...] = d
        d = d.astype(F32)
        left = jnp.concatenate([frame_shift(sz, d, by).astype(BF16) for by in (1, 0, -1)], axis=1)
        right = jnp.concatenate([tiles(k_ref, (base + 2 * n, base + 2 * n + 1)) for n in range(3)], axis=0)
        main = jnp.dot(left, right, preferred_element_type=F32)
        y = jnp.dot(dt_ref[...], tile(k_ref, base + 6), preferred_element_type=F32)
        rest = picked(frame_shift(sz, y, 1), [y, frame_shift(sz, y, -1), jnp.zeros_like(y)])
        da = jnp.concatenate([main, folded(rest)], axis=1).astype(BF16).astype(F32)
        mean_s, inv_s = moments(ars_ref, sz.counted)
        xhat_s = (s_ref[...] - mean_s) * inv_s
        es = da * slope(gs_ref[...] * xhat_s + hs_ref[...])
        es_ref[...] = es
        put_sums(sums_ref, es * xhat_s, es)

    outs = [
        struct((sz.rows, c), BF16),
        struct((sz.rows, 384), F32),
        struct((sz.nb, 2, 384), F32),
        struct((2, c), F32),
    ]
    return call(body, "temporal_back", outs, [], core, *e, mine, other, ar, back, gain, shift,
                s, ar_s, gain_s, shift_s, k, flops=6 * sz.rows * c * 288)


def norm_back_rows(sz, e_ref, s_ref, ar_ref, back_ref, g_ref):
    mean, inv = moments(ar_ref, sz.counted)
    got = jnp.sum(back_ref[...], axis=0)
    xhat = (s_ref[...] - mean) * inv
    d = g_ref[...] * inv * (e_ref[...] - (got[1:2] + xhat * got[0:1]) / sz.counted)
    return d.astype(BF16).astype(F32), got


def rest_patches(sz, small, large):
    lanes = slice(256, 384)
    out = []
    for q in range(3):
        at = [window(sz, small, large, 2 - o // 3, 2 - o % 3, lanes) for o in range(4 * q, min(4 * q + 4, 9))]
        at += [jnp.zeros_like(at[0])] * (4 - len(at))
        out.append(picked(at[0], at[1:]).astype(BF16))
    return jnp.concatenate(out, axis=1)


def tall(sz):
    full = -(-sz.rows // 16) * 16
    quarter = -(-sz.rows // 64) * 16
    return full, quarter


def put_tall(sz, out_ref, d):
    full, quarter = tall(sz)
    pad = jnp.zeros((4 * quarter - sz.rows, 128), F32)
    for n in range(2):
        v = jnp.concatenate([d[:, 128 * n : 128 * n + 128], pad[: full - sz.rows]], axis=0)
        out_ref[n * full : n * full + full] = v.astype(BF16)
    rest = jnp.concatenate([d[:, 256:], pad], axis=0)
    at = [rest[quarter * g : quarter * g + quarter] for g in range(4)]
    out_ref[2 * full :] = picked(at[0], at[1:]).astype(BF16)


def get_tall(sz, ref):
    full, quarter = tall(sz)
    main = [ref[n * full : n * full + full].astype(F32)[: sz.rows] for n in range(2)]
    packed = ref[2 * full :].astype(F32)
    rest = [folded(jnp.where(lane_group(packed) == g, packed, 0.0)) for g in range(4)]
    rest = jnp.concatenate(rest, axis=0)[: sz.rows]
    return jnp.concatenate(main + [rest], axis=1)


def tall_struct(sz):
    full, quarter = tall(sz)
    return struct((2 * full + quarter, 128), BF16)


def norm_back(sz, e, s, ar, back, gain):
    def body(e_ref, s_ref, ar_ref, back_ref, g_ref, d_ref, got_ref):
        d, got = norm_back_rows(sz, e_ref, s_ref, ar_ref, back_ref, g_ref)
        got_ref[...] = got
        put_tall(sz, d_ref, d)

    outs = [tall_struct(sz), struct((2, 384), F32)]
    return call(body, "norm_back", outs, [], e, s, ar, back, gain)


def conv_back_halves(sz, core_ref, d, k_ref, small, large):
    fill(sz, d, small, large)
    rest = rest_patches(sz, small, large)
    for h in (1 - core_ref[0], core_ref[0]):
        total = None
        for i in range(3):
            left = jnp.concatenate(
                [window(sz, small, large, 2 - i, 2 - j, slice(0, 256)).astype(BF16) for j in range(3)],
                axis=1,
            )
            right = tiles(k_ref, range(6 * i, 6 * i + 6), h)
            if i == 2:
                left = jnp.concatenate([left, rest], axis=1)
                right = jnp.concatenate([right, tiles(k_ref, range(18, 21), h)], axis=1)
            one = lax.dot_general(left, right, (((1,), (1,)), ((), ())), preferred_element_type=F32)
            total = one if total is None else total + one
        yield total


def middle_back(sz, core, e, s, ar, back, gain, k, mine, other, ar_t, gain_t, shift_t, copies_of_sums):
    half = k.shape[0] * k.shape[2] // 2

    def body(core_ref, e_ref, s_ref, ar_ref, back_ref, g_ref, k_ref, mine_ref, other_ref, art_ref, gt_ref, ht_ref,
             dother_ref, dmine_ref, sums_ref, got_ref, d_ref, small, large):
        d, got = norm_back_rows(sz, e_ref, s_ref, ar_ref, back_ref, g_ref)
        got_ref[...] = got
        put_tall(sz, d_ref, d)
        mean, inv = moments(art_ref, sz.counted)
        swapped = core_ref[0] == 1
        found = []
        ends = ((dother_ref, other_ref, True), (dmine_ref, mine_ref, False))
        for (out_ref, t_ref, away), total in zip(ends, conv_back_halves(sz, core_ref, d, k_ref, small, large)):
            def part(v):
                first, second = v[:, :half], v[:, half:]
                if away:
                    first, second = second, first
                return jnp.where(swapped, second, first)

            xhat = (t_ref[...].astype(F32) - part(mean)) * part(inv)
            out_ref[...] = total.astype(out_ref.dtype)
            total = total * slope(part(gt_ref[...]) * xhat + part(ht_ref[...]))
            found.append(
                jnp.concatenate(
                    [jnp.sum(total * xhat, axis=0, keepdims=True), jnp.sum(total, axis=0, keepdims=True)], axis=0
                )
            )
        first = jnp.where(swapped, found[0], found[1])
        second = jnp.where(swapped, found[1], found[0])
        both = jnp.concatenate([first, second], axis=1)
        sums_ref[...] = jnp.broadcast_to(both[None], sums_ref.shape)

    outs = [
        struct((sz.rows, half), BF16),
        struct((sz.rows, half), F32),
        struct((copies_of_sums, 2, 2 * half), F32),
        struct((2, 384), F32),
        tall_struct(sz),
    ]
    return call(body, "middle_back", outs, maps(sz, 384), core, e, s, ar, back, gain, k,
                mine, other, ar_t, gain_t, shift_t, flops=18 * sz.rows * 2 * half * 288)


def input_back(sz, place, d, k):
    half = k.shape[0] * k.shape[2] // 2
    n = sz.rows // sz.frames

    def body(place_ref, d_ref, k_ref, other_ref, mine_ref, small, large, woven):
        rows = get_tall(sz, d_ref)
        core = place_ref[1]
        for h, total in zip((1 - core, core), conv_back_halves(sz, place_ref.at[pl.ds(1, 1)], rows, k_ref, small, large)):
            put_lanes(woven, total, h * (half // 128))
        for y in range(sz.frames // 2):
            other_ref[y] = frame_of(sz, woven, 2 * y + 1 - core).astype(BF16)
            mine_ref[y] = frame_of(sz, woven, 2 * y + core)

    outs = [struct((sz.frames // 2, n, 2 * half), BF16), struct((sz.frames // 2, n, 2 * half), F32)]
    return call(body, "input_back", outs, maps(sz, 384) + [lanes_of(sz, 2 * half)], place, d, k,
                flops=18 * sz.rows * 2 * half * 288)


def put_tiles(out_ref, at, v):
    nblk, _, p, _ = out_ref.shape
    v = v.astype(BF16)
    for n in range(v.shape[1] // 128):
        out_ref[:, at + n] = v[:, 128 * n : 128 * n + 128].reshape(nblk, p, 128)


def parity_rows(sz, v, odd):
    c, n = v.shape
    v = v.reshape(sz.nb // 2, 2, c // sz.nb, n)
    return jnp.where(odd, v[:, 1], v[:, 0]).reshape(c // 2, n)


def transposed(sz, place, x):
    c = x.shape[1]

    def body(place_ref, x_ref, keep_ref, send_ref):
        v = x_ref[...].astype(F32).T
        odd = place_ref[0] == 1
        put_wide(keep_ref, parity_rows(sz, v, odd))
        put_wide(send_ref, parity_rows(sz, v, jnp.logical_not(odd)))

    return call(body, "transposed", [wide_struct(sz, c)] * 2, [], place, x)


def temporal_kernel_grad(sz, place, dt, wide, nblk):
    c = dt.shape[1]

    def body(place_ref, dt_ref, wide_ref, keep_ref, send_ref):
        v = jnp.dot(dt_ref[...].T, wide_ref[...], preferred_element_type=F32)
        odd = place_ref[0] == 1
        put_tiles(keep_ref, 0, parity_rows(sz, v, odd))
        put_tiles(send_ref, 0, parity_rows(sz, v, jnp.logical_not(odd)))

    outs = [struct((nblk // 2, n_tiles(3), c // nblk, 128), BF16)] * 2
    return call(body, "temporal_kernel_grad", outs, [], place, dt, wide, flops=2 * dt.size * wide.shape[1])


def kernel_grads(sz, lefts, ds, temporals):
    c = lefts[0].shape[0]
    nblk, _, p, _ = temporals[0].shape

    def body(la_ref, lb_ref, da_ref, db_ref, ta_ref, tb_ref, out_ref, sa, la, sb, lb):
        fill(sz, get_tall(sz, da_ref), sa, la)
        fill(sz, get_tall(sz, db_ref), sb, lb)

        def grad(make):
            return jnp.dot(la_ref[:, : sz.rows], make(sa, la), preferred_element_type=F32) + jnp.dot(
                lb_ref[:, : sz.rows], make(sb, lb), preferred_element_type=F32
            )

        for o in range(9):
            put_tiles(
                out_ref, 2 * o,
                grad(lambda s, l: window(sz, s, l, 2 - o // 3, 2 - o % 3, slice(0, 256)).astype(BF16)),
            )
        put_tiles(out_ref, 18, grad(lambda s, l: rest_patches(sz, s, l)))
        for n in range(7):
            out_ref[:, 21 + n] = (ta_ref[:, n].astype(F32) + tb_ref[:, n].astype(F32)).astype(BF16)

    outs = [struct((nblk, 28, p, 128), BF16)]
    return call(body, "kernel_grads", outs, maps(sz, 384) + maps(sz, 384), *lefts, *ds, *temporals,
                flops=2 * 18 * sz.rows * c * 288)[0]


def body(
    input_small, input_large, spatial_one, temporal_one, spatial_two, temporal_two,
    mid_gain, mid_shift, out_gain, out_shift, cotangent_small, cotangent_large,
):
    clips = input_small.shape[0]
    frames = lax.axis_size("tm")
    nb = lax.axis_size("batch")
    hs, hl = input_small.shape[2], input_large.shape[2]
    places = hs * hs + hl * hl
    sz = Sizes(hs, hl, clips * frames, frames, nb, float(places * clips * frames * nb))
    t = lax.axis_index("tm")
    core = (t % 2).astype(jnp.int32).reshape(1)

    def to_rows(small, large):
        return jnp.concatenate(
            [v[:, 0].reshape(clips, -1, v.shape[-1]) for v in (small, large)], axis=1
        ).reshape(clips * places, -1)

    def from_rows(rows):
        v = rows.reshape(clips, places, -1)
        s = v[:, : sz.ns].reshape(clips, 1, hs, hs, -1)
        l = v[:, sz.ns :].reshape(clips, 1, hl, hl, -1)
        return s, l

    b = lax.axis_index("batch")
    place = jnp.stack([b % 2, t % 2, t]).astype(jnp.int32)
    parities = [[i for i in range(nb) if i % 2 == q] for q in range(2)]

    rows = to_rows(input_small, input_large)
    cot_rows = to_rows(cotangent_small, cotangent_large)

    def beside(far_rows):
        two = spread_tm(pack([spatial_two], [temporal_two]))
        acts, two = after(jnp.stack([rows, cot_rows, far_rows]), two)
        return two, acts, swap(acts, "tm", 1), swap(acts, "tm", 2)

    pieces, at, (two, acts, other_core, got), free = fetch(
        pack([spatial_one], [temporal_one]), [swap(rows, "batch", 1)], beside
    )
    x, cot, xt, xt_far = weave(sz, place, (acts, other_core, got, swap(got, "tm", 1)))
    two = gather_batch(after(two, *free)[0])
    nblk = two.shape[0]

    gm, sm = channels(mid_gain, t), channels(mid_shift, t)
    small = [gm[0:1], gm[1:2], sm[0:1], sm[1:2], out_gain[0:1], out_gain[1:2], out_shift[0:1], out_shift[1:2]]
    gm0, gm1, sm0, sm1, go0, go1, so0, so1, core, place, x = after(*small, core, place, x)

    s1, sums, one = first_conv(sz, x, pieces, at)
    ar1 = shared(sums)
    a1, other, own = norm_temporal(sz, core, s1, ar1, gm0, sm0, one, 21)
    t1m, t1o = sum_tm(own, other)
    ar2 = shared(half_sums(sz, core, t1m, t1o))
    b1, s2, sums = second_conv(sz, core, t1m, t1o, ar2, go0, so0, two)
    ar3 = shared(sums)
    a2, other, own = norm_temporal(sz, core, s2, ar3, gm1, sm1, two, 21)

    def beside_t2(sent):
        bt, bt_send = transposed(sz, place, after(b1, sent)[0])
        return bt, swap(bt_send, "batch", 1)

    t2m, t2o, bt, bt_far = sum_tm(own, other, beside_t2)
    ar4 = shared(half_sums(sz, core, t2m, t2o))
    dpre, sums = output_slope(sz, core, t2m, t2o, ar4, go1, so1, x, cot)
    back4 = shared(sums)
    dt2, e3, sums, n4 = temporal_back(
        sz, core, (dpre,), t2m, t2o, ar4, back4, go1, so1, s2, ar3, gm1, sm1, two, 21
    )
    back3 = shared(sums)
    other, own, sums, n3, ds2 = middle_back(
        sz, core, e3, s2, ar3, back3, gm1, two, t1m, t1o, ar2, go0, so0, nb * frames
    )
    back2 = lax.all_to_all(sums, ("batch", "tm"), 0, 0, tiled=True)

    def beside_d1(sent):
        away, dt, d, _ = after(ds2, dt2, dpre, sent)
        away = swap(away, "batch", 1)
        tb_grad, tb_send = temporal_kernel_grad(sz, place, dt, a2, nblk)
        d, tb_send = after(d, tb_send)
        return (back2, away, tb_grad, tb_send, *own_output(sz, place, t2m, t2o, ar4, go1, so1, x, d))

    d1m, d1o, back2, ds2_far, tb_grad, tb_send, own_out, own_dpre = sum_tm(own, other, beside_d1)
    tb_far = swap(tb_send, "batch", 1)
    out_s, out_l = from_rows(own_out)
    dt1, e1, sums, n2 = temporal_back(
        sz, core, (d1m, d1o), t1m, t1o, ar2, back2, go0, so0, s1, ar1, gm0, sm0, one, 21
    )
    ta_grad, ta_send = temporal_kernel_grad(sz, place, dt1, a1, nblk)
    ta_got = swap(ta_send, "batch", 1)
    dk_two = kernel_grads(sz, (bt, bt_far), (ds2, ds2_far), (tb_grad, tb_far))
    sum_two = lax.psum_scatter(
        owners(dk_two, nb // 2, frames), "batch", scatter_dimension=0, axis_index_groups=parities
    )
    sums, ta_grad, _ = after(sums, ta_grad, dk_two)
    back1 = shared(sums)
    back1, ta_got = after(back1, ta_got)
    ds1, n1 = norm_back(sz, e1, s1, ar1, back1, gm0)
    ds1_got = swap(ds1, "batch", 1)
    other, own = input_back(sz, place, ds1, one)
    ds1_got, ta_got, other, own = after(ds1_got, ta_got, other, own)
    dk_one = kernel_grads(sz, (xt, xt_far), (ds1, ds1_got), (ta_grad, ta_got))
    moved = lax.all_to_all(
        owners(dk_one, nb // 2, frames).reshape((nb // 2 * frames, dk_one.shape[1], -1, 128)),
        ("batch", "tm"), 0, 0, tiled=True,
        axis_index_groups=[[i * frames + j for i in g for j in range(frames)] for g in parities],
    )
    sum_two, own, _ = after(sum_two, own, dk_one)
    grad_s, grad_l = from_rows(own_dpre + scatter_tm(own, other))
    grad_sb, grad_tb = unpack(spread_tm(sum_two)[None], 1, 1)

    n13 = jnp.stack([n1, n3], axis=1)
    n13 = pair(n13, swap(n13, "tm", 2), t // 2)
    n13 = jnp.swapaxes(pair(n13, swap(n13, "tm", 1), t % 2), 0, 1).reshape((frames, 4, 384))
    moved, grad_sb, grad_tb, n13 = after(moved, grad_sb, grad_tb, n13)
    grad_sa, grad_ta = unpack(moved.reshape((nb // 2, frames) + moved.shape[1:]), 1, 1)
    mids = all_channels(n13).reshape(2, 2, -1)
    return (
        out_s, out_l, grad_s, grad_l, grad_sa, grad_ta, grad_sb, grad_tb,
        mids[0], mids[1], jnp.stack([n2[0], n4[0]]), jnp.stack([n2[1], n4[1]]),
    )


def solution(mesh):
    act = P("batch", "tm", None, None, None)
    rows = P(None, ("batch", "tm"), None)
    cols = P(None, None, ("batch", "tm"))
    return jax.shard_map(
        body,
        mesh=mesh,
        in_specs=(act, act, rows, cols, rows, cols, P(), P(), P(), P(), act, act),
        out_specs=(act, act, act, act, rows, cols, rows, cols, P(), P(), P(), P()),
        check_vma=False,
    )
```

```python
import math

import jax
import jax.numpy as jnp
from jax import lax
from jax.experimental import pallas as pl
from jax.experimental.pallas import tpu as pltpu
from jax.sharding import PartitionSpec as P

EPS = 1e-05
F32 = jnp.float32
BF16 = jnp.bfloat16
VMEM_LIMIT = 30 * 1024 * 1024


def swap(value, axis, bit):
    n = lax.axis_size(axis)
    return lax.ppermute(value, axis, [(i, i ^ bit) for i in range(n)])


def shared(copies):
    return lax.all_to_all(copies, "batch", 0, 0, tiled=True)


def tm_bits():
    t = lax.axis_index("tm")
    return t % 2, t // 2


def pair(first, second, bit):
    return jnp.where(bit == 0, jnp.stack([first, second]), jnp.stack([second, first]))


def after(value, *others):
    return lax.optimization_barrier((value,) + others)


def sum_tm(mine, other, beside=None):
    mine = (mine.astype(F32) + swap(other, "tm", 1).astype(F32)).astype(BF16)
    got, *there = after(swap(mine, "tm", 2), *(beside(mine) if beside else ()))
    mine = (mine.astype(F32) + got.astype(F32)).astype(BF16)
    return (mine, swap(mine, "tm", 1), *there)


def scatter_tm(mine, other):
    _, y = tm_bits()
    mine = mine + swap(other, "tm", 1).astype(F32)
    own = lax.dynamic_index_in_dim(mine, y, 0, keepdims=False)
    away = lax.dynamic_index_in_dim(mine, 1 - y, 0, keepdims=False)
    return own + swap(away.astype(BF16), "tm", 2).astype(F32)


TILES = 27
REST = 24


def tiled(x):
    k, p, _ = x.shape
    q = -(-k // 4)
    main = x[:, :, :1024].reshape(k, p, 4, 2, 128)
    main = jnp.transpose(main, (2, 0, 3, 1, 4)).reshape(4, 2 * k, p, 128)
    rest = jnp.pad(x[:, :, 1024:], ((0, 4 * q - k), (0, 0), (0, 0))).reshape(q, 4, p, 4, 32)
    rest = jnp.transpose(rest, (3, 0, 2, 1, 4)).reshape(4, q, p, 128)
    return jnp.concatenate([main, rest], axis=1)


def untiled(y):
    k, p = 12, y.shape[2]
    q = -(-k // 4)
    main = jnp.transpose(y[:, : 2 * k].reshape(4, k, 2, p, 128), (1, 3, 0, 2, 4)).reshape(k, p, 1024)
    rest = y[:, 2 * k :].reshape(4, q, p, 4, 32)
    rest = jnp.transpose(rest, (1, 3, 2, 0, 4)).reshape(4 * q, p, 128)[:k]
    return jnp.concatenate([main, rest], axis=2)


def pack(spatial, temporal):
    temporal = jnp.swapaxes(temporal, 1, 2)
    p = spatial.shape[1]
    if p % 16:
        return tiled(jnp.concatenate([spatial, temporal]))

    def body(s_ref, t_ref, out_ref):
        rows = [s_ref[o].astype(F32) for o in range(9)] + [t_ref[o].astype(F32) for o in range(3)]
        group = lax.broadcasted_iota(jnp.int32, (p, 128), 1) // 32
        for t in range(4):
            for o in range(12):
                for h in range(2):
                    lane = 256 * t + 128 * h
                    out_ref[t, 2 * o + h] = rows[o][:, lane : lane + 128].astype(BF16)
            for q in range(3):
                tile = jnp.zeros((p, 128), F32)
                for r in range(4):
                    moved = pltpu.roll(rows[4 * q + r][:, 1024:], (32 * (r - t)) % 128, 1)
                    tile = jnp.where(group == r, moved, tile)
                out_ref[t, REST + q] = tile.astype(BF16)

    return call(body, "pack", [struct((4, TILES, p, 128), BF16)], [], spatial, temporal)[0]


def turned_tm(packed):
    t = lax.axis_index("tm")
    got = []
    for s in range(4):
        piece = lax.dynamic_index_in_dim(packed, t ^ s, 0, keepdims=False)
        got.append(swap(piece, "tm", s) if s else piece)
    return jnp.stack(got)


def spread_tm(packed):
    t = lax.axis_index("tm")
    got = turned_tm(packed)
    return jnp.stack([lax.dynamic_index_in_dim(got, t ^ s, 0, keepdims=False) for s in range(4)])


def blocks(whole):
    nb, nt, tiles, p, _ = whole.shape
    if p % 16 == 0:
        return whole.reshape(nb * nt, tiles, p, 128)
    v = jnp.moveaxis(whole.reshape(2, nb * nt // 2, tiles, p, 128), 2, 1)
    return v.reshape(2, tiles, nb * nt // 2 * p, 128)


def gather_batch(moved):
    return blocks(lax.all_gather(moved, "batch", axis=0))


def fetch(packed, ahead, beside):
    nb = lax.axis_size("batch")
    if nb != 8 or packed.shape[2] % 16:
        return [gather_batch(spread_tm(packed))], jnp.zeros((1,), jnp.int32), beside(*ahead), []
    b, t = lax.axis_index("batch"), lax.axis_index("tm")
    z, x = b // 2, b % 2

    def turn(u, by):
        return lax.ppermute(u, "batch", [(i, (i + by) % 8) for i in range(8)])

    v, *ahead = after(turned_tm(packed), *ahead)
    below, far = after(turn(v, 2), swap(v, "batch", 1))
    v, *ahead = after(v, below, *ahead)
    there = beside(*ahead[1:])
    above, far_below = after(turn(v, -2), swap(below, "batch", 1))
    opposite = [turn(after(below[:2], above)[0], 2), turn(above[2:], -2)]
    far_above = swap(above, "batch", 1)
    far_above, *there = after(far_above, *opposite, *there)
    opposite, there = there[:2], there[2:]
    far_opposite = [swap(o, "batch", 1) for o in opposite]
    pieces = [v, below, above] + opposite + [far, far_below, far_above] + far_opposite
    zs = [z, z - 1, z + 1, z + 2, z + 2]
    rows = [range(4), range(4), range(4), range(2), range(2, 4)]
    at = [4 * (2 * (w % 4) + x) + (t ^ r) for w, rs in zip(zs, rows) for r in rs]
    at += [4 * (2 * (w % 4) + 1 - x) + (t ^ r) for w, rs in zip(zs, rows) for r in rs]
    return pieces, jnp.stack(at).astype(jnp.int32), there, [far_above]


def owners(grads, nb, nt):
    nblk, tiles, p, _ = grads.shape
    if nblk == nb * nt:
        return grads.reshape(nb, nt, tiles, p, 128)
    own = nblk * p // (nb * nt)
    v = grads.reshape(nblk, tiles, nb * nt // nblk, own, 128)
    return jnp.moveaxis(v, 2, 1).reshape(nb, nt, tiles, own, 128)


def unpack(parts):
    n, _, total, p, _ = parts.shape
    if p % 16:
        summed = untiled(jnp.sum(parts.astype(F32), axis=0))
        return summed[:9], jnp.swapaxes(summed[9:], 1, 2)

    def body(in_ref, s_ref, t_ref):
        group = lax.broadcasted_iota(jnp.int32, (p, 128), 1) // 32

        def tile(t, i):
            v = in_ref[0, t, i].astype(F32)
            for m in range(1, n):
                v = v + in_ref[m, t, i].astype(F32)
            return v

        rest = [[tile(t, REST + q) for t in range(4)] for q in range(3)]
        for o in range(12):
            pieces = [tile(t, 2 * o + h) for t in range(4) for h in range(2)]
            last = jnp.zeros((p, 128), F32)
            for t in range(4):
                moved = pltpu.roll(rest[o // 4][t], (32 * (t - o % 4)) % 128, 1)
                last = jnp.where(group == t, moved, last)
            whole = jnp.concatenate(pieces + [last], axis=1)
            if o < 9:
                s_ref[o] = whole
            else:
                t_ref[o - 9] = whole

    spatial, temporal = call(body, "unpack", [struct((k, p, 1152), F32) for k in (9, 3)], [], parts)
    return spatial, jnp.swapaxes(temporal, 1, 2)


def channels(v, t):
    main = lax.dynamic_slice_in_dim(v, 256 * t, 256, v.ndim - 1)
    rest = lax.dynamic_slice_in_dim(v, 1024 + 32 * t, 32, v.ndim - 1)
    return jnp.concatenate([main] + [rest] * 4, axis=-1)


def all_channels(v):
    main = jnp.moveaxis(v[..., :256], 0, -2)
    rest = jnp.moveaxis(v[..., 256:288], 0, -2)
    lead = main.shape[:-2]
    return jnp.concatenate([main.reshape(lead + (-1,)), rest.reshape(lead + (-1,))], axis=-1)


class Sizes:
    def __init__(self, hs, hl, group, frames, nb, counted):
        self.hs, self.hl, self.group, self.frames, self.nb = hs, hl, group, frames, nb
        self.ns, self.nl = hs * hs, hl * hl
        self.cut = self.ns * group
        self.rows = (self.ns + self.nl) * group
        self.counted = counted


def call(body, name, outs, scratch, *args, flops=0, anywhere=(), out_anywhere=()):
    smem = pl.BlockSpec(memory_space=pltpu.SMEM)
    vmem = pl.BlockSpec(memory_space=pltpu.VMEM)
    hbm = pl.BlockSpec(memory_space=pl.ANY)
    moved = sum(math.prod(a.shape) * a.dtype.itemsize for a in (*args, *outs))
    return pl.pallas_call(
        body,
        out_shape=outs,
        in_specs=[
            smem if a.dtype == jnp.int32 else hbm if n in anywhere else vmem for n, a in enumerate(args)
        ],
        out_specs=[hbm if n in out_anywhere else vmem for n in range(len(outs))],
        scratch_shapes=scratch,
        name=name,
        compiler_params=pltpu.CompilerParams(vmem_limit_bytes=VMEM_LIMIT),
        cost_estimate=pl.CostEstimate(flops=flops, bytes_accessed=moved, transcendentals=0),
    )(*args)


def struct(shape, dtype):
    return jax.ShapeDtypeStruct(shape, dtype)


def moments(ar_ref, counted):
    s = jnp.sum(ar_ref[...], axis=0)
    mean = s[0:1] / counted
    return mean, lax.rsqrt(s[1:2] / counted - mean * mean + EPS)


def put_sums(out_ref, first, second):
    both = jnp.concatenate(
        [jnp.sum(first, axis=0, keepdims=True), jnp.sum(second, axis=0, keepdims=True)], axis=0
    )
    out_ref[...] = jnp.broadcast_to(both[None], out_ref.shape)


def sigmoid(v):
    return 1.0 / (1.0 + jnp.exp(-v))


def slope(v):
    sig = sigmoid(v)
    return sig * (1.0 + v * (1.0 - sig))


def ordered(core_ref, mine_ref, other_ref):
    first = core_ref[0] == 0
    mine, other = mine_ref[...].astype(F32), other_ref[...].astype(F32)
    return jnp.concatenate([jnp.where(first, mine, other), jnp.where(first, other, mine)], axis=1)


def fill(sz, rows, small_ref, large_ref):
    c = rows.shape[1]
    for ref, h, v in (
        (small_ref, sz.hs, rows[: sz.cut]),
        (large_ref, sz.hl, rows[sz.cut :]),
    ):
        ref[...] = jnp.zeros(ref.shape, F32)
        ref[1 : h + 1, 1 : h + 1] = v.reshape(h, h, sz.group, c)


def window(sz, small_ref, large_ref, i, j, lanes):
    c = lanes.stop - lanes.start
    s = small_ref[i : i + sz.hs, j : j + sz.hs, :, lanes].reshape(sz.cut, c)
    l = large_ref[i : i + sz.hl, j : j + sz.hl, :, lanes].reshape(sz.rows - sz.cut, c)
    return jnp.concatenate([s, l], axis=0)


def tile(k_ref, n, half=None):
    nblk, _, p, lanes = k_ref.shape
    if half is None:
        return k_ref[:, n].reshape(nblk * p, lanes)
    return k_ref[pl.ds(half * (nblk // 2), nblk // 2), n].reshape(nblk // 2 * p, lanes)


def tiles(k_ref, ns, half=None):
    return jnp.concatenate([tile(k_ref, n, half) for n in ns], axis=1)


def lane_group(v):
    return lax.broadcasted_iota(jnp.int32, (1, v.shape[1]), 1) // 32


def folded(v):
    v = v + pltpu.roll(v, 32, 1)
    return v + pltpu.roll(v, 64, 1)


def picked(first, rest):
    out = first
    for r, v in enumerate(rest):
        out = jnp.where(lane_group(first) == r + 1, v, out)
    return out


def conv_rows(sz, xb, small, large, ysmall, ylarge, k_ref):
    c = xb.shape[1]
    every = slice(0, c)
    main = None
    for i in range(3):
        left = jnp.concatenate(
            [window(sz, small, large, i, j, every).astype(BF16) for j in range(3)], axis=1
        )
        right = jnp.concatenate(
            [tiles(k_ref, (6 * i + 2 * j, 6 * i + 2 * j + 1)) for j in range(3)], axis=0
        )
        d = jnp.dot(left, right, preferred_element_type=F32)
        main = d if main is None else main + d
    y = jnp.dot(xb, tiles(k_ref, range(REST, REST + 3)), preferred_element_type=F32)
    fill(sz, y, ysmall, ylarge)
    rest = window(sz, ysmall, ylarge, 2, 2, slice(256, 384))
    rest = jnp.where(lane_group(rest) == 0, rest, 0.0)
    for q in range(2):
        at = [window(sz, ysmall, ylarge, (4 * q + r) // 3, (4 * q + r) % 3, slice(128 * q, 128 * q + 128)) for r in range(4)]
        rest = rest + picked(at[0], at[1:])
    return jnp.concatenate([main, folded(rest)], axis=1)


def maps(sz, c):
    def one(h):
        return pltpu.VMEM((h + 2, h + 2, sz.group, c), F32)

    return [one(sz.hs), one(sz.hl)]


def wide_struct(sz, c):
    return struct((c // 2, -(-sz.rows // 128) * 128), BF16)


def put_wide(out_ref, v):
    pad = jnp.zeros((v.shape[0], out_ref.shape[1] - v.shape[1]), F32)
    out_ref[...] = jnp.concatenate([v, pad], axis=1).astype(BF16)


def lanes_of(sz, c):
    return pltpu.VMEM((c // 128, sz.rows, 128), F32)


def put_lanes(woven, v, at=0):
    for n in range(v.shape[1] // 128):
        woven[at + n] = v[:, 128 * n : 128 * n + 128]


def weave(sz, place, frames_of):
    _, n, c = frames_of[0].shape
    places = sz.rows // sz.group
    clips = sz.group // sz.frames

    def body(place_ref, *refs):
        srcs, (rows_ref, cot_rows_ref, xt_ref, ft_ref, woven) = refs[:4], refs[4:]
        for a, dst, turned in ((1, cot_rows_ref, None), (0, rows_ref, xt_ref), (2, None, ft_ref)):
            for s, src in enumerate(srcs):
                v = src[a].astype(F32)
                f = place_ref[2] ^ s
                for m in range(clips):
                    rows = v[places * m : places * m + places]
                    for n in range(c // 128):
                        woven[n, pl.ds(sz.frames * m + f, places, stride=sz.group)] = rows[:, 128 * n : 128 * n + 128]
            if dst is not None:
                for n in range(c // 128):
                    dst[:, 128 * n : 128 * n + 128] = woven[n].astype(BF16)
            if turned is not None:
                v = jnp.concatenate([woven[n] for n in range(c // 128)], axis=1).T
                put_wide(turned, parity_rows(sz, v, place_ref[0] == 1))

    outs = [struct((sz.rows, c), BF16)] * 2 + [wide_struct(sz, c)] * 2
    return call(body, "weave", outs, [lanes_of(sz, c)], place, *frames_of)


def frame_of(sz, woven, frame):
    places = sz.rows // sz.group
    out = []
    for m in range(sz.group // sz.frames):
        at = pl.ds(sz.frames * m + frame, places, stride=sz.group)
        out.append(jnp.concatenate([woven[n, at] for n in range(woven.shape[0])], axis=1))
    return jnp.concatenate(out, axis=0)


def first_conv(sz, x, pieces, at):
    c = x.shape[1]
    n = len(pieces)
    nblk = sum(v.shape[0] for v in pieces)
    _, _, p, lanes = pieces[0].shape
    whole = n == 1

    def body(x_ref, at_ref, *refs):
        parts, (s_ref, sums_ref, out_ref) = refs[:n], refs[n : n + 3]
        small, large, ysmall, ylarge, k_ref, sems = refs[n + 3 :]
        if whole:
            copies = [pltpu.make_async_copy(parts[0], k_ref, sems.at[0])]
        else:
            copies = []
            for v in parts:
                for r in range(v.shape[0]):
                    m = len(copies)
                    copies.append(pltpu.make_async_copy(v.at[r], k_ref.at[at_ref[m]], sems.at[m]))
        for copy in copies:
            copy.start()
        fill(sz, x_ref[...].astype(F32), small, large)
        for copy in copies:
            copy.wait()
        back = pltpu.make_async_copy(k_ref, out_ref, sems.at[nblk])
        back.start()
        total = conv_rows(sz, x_ref[...], small, large, ysmall, ylarge, k_ref)
        s_ref[...] = total
        put_sums(sums_ref, total, total * total)
        back.wait()

    k = struct((nblk, TILES, p, lanes), BF16)
    outs = [struct((sz.rows, 384), F32), struct((sz.nb, 2, 384), F32), k]
    scratch = [pltpu.VMEM(k.shape, BF16), pltpu.SemaphoreType.DMA((nblk + 1,))]
    return call(body, "conv_one", outs, maps(sz, c) + maps(sz, 384) + scratch, x, at, *pieces,
                flops=18 * sz.rows * c * 288, anywhere=range(2, 2 + n), out_anywhere=(2,))


def second_conv(sz, core, mine, other, ar, gain, shift, k):
    c = gain.shape[1]

    def body(core_ref, mine_ref, other_ref, ar_ref, g_ref, h_ref, k_ref, b_ref, s_ref, sums_ref,
             small, large, ysmall, ylarge):
        mean, inv = moments(ar_ref, sz.counted)
        p = g_ref[...] * ((ordered(core_ref, mine_ref, other_ref) - mean) * inv) + h_ref[...]
        b = (p * sigmoid(p)).astype(BF16)
        b_ref[...] = b
        fill(sz, b.astype(F32), small, large)
        total = conv_rows(sz, b, small, large, ysmall, ylarge, k_ref)
        s_ref[...] = total
        put_sums(sums_ref, total, total * total)

    outs = [struct((sz.rows, c), BF16), struct((sz.rows, 384), F32), struct((sz.nb, 2, 384), F32)]
    return call(body, "conv_two", outs, maps(sz, c) + maps(sz, 384),
                core, mine, other, ar, gain, shift, k, flops=18 * sz.rows * c * 288)


def frame_shift(sz, v, by):
    if by == 0:
        return v
    c = v.shape[1]
    v = v.reshape(-1, sz.group, c)
    frame = lax.broadcasted_iota(jnp.int32, (1, sz.group, c), 1) % sz.frames
    moved = pltpu.roll(v, (-by) % sz.group, 1)
    inside = (frame + by >= 0) & (frame + by < sz.frames)
    return jnp.where(inside, moved, 0.0).reshape(-1, c)


def norm_temporal(sz, place, s, ar, gain, shift, k):
    half = k.shape[0] * k.shape[2] // 2
    part = half // 2

    def body(place_ref, s_ref, ar_ref, g_ref, h_ref, k_ref, wide_ref, o1_ref, o0_ref, m1_ref, m0_ref):
        core, low = place_ref[1], place_ref[2] < 2
        mean, inv = moments(ar_ref, sz.counted)
        p = g_ref[...] * ((s_ref[...] - mean) * inv) + h_ref[...]
        a = (p * sigmoid(p)).astype(BF16).astype(F32)
        moved = [frame_shift(sz, a, by) for by in (-1, 0, 1)]
        rest = picked(jnp.zeros_like(a[:, 256:]), [m[:, 256:] for m in moved])
        wide = jnp.concatenate([m[:, :256] for m in moved] + [rest], axis=1).astype(BF16)
        wide_ref[...] = wide
        for away_ref, keep_ref, h in ((o1_ref, o0_ref, 1 - core), (m1_ref, m0_ref, core)):
            right = tiles(k_ref, (*range(18, 24), REST + 2), h)
            t = lax.dot_general(wide, right, (((1,), (1,)), ((), ())), preferred_element_type=F32)
            away_ref[...] = jnp.where(low, t[:, part:], t[:, :part]).astype(away_ref.dtype)
            keep_ref[...] = jnp.where(low, t[:, :part], t[:, part:]).astype(keep_ref.dtype)

    outs = [struct((sz.rows, 896), BF16)] + [struct((sz.rows, part), d) for d in (BF16, BF16, F32, F32)]
    return call(body, "norm_temporal", outs, [], place, s, ar, gain, shift, k,
                flops=6 * sz.rows * 2 * half * 288)


def quarter_sums(sz, mine, got_core, got_y):
    def body(mine_ref, core_ref, y_ref, q_ref, sums_ref):
        v = (mine_ref[...] + core_ref[...].astype(F32)).astype(BF16).astype(F32) + y_ref[...].astype(F32)
        v = v.astype(BF16)
        q_ref[...] = v
        v = v.astype(F32)
        put_sums(sums_ref, v, v * v)

    part = mine.shape[1]
    outs = [struct((sz.rows, part), BF16), struct((2 * sz.nb, 2, part), F32)]
    return call(body, "quarter_sums", outs, [], mine, got_core, got_y)


def joined(sz, place, quarters, ars):
    part = quarters[0].shape[1]

    def body(place_ref, q0_ref, q1_ref, c0_ref, c1_ref, ma_ref, ca_ref, mine_ref, other_ref, sums_ref):
        first, low = place_ref[1] == 0, place_ref[2] < 2
        for own, away, out_ref in ((q0_ref, q1_ref, mine_ref), (c0_ref, c1_ref, other_ref)):
            a, b = own[...].astype(F32), away[...].astype(F32)
            v = jnp.concatenate([jnp.where(low, a, b), jnp.where(low, b, a)], axis=1)
            out_ref[...] = v.astype(BF16)

        def total(ref):
            return jnp.concatenate(
                [sum(ref[2 * m + y] for m in range(1, sz.nb)) + ref[y] for y in range(2)], axis=1
            )

        m, o = total(ma_ref), total(ca_ref)
        sums_ref[0] = jnp.concatenate([jnp.where(first, m, o), jnp.where(first, o, m)], axis=1)

    outs = [struct((sz.rows, 2 * part), BF16)] * 2 + [struct((1, 2, 4 * part), F32)]
    return call(body, "joined", outs, [], place, *quarters, *ars)


def exchange(sz, place, o1, o0, m1, m0, beside=None):
    nt = lax.axis_size("tm")
    got1, got0 = swap(o1, "tm", 1), swap(o0, "tm", 1)
    sent = (m1 + got1.astype(F32)).astype(BF16)
    there = beside(sent) if beside else ()
    q, sums = quarter_sums(sz, m0, got0, swap(sent, "tm", 2))
    groups = [[nt * b + 2 * y + c for b in range(sz.nb) for y in range(nt // 2)] for c in range(2)]
    ar = lax.all_to_all(sums, ("batch", "tm"), 0, 0, tiled=True, axis_index_groups=groups)
    back = swap(q, "tm", 2)
    own_core = swap(q, "tm", 1)
    back, ar, own_core, *there = after(back, ar, own_core, *there)
    quarters = (q, back, own_core, swap(back, "tm", 1))
    return (*joined(sz, place, quarters, (ar, swap(ar, "tm", 1))), *there)


def output_slope(sz, core, mine, other, ar, gain, shift, x, cot):
    c = x.shape[1]

    def body(core_ref, mine_ref, other_ref, ar_ref, g_ref, h_ref, x_ref, cot_ref, d_ref, sums_ref):
        mean, inv = moments(ar_ref, sz.counted)
        xhat = (ordered(core_ref, mine_ref, other_ref) - mean) * inv
        pre = x_ref[...].astype(F32) + (g_ref[...] * xhat + h_ref[...])
        d = cot_ref[...].astype(F32) * slope(pre)
        d_ref[...] = d
        put_sums(sums_ref, d * xhat, d)

    outs = [struct((sz.rows, c), F32), struct((sz.nb, 2, c), F32)]
    return call(body, "output_slope", outs, [], core, mine, other, ar, gain, shift, x, cot)


def own_output(sz, place, mine, other, ar, gain, shift, x, d):
    c = x.shape[1]
    n = sz.rows // sz.frames

    def body(place_ref, mine_ref, other_ref, ar_ref, g_ref, h_ref, x_ref, d_ref, out_ref, own_ref, woven):
        put_lanes(woven, d_ref[...])
        own_ref[...] = frame_of(sz, woven, place_ref[2])
        mean, inv = moments(ar_ref, sz.counted)
        xhat = (ordered(place_ref.at[pl.ds(1, 1)], mine_ref, other_ref) - mean) * inv
        pre = x_ref[...].astype(F32) + (g_ref[...] * xhat + h_ref[...])
        put_lanes(woven, pre * sigmoid(pre))
        out_ref[...] = frame_of(sz, woven, place_ref[2]).astype(BF16)

    outs = [struct((n, c), BF16), struct((n, c), F32)]
    return call(body, "own_output", outs, [lanes_of(sz, c)], place, mine, other, ar, gain, shift, x, d)


def temporal_back(sz, core, e, mine, other, ar, back, gain, shift, s, ar_s, gain_s, shift_s, k):
    c = gain.shape[1]
    given = len(e)

    def body(core_ref, *refs):
        e_refs, refs = refs[:given], refs[given:]
        (mine_ref, other_ref, ar_ref, back_ref, g_ref, h_ref, s_ref, ars_ref, gs_ref, hs_ref, k_ref,
         dt_ref, es_ref, sums_ref, got_ref) = refs
        mean, inv = moments(ar_ref, sz.counted)
        got = jnp.sum(back_ref[...], axis=0)
        got_ref[...] = got
        xhat = (ordered(core_ref, mine_ref, other_ref) - mean) * inv
        if given == 1:
            up = e_refs[0][...]
        else:
            up = ordered(core_ref, *e_refs) * slope(g_ref[...] * xhat + h_ref[...])
        d = g_ref[...] * inv * (up - (got[1:2] + xhat * got[0:1]) / sz.counted)
        d = d.astype(BF16)
        dt_ref[...] = d
        d = d.astype(F32)
        left = jnp.concatenate([frame_shift(sz, d, by).astype(BF16) for by in (1, 0, -1)], axis=1)
        right = jnp.concatenate([tiles(k_ref, (18 + 2 * n, 19 + 2 * n)) for n in range(3)], axis=0)
        main = jnp.dot(left, right, preferred_element_type=F32)
        y = jnp.dot(dt_ref[...], tile(k_ref, REST + 2), preferred_element_type=F32)
        rest = picked(jnp.zeros_like(y), [frame_shift(sz, y, by) for by in (1, 0, -1)])
        da = jnp.concatenate([main, folded(rest)], axis=1).astype(BF16).astype(F32)
        mean_s, inv_s = moments(ars_ref, sz.counted)
        xhat_s = (s_ref[...] - mean_s) * inv_s
        es = da * slope(gs_ref[...] * xhat_s + hs_ref[...])
        es_ref[...] = es
        put_sums(sums_ref, es * xhat_s, es)

    outs = [
        struct((sz.rows, c), BF16),
        struct((sz.rows, 384), F32),
        struct((sz.nb, 2, 384), F32),
        struct((2, c), F32),
    ]
    return call(body, "temporal_back", outs, [], core, *e, mine, other, ar, back, gain, shift,
                s, ar_s, gain_s, shift_s, k, flops=6 * sz.rows * c * 288)


def norm_back_rows(sz, e_ref, s_ref, ar_ref, back_ref, g_ref):
    mean, inv = moments(ar_ref, sz.counted)
    got = jnp.sum(back_ref[...], axis=0)
    xhat = (s_ref[...] - mean) * inv
    d = g_ref[...] * inv * (e_ref[...] - (got[1:2] + xhat * got[0:1]) / sz.counted)
    return d.astype(BF16).astype(F32), got


def rest_patches(sz, small, large):
    lanes = slice(256, 384)
    out = []
    for q in range(3):
        at = [window(sz, small, large, 2 - o // 3, 2 - o % 3, lanes) for o in range(4 * q, min(4 * q + 4, 9))]
        at += [jnp.zeros_like(at[0])] * (4 - len(at))
        out.append(picked(at[0], at[1:]).astype(BF16))
    return jnp.concatenate(out, axis=1)


def tall(sz):
    full = -(-sz.rows // 16) * 16
    quarter = -(-sz.rows // 64) * 16
    return full, quarter


def put_tall(sz, out_ref, d):
    full, quarter = tall(sz)
    pad = jnp.zeros((4 * quarter - sz.rows, 128), F32)
    for n in range(2):
        v = jnp.concatenate([d[:, 128 * n : 128 * n + 128], pad[: full - sz.rows]], axis=0)
        out_ref[n * full : n * full + full] = v.astype(BF16)
    rest = jnp.concatenate([d[:, 256:], pad], axis=0)
    at = [rest[quarter * g : quarter * g + quarter] for g in range(4)]
    out_ref[2 * full :] = picked(at[0], at[1:]).astype(BF16)


def get_tall(sz, ref):
    full, quarter = tall(sz)
    main = [ref[n * full : n * full + full].astype(F32)[: sz.rows] for n in range(2)]
    packed = ref[2 * full :].astype(F32)
    rest = [folded(jnp.where(lane_group(packed) == g, packed, 0.0)) for g in range(4)]
    rest = jnp.concatenate(rest, axis=0)[: sz.rows]
    return jnp.concatenate(main + [rest], axis=1)


def tall_struct(sz):
    full, quarter = tall(sz)
    return struct((2 * full + quarter, 128), BF16)


def norm_back(sz, e, s, ar, back, gain):
    def body(e_ref, s_ref, ar_ref, back_ref, g_ref, d_ref, got_ref):
        d, got = norm_back_rows(sz, e_ref, s_ref, ar_ref, back_ref, g_ref)
        got_ref[...] = got
        put_tall(sz, d_ref, d)

    outs = [tall_struct(sz), struct((2, 384), F32)]
    return call(body, "norm_back", outs, [], e, s, ar, back, gain)


def conv_back_halves(sz, core_ref, d, k_ref, small, large):
    fill(sz, d, small, large)
    rest = rest_patches(sz, small, large)
    for h in (1 - core_ref[0], core_ref[0]):
        total = None
        for i in range(3):
            left = jnp.concatenate(
                [window(sz, small, large, 2 - i, 2 - j, slice(0, 256)).astype(BF16) for j in range(3)],
                axis=1,
            )
            right = tiles(k_ref, range(6 * i, 6 * i + 6), h)
            if i == 2:
                left = jnp.concatenate([left, rest], axis=1)
                right = jnp.concatenate([right, tiles(k_ref, range(REST, REST + 3), h)], axis=1)
            one = lax.dot_general(left, right, (((1,), (1,)), ((), ())), preferred_element_type=F32)
            total = one if total is None else total + one
        yield total


def middle_back(sz, core, e, s, ar, back, gain, k, mine, other, ar_t, gain_t, shift_t, copies_of_sums):
    half = k.shape[0] * k.shape[2] // 2

    def body(core_ref, e_ref, s_ref, ar_ref, back_ref, g_ref, k_ref, mine_ref, other_ref, art_ref, gt_ref, ht_ref,
             dother_ref, dmine_ref, sums_ref, got_ref, d_ref, small, large):
        d, got = norm_back_rows(sz, e_ref, s_ref, ar_ref, back_ref, g_ref)
        got_ref[...] = got
        put_tall(sz, d_ref, d)
        mean, inv = moments(art_ref, sz.counted)
        swapped = core_ref[0] == 1
        found = []
        ends = ((dother_ref, other_ref, True), (dmine_ref, mine_ref, False))
        for (out_ref, t_ref, away), total in zip(ends, conv_back_halves(sz, core_ref, d, k_ref, small, large)):
            def part(v):
                first, second = v[:, :half], v[:, half:]
                if away:
                    first, second = second, first
                return jnp.where(swapped, second, first)

            xhat = (t_ref[...].astype(F32) - part(mean)) * part(inv)
            out_ref[...] = total.astype(out_ref.dtype)
            total = total * slope(part(gt_ref[...]) * xhat + part(ht_ref[...]))
            found.append(
                jnp.concatenate(
                    [jnp.sum(total * xhat, axis=0, keepdims=True), jnp.sum(total, axis=0, keepdims=True)], axis=0
                )
            )
        first = jnp.where(swapped, found[0], found[1])
        second = jnp.where(swapped, found[1], found[0])
        both = jnp.concatenate([first, second], axis=1)
        sums_ref[...] = jnp.broadcast_to(both[None], sums_ref.shape)

    outs = [
        struct((sz.rows, half), BF16),
        struct((sz.rows, half), F32),
        struct((copies_of_sums, 2, 2 * half), F32),
        struct((2, 384), F32),
        tall_struct(sz),
    ]
    return call(body, "middle_back", outs, maps(sz, 384), core, e, s, ar, back, gain, k,
                mine, other, ar_t, gain_t, shift_t, flops=18 * sz.rows * 2 * half * 288)


def input_back(sz, place, d, k):
    half = k.shape[0] * k.shape[2] // 2
    n = sz.rows // sz.frames

    def body(place_ref, d_ref, k_ref, other_ref, mine_ref, small, large, woven):
        rows = get_tall(sz, d_ref)
        core = place_ref[1]
        for h, total in zip((1 - core, core), conv_back_halves(sz, place_ref.at[pl.ds(1, 1)], rows, k_ref, small, large)):
            put_lanes(woven, total, h * (half // 128))
        for y in range(sz.frames // 2):
            other_ref[y] = frame_of(sz, woven, 2 * y + 1 - core).astype(BF16)
            mine_ref[y] = frame_of(sz, woven, 2 * y + core)

    outs = [struct((sz.frames // 2, n, 2 * half), BF16), struct((sz.frames // 2, n, 2 * half), F32)]
    return call(body, "input_back", outs, maps(sz, 384) + [lanes_of(sz, 2 * half)], place, d, k,
                flops=18 * sz.rows * 2 * half * 288)


def put_tiles(out_ref, at, v):
    nblk, _, p, _ = out_ref.shape
    v = v.astype(BF16)
    for n in range(v.shape[1] // 128):
        out_ref[:, at + n] = v[:, 128 * n : 128 * n + 128].reshape(nblk, p, 128)


def parity_rows(sz, v, odd):
    c, n = v.shape
    v = v.reshape(sz.nb // 2, 2, c // sz.nb, n)
    return jnp.where(odd, v[:, 1], v[:, 0]).reshape(c // 2, n)


def transposed(sz, place, x):
    c = x.shape[1]

    def body(place_ref, x_ref, keep_ref, send_ref):
        v = x_ref[...].astype(F32).T
        odd = place_ref[0] == 1
        put_wide(keep_ref, parity_rows(sz, v, odd))
        put_wide(send_ref, parity_rows(sz, v, jnp.logical_not(odd)))

    return call(body, "transposed", [wide_struct(sz, c)] * 2, [], place, x)


def temporal_kernel_grad(sz, place, dt, wide, nblk):
    c = dt.shape[1]

    def body(place_ref, dt_ref, wide_ref, keep_ref, send_ref):
        v = jnp.dot(dt_ref[...].T, wide_ref[...], preferred_element_type=F32)
        odd = place_ref[0] == 1
        put_tiles(keep_ref, 0, parity_rows(sz, v, odd))
        put_tiles(send_ref, 0, parity_rows(sz, v, jnp.logical_not(odd)))

    outs = [struct((nblk // 2, 7, c // nblk, 128), BF16)] * 2
    return call(body, "temporal_kernel_grad", outs, [], place, dt, wide, flops=2 * dt.size * wide.shape[1])


def kernel_grads(sz, lefts, ds, temporals):
    c = lefts[0].shape[0]
    nblk, _, p, _ = temporals[0].shape

    def body(la_ref, lb_ref, da_ref, db_ref, ta_ref, tb_ref, out_ref, sa, la, sb, lb):
        fill(sz, get_tall(sz, da_ref), sa, la)
        fill(sz, get_tall(sz, db_ref), sb, lb)

        def grad(make):
            return jnp.dot(la_ref[:, : sz.rows], make(sa, la), preferred_element_type=F32) + jnp.dot(
                lb_ref[:, : sz.rows], make(sb, lb), preferred_element_type=F32
            )

        for o in range(9):
            put_tiles(
                out_ref, 2 * o,
                grad(lambda s, l: window(sz, s, l, 2 - o // 3, 2 - o % 3, slice(0, 256)).astype(BF16)),
            )
        rest = grad(lambda s, l: rest_patches(sz, s, l))
        put_tiles(out_ref, REST, rest[:, :256])
        for n in range(7):
            v = ta_ref[:, n].astype(F32) + tb_ref[:, n].astype(F32)
            if n < 6:
                out_ref[:, 18 + n] = v.astype(BF16)
            else:
                put_tiles(out_ref, REST + 2, v.reshape(c, 128) + rest[:, 256:])

    outs = [struct((nblk, TILES, p, 128), BF16)]
    return call(body, "kernel_grads", outs, maps(sz, 384) + maps(sz, 384), *lefts, *ds, *temporals,
                flops=2 * 18 * sz.rows * c * 288)[0]


def body(
    input_small, input_large, spatial_one, temporal_one, spatial_two, temporal_two,
    mid_gain, mid_shift, out_gain, out_shift, cotangent_small, cotangent_large,
):
    clips = input_small.shape[0]
    frames = lax.axis_size("tm")
    nb = lax.axis_size("batch")
    hs, hl = input_small.shape[2], input_large.shape[2]
    places = hs * hs + hl * hl
    sz = Sizes(hs, hl, clips * frames, frames, nb, float(places * clips * frames * nb))
    t = lax.axis_index("tm")
    core = (t % 2).astype(jnp.int32).reshape(1)

    def to_rows(small, large):
        return jnp.concatenate(
            [v[:, 0].reshape(clips, -1, v.shape[-1]) for v in (small, large)], axis=1
        ).reshape(clips * places, -1)

    def from_rows(rows):
        v = rows.reshape(clips, places, -1)
        s = v[:, : sz.ns].reshape(clips, 1, hs, hs, -1)
        l = v[:, sz.ns :].reshape(clips, 1, hl, hl, -1)
        return s, l

    b = lax.axis_index("batch")
    place = jnp.stack([b % 2, t % 2, t]).astype(jnp.int32)
    parities = [[i for i in range(nb) if i % 2 == q] for q in range(2)]

    rows = to_rows(input_small, input_large)
    cot_rows = to_rows(cotangent_small, cotangent_large)

    def beside(far_rows):
        two = spread_tm(pack(spatial_two, temporal_two))
        acts, two = after(jnp.stack([rows, cot_rows, far_rows]), two)
        return two, acts, swap(acts, "tm", 1), swap(acts, "tm", 2)

    packed, rows = after(pack(spatial_one, temporal_one), rows)
    pieces, at, (two, acts, other_core, got), free = fetch(packed, [swap(rows, "batch", 1)], beside)
    x, cot, xt, xt_far = weave(sz, place, (acts, other_core, got, swap(got, "tm", 1)))
    two = gather_batch(after(two, *free)[0])
    nblk = two.shape[0]

    gm, sm = channels(mid_gain, t), channels(mid_shift, t)
    small = [gm[0:1], gm[1:2], sm[0:1], sm[1:2], out_gain[0:1], out_gain[1:2], out_shift[0:1], out_shift[1:2]]
    gm0, gm1, sm0, sm1, go0, go1, so0, so1, core, place, x = after(*small, core, place, x)

    s1, sums, one = first_conv(sz, x, pieces, at)
    ar1 = shared(sums)
    a1, *parts = norm_temporal(sz, place, s1, ar1, gm0, sm0, one)
    t1m, t1o, ar2 = exchange(sz, place, *parts)
    b1, s2, sums = second_conv(sz, core, t1m, t1o, ar2, go0, so0, two)
    ar3 = shared(sums)
    a2, *parts = norm_temporal(sz, place, s2, ar3, gm1, sm1, two)

    def beside_t2(sent):
        bt, bt_send = transposed(sz, place, after(b1, sent)[0])
        return bt, swap(bt_send, "batch", 1)

    t2m, t2o, ar4, bt, bt_far = exchange(sz, place, *parts, beside_t2)
    dpre, sums = output_slope(sz, core, t2m, t2o, ar4, go1, so1, x, cot)
    back4 = shared(sums)
    dt2, e3, sums, n4 = temporal_back(
        sz, core, (dpre,), t2m, t2o, ar4, back4, go1, so1, s2, ar3, gm1, sm1, two
    )
    back3 = shared(sums)
    other, own, sums, n3, ds2 = middle_back(
        sz, core, e3, s2, ar3, back3, gm1, two, t1m, t1o, ar2, go0, so0, nb * frames
    )
    back2 = lax.all_to_all(sums, ("batch", "tm"), 0, 0, tiled=True)

    def beside_d1(sent):
        away, dt, d, _ = after(ds2, dt2, dpre, sent)
        away = swap(away, "batch", 1)
        tb_grad, tb_send = temporal_kernel_grad(sz, place, dt, a2, nblk)
        d, tb_send = after(d, tb_send)
        return (back2, away, tb_grad, tb_send, *own_output(sz, place, t2m, t2o, ar4, go1, so1, x, d))

    d1m, d1o, back2, ds2_far, tb_grad, tb_send, own_out, own_dpre = sum_tm(own, other, beside_d1)
    tb_far = swap(tb_send, "batch", 1)
    out_s, out_l = from_rows(own_out)
    dt1, e1, sums, n2 = temporal_back(
        sz, core, (d1m, d1o), t1m, t1o, ar2, back2, go0, so0, s1, ar1, gm0, sm0, one
    )
    ta_grad, ta_send = temporal_kernel_grad(sz, place, dt1, a1, nblk)
    ta_got = swap(ta_send, "batch", 1)
    dk_two = kernel_grads(sz, (bt, bt_far), (ds2, ds2_far), (tb_grad, tb_far))
    sum_two = lax.psum_scatter(
        owners(dk_two, nb // 2, frames), "batch", scatter_dimension=0, axis_index_groups=parities
    )
    sums, ta_grad, _ = after(sums, ta_grad, dk_two)
    back1 = shared(sums)
    back1, ta_got = after(back1, ta_got)
    ds1, n1 = norm_back(sz, e1, s1, ar1, back1, gm0)
    ds1_got = swap(ds1, "batch", 1)
    other, own = input_back(sz, place, ds1, one)
    ds1_got, ta_got, other, own = after(ds1_got, ta_got, other, own)
    dk_one = kernel_grads(sz, (xt, xt_far), (ds1, ds1_got), (ta_grad, ta_got))
    moved = lax.all_to_all(
        owners(dk_one, nb // 2, frames).reshape((nb // 2 * frames, dk_one.shape[1], -1, 128)),
        ("batch", "tm"), 0, 0, tiled=True,
        axis_index_groups=[[i * frames + j for i in g for j in range(frames)] for g in parities],
    )
    sum_two, own, _ = after(sum_two, own, dk_one)
    grad_s, grad_l = from_rows(own_dpre + scatter_tm(own, other))
    grad_sb, grad_tb = unpack(spread_tm(sum_two)[None])

    n13 = jnp.stack([n1, n3], axis=1)
    n13 = pair(n13, swap(n13, "tm", 2), t // 2)
    n13 = jnp.swapaxes(pair(n13, swap(n13, "tm", 1), t % 2), 0, 1).reshape((frames, 4, 384))
    moved, grad_sb, grad_tb, n13 = after(moved, grad_sb, grad_tb, n13)
    grad_sa, grad_ta = unpack(moved.reshape((nb // 2, frames) + moved.shape[1:]))
    mids = all_channels(n13).reshape(2, 2, -1)
    return (
        out_s, out_l, grad_s, grad_l, grad_sa, grad_ta, grad_sb, grad_tb,
        mids[0], mids[1], jnp.stack([n2[0], n4[0]]), jnp.stack([n2[1], n4[1]]),
    )


def solution(mesh):
    act = P("batch", "tm", None, None, None)
    rows = P(None, ("batch", "tm"), None)
    cols = P(None, None, ("batch", "tm"))
    return jax.shard_map(
        body,
        mesh=mesh,
        in_specs=(act, act, rows, cols, rows, cols, P(), P(), P(), P(), act, act),
        out_specs=(act, act, act, act, rows, cols, rows, cols, P(), P(), P(), P()),
        check_vma=False,
    )
```

```python
import math

import jax
import jax.numpy as jnp
from jax import lax
from jax.experimental import pallas as pl
from jax.experimental.pallas import tpu as pltpu
from jax.sharding import PartitionSpec as P

EPS = 1e-05
F32 = jnp.float32
BF16 = jnp.bfloat16
VMEM_LIMIT = 30 * 1024 * 1024


def swap(value, axis, bit):
    n = lax.axis_size(axis)
    return lax.ppermute(value, axis, [(i, i ^ bit) for i in range(n)])


def shared(copies):
    return lax.all_to_all(copies, "batch", 0, 0, tiled=True)


def tm_bits():
    t = lax.axis_index("tm")
    return t % 2, t // 2


def pair(first, second, bit):
    return jnp.where(bit == 0, jnp.stack([first, second]), jnp.stack([second, first]))


def after(value, *others):
    return lax.optimization_barrier((value,) + others)


def sum_tm(mine, other, beside=None):
    mine = (mine.astype(F32) + swap(other, "tm", 1).astype(F32)).astype(BF16)
    got, *there = after(swap(mine, "tm", 2), *(beside(mine) if beside else ()))
    mine = (mine.astype(F32) + got.astype(F32)).astype(BF16)
    return (mine, swap(mine, "tm", 1), *there)


def scatter_tm(mine, other):
    _, y = tm_bits()
    mine = mine + swap(other, "tm", 1).astype(F32)
    own = lax.dynamic_index_in_dim(mine, y, 0, keepdims=False)
    away = lax.dynamic_index_in_dim(mine, 1 - y, 0, keepdims=False)
    return own + swap(away.astype(BF16), "tm", 2).astype(F32)


TILES = 27
REST = 24


def tiled(x):
    k, p, _ = x.shape
    q = -(-k // 4)
    main = x[:, :, :1024].reshape(k, p, 4, 2, 128)
    main = jnp.transpose(main, (2, 0, 3, 1, 4)).reshape(4, 2 * k, p, 128)
    rest = jnp.pad(x[:, :, 1024:], ((0, 4 * q - k), (0, 0), (0, 0))).reshape(q, 4, p, 4, 32)
    rest = jnp.transpose(rest, (3, 0, 2, 1, 4)).reshape(4, q, p, 128)
    return jnp.concatenate([main, rest], axis=1)


def untiled(y):
    k, p = 12, y.shape[2]
    q = -(-k // 4)
    main = jnp.transpose(y[:, : 2 * k].reshape(4, k, 2, p, 128), (1, 3, 0, 2, 4)).reshape(k, p, 1024)
    rest = y[:, 2 * k :].reshape(4, q, p, 4, 32)
    rest = jnp.transpose(rest, (1, 3, 2, 0, 4)).reshape(4 * q, p, 128)[:k]
    return jnp.concatenate([main, rest], axis=2)


def pack(spatial, temporal):
    temporal = jnp.swapaxes(temporal, 1, 2)
    p = spatial.shape[1]
    if p % 16:
        return tiled(jnp.concatenate([spatial, temporal]))

    def body(s_ref, t_ref, out_ref):
        rows = [s_ref[o].astype(F32) for o in range(9)] + [t_ref[o].astype(F32) for o in range(3)]
        group = lax.broadcasted_iota(jnp.int32, (p, 128), 1) // 32
        for t in range(4):
            for o in range(12):
                for h in range(2):
                    lane = 256 * t + 128 * h
                    out_ref[t, 2 * o + h] = rows[o][:, lane : lane + 128].astype(BF16)
            for q in range(3):
                tile = jnp.zeros((p, 128), F32)
                for r in range(4):
                    moved = pltpu.roll(rows[4 * q + r][:, 1024:], (32 * (r - t)) % 128, 1)
                    tile = jnp.where(group == r, moved, tile)
                out_ref[t, REST + q] = tile.astype(BF16)

    return call(body, "pack", [struct((4, TILES, p, 128), BF16)], [], spatial, temporal)[0]


def turned_tm(packed):
    t = lax.axis_index("tm")
    got = []
    for s in range(4):
        piece = lax.dynamic_index_in_dim(packed, t ^ s, 0, keepdims=False)
        got.append(swap(piece, "tm", s) if s else piece)
    return jnp.stack(got)


def spread_tm(packed):
    t = lax.axis_index("tm")
    got = turned_tm(packed)
    return jnp.stack([lax.dynamic_index_in_dim(got, t ^ s, 0, keepdims=False) for s in range(4)])


def blocks(whole):
    nb, nt, tiles, p, _ = whole.shape
    if p % 16 == 0:
        return whole.reshape(nb * nt, tiles, p, 128)
    v = jnp.moveaxis(whole.reshape(2, nb * nt // 2, tiles, p, 128), 2, 1)
    return v.reshape(2, tiles, nb * nt // 2 * p, 128)


def gather_batch(moved):
    return blocks(lax.all_gather(moved, "batch", axis=0))


def fetch(packed, ahead, beside):
    nb = lax.axis_size("batch")
    if nb != 8 or packed.shape[2] % 16:
        return [gather_batch(spread_tm(packed))], jnp.zeros((1,), jnp.int32), beside(*ahead), []
    b, t = lax.axis_index("batch"), lax.axis_index("tm")
    z, x = b // 2, b % 2

    def turn(u, by):
        return lax.ppermute(u, "batch", [(i, (i + by) % 8) for i in range(8)])

    v = turned_tm(packed)
    below, far, *ahead = after(turn(v, 2), swap(v, "batch", 1), *ahead)
    v, *ahead = after(v, below, *ahead)
    there = beside(*ahead[1:])
    above, far_below = after(turn(v, -2), swap(below, "batch", 1))
    opposite = [turn(after(below[:2], above)[0], 2), turn(above[2:], -2)]
    far_above = swap(above, "batch", 1)
    far_above, *there = after(far_above, *opposite, *there)
    opposite, there = there[:2], there[2:]
    far_opposite = [swap(o, "batch", 1) for o in opposite]
    pieces = [v, below, above] + opposite + [far, far_below, far_above] + far_opposite
    zs = [z, z - 1, z + 1, z + 2, z + 2]
    rows = [range(4), range(4), range(4), range(2), range(2, 4)]
    at = [4 * (2 * (w % 4) + x) + (t ^ r) for w, rs in zip(zs, rows) for r in rs]
    at += [4 * (2 * (w % 4) + 1 - x) + (t ^ r) for w, rs in zip(zs, rows) for r in rs]
    return pieces, jnp.stack(at).astype(jnp.int32), there, [far_above]


def owners(grads, nb, nt):
    nblk, tiles, p, _ = grads.shape
    if nblk == nb * nt:
        return grads.reshape(nb, nt, tiles, p, 128)
    own = nblk * p // (nb * nt)
    v = grads.reshape(nblk, tiles, nb * nt // nblk, own, 128)
    return jnp.moveaxis(v, 2, 1).reshape(nb, nt, tiles, own, 128)


def unpack(parts):
    n, _, total, p, _ = parts.shape
    if p % 16:
        summed = untiled(jnp.sum(parts.astype(F32), axis=0))
        return summed[:9], jnp.swapaxes(summed[9:], 1, 2)

    def body(in_ref, s_ref, t_ref):
        group = lax.broadcasted_iota(jnp.int32, (p, 128), 1) // 32

        def tile(t, i):
            v = in_ref[0, t, i].astype(F32)
            for m in range(1, n):
                v = v + in_ref[m, t, i].astype(F32)
            return v

        rest = [[tile(t, REST + q) for t in range(4)] for q in range(3)]
        for o in range(12):
            pieces = [tile(t, 2 * o + h) for t in range(4) for h in range(2)]
            last = jnp.zeros((p, 128), F32)
            for t in range(4):
                moved = pltpu.roll(rest[o // 4][t], (32 * (t - o % 4)) % 128, 1)
                last = jnp.where(group == t, moved, last)
            whole = jnp.concatenate(pieces + [last], axis=1)
            if o < 9:
                s_ref[o] = whole
            else:
                t_ref[o - 9] = whole

    spatial, temporal = call(body, "unpack", [struct((k, p, 1152), F32) for k in (9, 3)], [], parts)
    return spatial, jnp.swapaxes(temporal, 1, 2)


def channels(v, t):
    main = lax.dynamic_slice_in_dim(v, 256 * t, 256, v.ndim - 1)
    rest = lax.dynamic_slice_in_dim(v, 1024 + 32 * t, 32, v.ndim - 1)
    return jnp.concatenate([main] + [rest] * 4, axis=-1)


def all_channels(v):
    main = jnp.moveaxis(v[..., :256], 0, -2)
    rest = jnp.moveaxis(v[..., 256:288], 0, -2)
    lead = main.shape[:-2]
    return jnp.concatenate([main.reshape(lead + (-1,)), rest.reshape(lead + (-1,))], axis=-1)


class Sizes:
    def __init__(self, hs, hl, group, frames, nb, counted):
        self.hs, self.hl, self.group, self.frames, self.nb = hs, hl, group, frames, nb
        self.ns, self.nl = hs * hs, hl * hl
        self.cut = self.ns * group
        self.rows = (self.ns + self.nl) * group
        self.counted = counted


def call(body, name, outs, scratch, *args, flops=0, anywhere=(), out_anywhere=()):
    smem = pl.BlockSpec(memory_space=pltpu.SMEM)
    vmem = pl.BlockSpec(memory_space=pltpu.VMEM)
    hbm = pl.BlockSpec(memory_space=pl.ANY)
    moved = sum(math.prod(a.shape) * a.dtype.itemsize for a in (*args, *outs))
    return pl.pallas_call(
        body,
        out_shape=outs,
        in_specs=[
            smem if a.dtype == jnp.int32 else hbm if n in anywhere else vmem for n, a in enumerate(args)
        ],
        out_specs=[hbm if n in out_anywhere else vmem for n in range(len(outs))],
        scratch_shapes=scratch,
        name=name,
        compiler_params=pltpu.CompilerParams(vmem_limit_bytes=VMEM_LIMIT),
        cost_estimate=pl.CostEstimate(flops=flops, bytes_accessed=moved, transcendentals=0),
    )(*args)


def struct(shape, dtype):
    return jax.ShapeDtypeStruct(shape, dtype)


def moments(ar_ref, counted):
    s = jnp.sum(ar_ref[...], axis=0)
    mean = s[0:1] / counted
    return mean, lax.rsqrt(s[1:2] / counted - mean * mean + EPS)


def put_sums(out_ref, first, second):
    both = jnp.concatenate(
        [jnp.sum(first, axis=0, keepdims=True), jnp.sum(second, axis=0, keepdims=True)], axis=0
    )
    out_ref[...] = jnp.broadcast_to(both[None], out_ref.shape)


def sigmoid(v):
    return 1.0 / (1.0 + jnp.exp(-v))


def slope(v):
    sig = sigmoid(v)
    return sig * (1.0 + v * (1.0 - sig))


def ordered(core_ref, mine_ref, other_ref):
    first = core_ref[0] == 0
    mine, other = mine_ref[...].astype(F32), other_ref[...].astype(F32)
    return jnp.concatenate([jnp.where(first, mine, other), jnp.where(first, other, mine)], axis=1)


def fill(sz, rows, small_ref, large_ref):
    c = rows.shape[1]
    for ref, h, v in (
        (small_ref, sz.hs, rows[: sz.cut]),
        (large_ref, sz.hl, rows[sz.cut :]),
    ):
        ref[...] = jnp.zeros(ref.shape, F32)
        ref[1 : h + 1, 1 : h + 1] = v.reshape(h, h, sz.group, c)


def window(sz, small_ref, large_ref, i, j, lanes):
    c = lanes.stop - lanes.start
    s = small_ref[i : i + sz.hs, j : j + sz.hs, :, lanes].reshape(sz.cut, c)
    l = large_ref[i : i + sz.hl, j : j + sz.hl, :, lanes].reshape(sz.rows - sz.cut, c)
    return jnp.concatenate([s, l], axis=0)


def tile(k_ref, n, half=None):
    nblk, _, p, lanes = k_ref.shape
    if half is None:
        return k_ref[:, n].reshape(nblk * p, lanes)
    return k_ref[pl.ds(half * (nblk // 2), nblk // 2), n].reshape(nblk // 2 * p, lanes)


def tiles(k_ref, ns, half=None):
    return jnp.concatenate([tile(k_ref, n, half) for n in ns], axis=1)


def lane_group(v):
    return lax.broadcasted_iota(jnp.int32, (1, v.shape[1]), 1) // 32


def folded(v):
    v = v + pltpu.roll(v, 32, 1)
    return v + pltpu.roll(v, 64, 1)


def picked(first, rest):
    out = first
    for r, v in enumerate(rest):
        out = jnp.where(lane_group(first) == r + 1, v, out)
    return out


def conv_rows(sz, xb, small, large, ysmall, ylarge, k_ref):
    c = xb.shape[1]
    every = slice(0, c)
    main = None
    for i in range(3):
        left = jnp.concatenate(
            [window(sz, small, large, i, j, every).astype(BF16) for j in range(3)], axis=1
        )
        right = jnp.concatenate(
            [tiles(k_ref, (6 * i + 2 * j, 6 * i + 2 * j + 1)) for j in range(3)], axis=0
        )
        d = jnp.dot(left, right, preferred_element_type=F32)
        main = d if main is None else main + d
    y = jnp.dot(xb, tiles(k_ref, range(REST, REST + 3)), preferred_element_type=F32)
    fill(sz, y, ysmall, ylarge)
    rest = window(sz, ysmall, ylarge, 2, 2, slice(256, 384))
    rest = jnp.where(lane_group(rest) == 0, rest, 0.0)
    for q in range(2):
        at = [window(sz, ysmall, ylarge, (4 * q + r) // 3, (4 * q + r) % 3, slice(128 * q, 128 * q + 128)) for r in range(4)]
        rest = rest + picked(at[0], at[1:])
    return jnp.concatenate([main, folded(rest)], axis=1)


def maps(sz, c):
    def one(h):
        return pltpu.VMEM((h + 2, h + 2, sz.group, c), F32)

    return [one(sz.hs), one(sz.hl)]


def wide_struct(sz, c):
    return struct((c // 2, -(-sz.rows // 128) * 128), BF16)


def put_wide(out_ref, v):
    pad = jnp.zeros((v.shape[0], out_ref.shape[1] - v.shape[1]), F32)
    out_ref[...] = jnp.concatenate([v, pad], axis=1).astype(BF16)


def lanes_of(sz, c):
    return pltpu.VMEM((c // 128, sz.rows, 128), F32)


def put_lanes(woven, v, at=0):
    for n in range(v.shape[1] // 128):
        woven[at + n] = v[:, 128 * n : 128 * n + 128]


def weave(sz, place, frames_of):
    _, n, c = frames_of[0].shape
    places = sz.rows // sz.group
    clips = sz.group // sz.frames

    def body(place_ref, *refs):
        srcs, (rows_ref, cot_rows_ref, xt_ref, ft_ref, woven) = refs[:4], refs[4:]
        for a, dst, turned in ((1, cot_rows_ref, None), (0, rows_ref, xt_ref), (2, None, ft_ref)):
            for s, src in enumerate(srcs):
                v = src[a].astype(F32)
                f = place_ref[2] ^ s
                for m in range(clips):
                    rows = v[places * m : places * m + places]
                    for n in range(c // 128):
                        woven[n, pl.ds(sz.frames * m + f, places, stride=sz.group)] = rows[:, 128 * n : 128 * n + 128]
            if dst is not None:
                for n in range(c // 128):
                    dst[:, 128 * n : 128 * n + 128] = woven[n].astype(BF16)
            if turned is not None:
                v = jnp.concatenate([woven[n] for n in range(c // 128)], axis=1).T
                put_wide(turned, parity_rows(sz, v, place_ref[0] == 1))

    outs = [struct((sz.rows, c), BF16)] * 2 + [wide_struct(sz, c)] * 2
    return call(body, "weave", outs, [lanes_of(sz, c)], place, *frames_of)


def frame_of(sz, woven, frame):
    places = sz.rows // sz.group
    out = []
    for m in range(sz.group // sz.frames):
        at = pl.ds(sz.frames * m + frame, places, stride=sz.group)
        out.append(jnp.concatenate([woven[n, at] for n in range(woven.shape[0])], axis=1))
    return jnp.concatenate(out, axis=0)


def first_conv(sz, x, pieces, at):
    c = x.shape[1]
    n = len(pieces)
    nblk = sum(v.shape[0] for v in pieces)
    _, _, p, lanes = pieces[0].shape
    whole = n == 1

    def body(x_ref, at_ref, *refs):
        parts, (s_ref, sums_ref, out_ref) = refs[:n], refs[n : n + 3]
        small, large, ysmall, ylarge, k_ref, sems = refs[n + 3 :]
        if whole:
            copies = [pltpu.make_async_copy(parts[0], k_ref, sems.at[0])]
        else:
            copies = []
            for v in parts:
                for r in range(v.shape[0]):
                    m = len(copies)
                    copies.append(pltpu.make_async_copy(v.at[r], k_ref.at[at_ref[m]], sems.at[m]))
        for copy in copies:
            copy.start()
        fill(sz, x_ref[...].astype(F32), small, large)
        for copy in copies:
            copy.wait()
        back = pltpu.make_async_copy(k_ref, out_ref, sems.at[nblk])
        back.start()
        total = conv_rows(sz, x_ref[...], small, large, ysmall, ylarge, k_ref)
        s_ref[...] = total
        put_sums(sums_ref, total, total * total)
        back.wait()

    k = struct((nblk, TILES, p, lanes), BF16)
    outs = [struct((sz.rows, 384), F32), struct((sz.nb, 2, 384), F32), k]
    scratch = [pltpu.VMEM(k.shape, BF16), pltpu.SemaphoreType.DMA((nblk + 1,))]
    return call(body, "conv_one", outs, maps(sz, c) + maps(sz, 384) + scratch, x, at, *pieces,
                flops=18 * sz.rows * c * 288, anywhere=range(2, 2 + n), out_anywhere=(2,))


def second_conv(sz, core, mine, other, ar, gain, shift, k):
    c = gain.shape[1]

    def body(core_ref, mine_ref, other_ref, ar_ref, g_ref, h_ref, k_ref, b_ref, s_ref, sums_ref,
             small, large, ysmall, ylarge):
        mean, inv = moments(ar_ref, sz.counted)
        p = g_ref[...] * ((ordered(core_ref, mine_ref, other_ref) - mean) * inv) + h_ref[...]
        b = (p * sigmoid(p)).astype(BF16)
        b_ref[...] = b
        fill(sz, b.astype(F32), small, large)
        total = conv_rows(sz, b, small, large, ysmall, ylarge, k_ref)
        s_ref[...] = total
        put_sums(sums_ref, total, total * total)

    outs = [struct((sz.rows, c), BF16), struct((sz.rows, 384), F32), struct((sz.nb, 2, 384), F32)]
    return call(body, "conv_two", outs, maps(sz, c) + maps(sz, 384),
                core, mine, other, ar, gain, shift, k, flops=18 * sz.rows * c * 288)


def frame_shift(sz, v, by):
    if by == 0:
        return v
    c = v.shape[1]
    v = v.reshape(-1, sz.group, c)
    frame = lax.broadcasted_iota(jnp.int32, (1, sz.group, c), 1) % sz.frames
    moved = pltpu.roll(v, (-by) % sz.group, 1)
    inside = (frame + by >= 0) & (frame + by < sz.frames)
    return jnp.where(inside, moved, 0.0).reshape(-1, c)


def norm_temporal(sz, place, s, ar, gain, shift, k):
    half = k.shape[0] * k.shape[2] // 2
    part = half // 2

    def body(place_ref, s_ref, ar_ref, g_ref, h_ref, k_ref, wide_ref, o1_ref, o0_ref, m1_ref, m0_ref):
        core, low = place_ref[1], place_ref[2] < 2
        mean, inv = moments(ar_ref, sz.counted)
        p = g_ref[...] * ((s_ref[...] - mean) * inv) + h_ref[...]
        a = (p * sigmoid(p)).astype(BF16).astype(F32)
        moved = [frame_shift(sz, a, by) for by in (-1, 0, 1)]
        rest = picked(jnp.zeros_like(a[:, 256:]), [m[:, 256:] for m in moved])
        wide = jnp.concatenate([m[:, :256] for m in moved] + [rest], axis=1).astype(BF16)
        wide_ref[...] = wide
        for away_ref, keep_ref, h in ((o1_ref, o0_ref, 1 - core), (m1_ref, m0_ref, core)):
            right = tiles(k_ref, (*range(18, 24), REST + 2), h)
            t = lax.dot_general(wide, right, (((1,), (1,)), ((), ())), preferred_element_type=F32)
            away_ref[...] = jnp.where(low, t[:, part:], t[:, :part]).astype(away_ref.dtype)
            keep_ref[...] = jnp.where(low, t[:, :part], t[:, part:]).astype(keep_ref.dtype)

    outs = [struct((sz.rows, 896), BF16)] + [struct((sz.rows, part), d) for d in (BF16, BF16, F32, F32)]
    return call(body, "norm_temporal", outs, [], place, s, ar, gain, shift, k,
                flops=6 * sz.rows * 2 * half * 288)


def quarter_sums(sz, mine, got_core, got_y):
    def body(mine_ref, core_ref, y_ref, q_ref, sums_ref):
        v = (mine_ref[...] + core_ref[...].astype(F32)).astype(BF16).astype(F32) + y_ref[...].astype(F32)
        v = v.astype(BF16)
        q_ref[...] = v
        v = v.astype(F32)
        put_sums(sums_ref, v, v * v)

    part = mine.shape[1]
    outs = [struct((sz.rows, part), BF16), struct((2 * sz.nb, 2, part), F32)]
    return call(body, "quarter_sums", outs, [], mine, got_core, got_y)


def joined(sz, place, quarters, ars):
    part = quarters[0].shape[1]

    def body(place_ref, q0_ref, q1_ref, c0_ref, c1_ref, ma_ref, ca_ref, mine_ref, other_ref, sums_ref):
        first, low = place_ref[1] == 0, place_ref[2] < 2
        for own, away, out_ref in ((q0_ref, q1_ref, mine_ref), (c0_ref, c1_ref, other_ref)):
            a, b = own[...].astype(F32), away[...].astype(F32)
            v = jnp.concatenate([jnp.where(low, a, b), jnp.where(low, b, a)], axis=1)
            out_ref[...] = v.astype(BF16)

        def total(ref):
            return jnp.concatenate(
                [sum(ref[2 * m + y] for m in range(1, sz.nb)) + ref[y] for y in range(2)], axis=1
            )

        m, o = total(ma_ref), total(ca_ref)
        sums_ref[0] = jnp.concatenate([jnp.where(first, m, o), jnp.where(first, o, m)], axis=1)

    outs = [struct((sz.rows, 2 * part), BF16)] * 2 + [struct((1, 2, 4 * part), F32)]
    return call(body, "joined", outs, [], place, *quarters, *ars)


def exchange(sz, place, o1, o0, m1, m0, beside=None):
    nt = lax.axis_size("tm")
    got1, got0 = swap(o1, "tm", 1), swap(o0, "tm", 1)
    sent = (m1 + got1.astype(F32)).astype(BF16)
    there = beside(sent) if beside else ()
    q, sums = quarter_sums(sz, m0, got0, swap(sent, "tm", 2))
    groups = [[nt * b + 2 * y + c for b in range(sz.nb) for y in range(nt // 2)] for c in range(2)]
    ar = lax.all_to_all(sums, ("batch", "tm"), 0, 0, tiled=True, axis_index_groups=groups)
    back = swap(q, "tm", 2)
    own_core = swap(q, "tm", 1)
    back, ar, own_core, *there = after(back, ar, own_core, *there)
    quarters = (q, back, own_core, swap(back, "tm", 1))
    return (*joined(sz, place, quarters, (ar, swap(ar, "tm", 1))), *there)


def output_slope(sz, core, mine, other, ar, gain, shift, x, cot):
    c = x.shape[1]

    def body(core_ref, mine_ref, other_ref, ar_ref, g_ref, h_ref, x_ref, cot_ref, d_ref, sums_ref):
        mean, inv = moments(ar_ref, sz.counted)
        xhat = (ordered(core_ref, mine_ref, other_ref) - mean) * inv
        pre = x_ref[...].astype(F32) + (g_ref[...] * xhat + h_ref[...])
        d = cot_ref[...].astype(F32) * slope(pre)
        d_ref[...] = d
        put_sums(sums_ref, d * xhat, d)

    outs = [struct((sz.rows, c), F32), struct((sz.nb, 2, c), F32)]
    return call(body, "output_slope", outs, [], core, mine, other, ar, gain, shift, x, cot)


def own_output(sz, place, mine, other, ar, gain, shift, x, d):
    c = x.shape[1]
    n = sz.rows // sz.frames

    def body(place_ref, mine_ref, other_ref, ar_ref, g_ref, h_ref, x_ref, d_ref, out_ref, own_ref, woven):
        put_lanes(woven, d_ref[...])
        own_ref[...] = frame_of(sz, woven, place_ref[2])
        mean, inv = moments(ar_ref, sz.counted)
        xhat = (ordered(place_ref.at[pl.ds(1, 1)], mine_ref, other_ref) - mean) * inv
        pre = x_ref[...].astype(F32) + (g_ref[...] * xhat + h_ref[...])
        put_lanes(woven, pre * sigmoid(pre))
        out_ref[...] = frame_of(sz, woven, place_ref[2]).astype(BF16)

    outs = [struct((n, c), BF16), struct((n, c), F32)]
    return call(body, "own_output", outs, [lanes_of(sz, c)], place, mine, other, ar, gain, shift, x, d)


def temporal_back(sz, core, e, mine, other, ar, back, gain, shift, s, ar_s, gain_s, shift_s, k):
    c = gain.shape[1]
    given = len(e)

    def body(core_ref, *refs):
        e_refs, refs = refs[:given], refs[given:]
        (mine_ref, other_ref, ar_ref, back_ref, g_ref, h_ref, s_ref, ars_ref, gs_ref, hs_ref, k_ref,
         dt_ref, es_ref, sums_ref, got_ref) = refs
        mean, inv = moments(ar_ref, sz.counted)
        got = jnp.sum(back_ref[...], axis=0)
        got_ref[...] = got
        xhat = (ordered(core_ref, mine_ref, other_ref) - mean) * inv
        if given == 1:
            up = e_refs[0][...]
        else:
            up = ordered(core_ref, *e_refs) * slope(g_ref[...] * xhat + h_ref[...])
        d = g_ref[...] * inv * (up - (got[1:2] + xhat * got[0:1]) / sz.counted)
        d = d.astype(BF16)
        dt_ref[...] = d
        d = d.astype(F32)
        left = jnp.concatenate([frame_shift(sz, d, by).astype(BF16) for by in (1, 0, -1)], axis=1)
        right = jnp.concatenate([tiles(k_ref, (18 + 2 * n, 19 + 2 * n)) for n in range(3)], axis=0)
        main = jnp.dot(left, right, preferred_element_type=F32)
        y = jnp.dot(dt_ref[...], tile(k_ref, REST + 2), preferred_element_type=F32)
        rest = picked(jnp.zeros_like(y), [frame_shift(sz, y, by) for by in (1, 0, -1)])
        da = jnp.concatenate([main, folded(rest)], axis=1).astype(BF16).astype(F32)
        mean_s, inv_s = moments(ars_ref, sz.counted)
        xhat_s = (s_ref[...] - mean_s) * inv_s
        es = da * slope(gs_ref[...] * xhat_s + hs_ref[...])
        es_ref[...] = es
        put_sums(sums_ref, es * xhat_s, es)

    outs = [
        struct((sz.rows, c), BF16),
        struct((sz.rows, 384), F32),
        struct((sz.nb, 2, 384), F32),
        struct((2, c), F32),
    ]
    return call(body, "temporal_back", outs, [], core, *e, mine, other, ar, back, gain, shift,
                s, ar_s, gain_s, shift_s, k, flops=6 * sz.rows * c * 288)


def norm_back_rows(sz, e_ref, s_ref, ar_ref, back_ref, g_ref):
    mean, inv = moments(ar_ref, sz.counted)
    got = jnp.sum(back_ref[...], axis=0)
    xhat = (s_ref[...] - mean) * inv
    d = g_ref[...] * inv * (e_ref[...] - (got[1:2] + xhat * got[0:1]) / sz.counted)
    return d.astype(BF16).astype(F32), got


def rest_patches(sz, small, large):
    lanes = slice(256, 384)
    out = []
    for q in range(3):
        at = [window(sz, small, large, 2 - o // 3, 2 - o % 3, lanes) for o in range(4 * q, min(4 * q + 4, 9))]
        at += [jnp.zeros_like(at[0])] * (4 - len(at))
        out.append(picked(at[0], at[1:]).astype(BF16))
    return jnp.concatenate(out, axis=1)


def tall(sz):
    full = -(-sz.rows // 16) * 16
    quarter = -(-sz.rows // 64) * 16
    return full, quarter


def put_tall(sz, out_ref, d):
    full, quarter = tall(sz)
    pad = jnp.zeros((4 * quarter - sz.rows, 128), F32)
    for n in range(2):
        v = jnp.concatenate([d[:, 128 * n : 128 * n + 128], pad[: full - sz.rows]], axis=0)
        out_ref[n * full : n * full + full] = v.astype(BF16)
    rest = jnp.concatenate([d[:, 256:], pad], axis=0)
    at = [rest[quarter * g : quarter * g + quarter] for g in range(4)]
    out_ref[2 * full :] = picked(at[0], at[1:]).astype(BF16)


def get_tall(sz, ref):
    full, quarter = tall(sz)
    main = [ref[n * full : n * full + full].astype(F32)[: sz.rows] for n in range(2)]
    packed = ref[2 * full :].astype(F32)
    rest = [folded(jnp.where(lane_group(packed) == g, packed, 0.0)) for g in range(4)]
    rest = jnp.concatenate(rest, axis=0)[: sz.rows]
    return jnp.concatenate(main + [rest], axis=1)


def tall_struct(sz):
    full, quarter = tall(sz)
    return struct((2 * full + quarter, 128), BF16)


def norm_back(sz, e, s, ar, back, gain):
    def body(e_ref, s_ref, ar_ref, back_ref, g_ref, d_ref, got_ref):
        d, got = norm_back_rows(sz, e_ref, s_ref, ar_ref, back_ref, g_ref)
        got_ref[...] = got
        put_tall(sz, d_ref, d)

    outs = [tall_struct(sz), struct((2, 384), F32)]
    return call(body, "norm_back", outs, [], e, s, ar, back, gain)


def conv_back_halves(sz, core_ref, d, k_ref, small, large):
    fill(sz, d, small, large)
    rest = rest_patches(sz, small, large)
    for h in (1 - core_ref[0], core_ref[0]):
        total = None
        for i in range(3):
            left = jnp.concatenate(
                [window(sz, small, large, 2 - i, 2 - j, slice(0, 256)).astype(BF16) for j in range(3)],
                axis=1,
            )
            right = tiles(k_ref, range(6 * i, 6 * i + 6), h)
            if i == 2:
                left = jnp.concatenate([left, rest], axis=1)
                right = jnp.concatenate([right, tiles(k_ref, range(REST, REST + 3), h)], axis=1)
            one = lax.dot_general(left, right, (((1,), (1,)), ((), ())), preferred_element_type=F32)
            total = one if total is None else total + one
        yield total


def middle_back(sz, core, e, s, ar, back, gain, k, mine, other, ar_t, gain_t, shift_t, copies_of_sums):
    half = k.shape[0] * k.shape[2] // 2

    def body(core_ref, e_ref, s_ref, ar_ref, back_ref, g_ref, k_ref, mine_ref, other_ref, art_ref, gt_ref, ht_ref,
             dother_ref, dmine_ref, sums_ref, got_ref, d_ref, small, large):
        d, got = norm_back_rows(sz, e_ref, s_ref, ar_ref, back_ref, g_ref)
        got_ref[...] = got
        put_tall(sz, d_ref, d)
        mean, inv = moments(art_ref, sz.counted)
        swapped = core_ref[0] == 1
        found = []
        ends = ((dother_ref, other_ref, True), (dmine_ref, mine_ref, False))
        for (out_ref, t_ref, away), total in zip(ends, conv_back_halves(sz, core_ref, d, k_ref, small, large)):
            def part(v):
                first, second = v[:, :half], v[:, half:]
                if away:
                    first, second = second, first
                return jnp.where(swapped, second, first)

            xhat = (t_ref[...].astype(F32) - part(mean)) * part(inv)
            out_ref[...] = total.astype(out_ref.dtype)
            total = total * slope(part(gt_ref[...]) * xhat + part(ht_ref[...]))
            found.append(
                jnp.concatenate(
                    [jnp.sum(total * xhat, axis=0, keepdims=True), jnp.sum(total, axis=0, keepdims=True)], axis=0
                )
            )
        first = jnp.where(swapped, found[0], found[1])
        second = jnp.where(swapped, found[1], found[0])
        both = jnp.concatenate([first, second], axis=1)
        sums_ref[...] = jnp.broadcast_to(both[None], sums_ref.shape)

    outs = [
        struct((sz.rows, half), BF16),
        struct((sz.rows, half), F32),
        struct((copies_of_sums, 2, 2 * half), F32),
        struct((2, 384), F32),
        tall_struct(sz),
    ]
    return call(body, "middle_back", outs, maps(sz, 384), core, e, s, ar, back, gain, k,
                mine, other, ar_t, gain_t, shift_t, flops=18 * sz.rows * 2 * half * 288)


def input_back(sz, place, d, k):
    half = k.shape[0] * k.shape[2] // 2
    n = sz.rows // sz.frames

    def body(place_ref, d_ref, k_ref, other_ref, mine_ref, small, large, woven):
        rows = get_tall(sz, d_ref)
        core = place_ref[1]
        for h, total in zip((1 - core, core), conv_back_halves(sz, place_ref.at[pl.ds(1, 1)], rows, k_ref, small, large)):
            put_lanes(woven, total, h * (half // 128))
        for y in range(sz.frames // 2):
            other_ref[y] = frame_of(sz, woven, 2 * y + 1 - core).astype(BF16)
            mine_ref[y] = frame_of(sz, woven, 2 * y + core)

    outs = [struct((sz.frames // 2, n, 2 * half), BF16), struct((sz.frames // 2, n, 2 * half), F32)]
    return call(body, "input_back", outs, maps(sz, 384) + [lanes_of(sz, 2 * half)], place, d, k,
                flops=18 * sz.rows * 2 * half * 288)


def put_tiles(out_ref, at, v):
    nblk, _, p, _ = out_ref.shape
    v = v.astype(BF16)
    for n in range(v.shape[1] // 128):
        out_ref[:, at + n] = v[:, 128 * n : 128 * n + 128].reshape(nblk, p, 128)


def parity_rows(sz, v, odd):
    c, n = v.shape
    v = v.reshape(sz.nb // 2, 2, c // sz.nb, n)
    return jnp.where(odd, v[:, 1], v[:, 0]).reshape(c // 2, n)


def transposed(sz, place, x):
    c = x.shape[1]

    def body(place_ref, x_ref, keep_ref, send_ref):
        v = x_ref[...].astype(F32).T
        odd = place_ref[0] == 1
        put_wide(keep_ref, parity_rows(sz, v, odd))
        put_wide(send_ref, parity_rows(sz, v, jnp.logical_not(odd)))

    return call(body, "transposed", [wide_struct(sz, c)] * 2, [], place, x)


def temporal_kernel_grad(sz, place, dt, wide, nblk):
    c = dt.shape[1]

    def body(place_ref, dt_ref, wide_ref, keep_ref, send_ref):
        v = jnp.dot(dt_ref[...].T, wide_ref[...], preferred_element_type=F32)
        odd = place_ref[0] == 1
        put_tiles(keep_ref, 0, parity_rows(sz, v, odd))
        put_tiles(send_ref, 0, parity_rows(sz, v, jnp.logical_not(odd)))

    outs = [struct((nblk // 2, 7, c // nblk, 128), BF16)] * 2
    return call(body, "temporal_kernel_grad", outs, [], place, dt, wide, flops=2 * dt.size * wide.shape[1])


def kernel_grads(sz, lefts, ds, temporals):
    c = lefts[0].shape[0]
    nblk, _, p, _ = temporals[0].shape

    def body(la_ref, lb_ref, da_ref, db_ref, ta_ref, tb_ref, out_ref, sa, la, sb, lb):
        fill(sz, get_tall(sz, da_ref), sa, la)
        fill(sz, get_tall(sz, db_ref), sb, lb)

        def grad(make):
            return jnp.dot(la_ref[:, : sz.rows], make(sa, la), preferred_element_type=F32) + jnp.dot(
                lb_ref[:, : sz.rows], make(sb, lb), preferred_element_type=F32
            )

        for o in range(9):
            put_tiles(
                out_ref, 2 * o,
                grad(lambda s, l: window(sz, s, l, 2 - o // 3, 2 - o % 3, slice(0, 256)).astype(BF16)),
            )
        rest = grad(lambda s, l: rest_patches(sz, s, l))
        put_tiles(out_ref, REST, rest[:, :256])
        for n in range(7):
            v = ta_ref[:, n].astype(F32) + tb_ref[:, n].astype(F32)
            if n < 6:
                out_ref[:, 18 + n] = v.astype(BF16)
            else:
                put_tiles(out_ref, REST + 2, v.reshape(c, 128) + rest[:, 256:])

    outs = [struct((nblk, TILES, p, 128), BF16)]
    return call(body, "kernel_grads", outs, maps(sz, 384) + maps(sz, 384), *lefts, *ds, *temporals,
                flops=2 * 18 * sz.rows * c * 288)[0]


def body(
    input_small, input_large, spatial_one, temporal_one, spatial_two, temporal_two,
    mid_gain, mid_shift, out_gain, out_shift, cotangent_small, cotangent_large,
):
    clips = input_small.shape[0]
    frames = lax.axis_size("tm")
    nb = lax.axis_size("batch")
    hs, hl = input_small.shape[2], input_large.shape[2]
    places = hs * hs + hl * hl
    sz = Sizes(hs, hl, clips * frames, frames, nb, float(places * clips * frames * nb))
    t = lax.axis_index("tm")
    core = (t % 2).astype(jnp.int32).reshape(1)

    def to_rows(small, large):
        return jnp.concatenate(
            [v[:, 0].reshape(clips, -1, v.shape[-1]) for v in (small, large)], axis=1
        ).reshape(clips * places, -1)

    def from_rows(rows):
        v = rows.reshape(clips, places, -1)
        s = v[:, : sz.ns].reshape(clips, 1, hs, hs, -1)
        l = v[:, sz.ns :].reshape(clips, 1, hl, hl, -1)
        return s, l

    b = lax.axis_index("batch")
    place = jnp.stack([b % 2, t % 2, t]).astype(jnp.int32)
    parities = [[i for i in range(nb) if i % 2 == q] for q in range(2)]

    rows = to_rows(input_small, input_large)
    cot_rows = to_rows(cotangent_small, cotangent_large)

    def beside(far_rows):
        two = spread_tm(pack(spatial_two, temporal_two))
        acts, two = after(jnp.stack([rows, cot_rows, far_rows]), two)
        return two, acts, swap(acts, "tm", 1), swap(acts, "tm", 2)

    packed, rows = after(pack(spatial_one, temporal_one), rows)
    pieces, at, (two, acts, other_core, got), free = fetch(packed, [swap(rows, "batch", 1)], beside)
    x, cot, xt, xt_far = weave(sz, place, (acts, other_core, got, swap(got, "tm", 1)))
    two = gather_batch(after(two, *free)[0])
    nblk = two.shape[0]

    gm, sm = channels(mid_gain, t), channels(mid_shift, t)
    small = [gm[0:1], gm[1:2], sm[0:1], sm[1:2], out_gain[0:1], out_gain[1:2], out_shift[0:1], out_shift[1:2]]
    gm0, gm1, sm0, sm1, go0, go1, so0, so1, core, place, x = after(*small, core, place, x)

    s1, sums, one = first_conv(sz, x, pieces, at)
    ar1 = shared(sums)
    a1, *parts = norm_temporal(sz, place, s1, ar1, gm0, sm0, one)
    t1m, t1o, ar2 = exchange(sz, place, *parts)
    b1, s2, sums = second_conv(sz, core, t1m, t1o, ar2, go0, so0, two)
    ar3 = shared(sums)
    a2, *parts = norm_temporal(sz, place, s2, ar3, gm1, sm1, two)

    def beside_t2(sent):
        bt, bt_send = transposed(sz, place, after(b1, sent)[0])
        return bt, swap(bt_send, "batch", 1)

    t2m, t2o, ar4, bt, bt_far = exchange(sz, place, *parts, beside_t2)
    dpre, sums = output_slope(sz, core, t2m, t2o, ar4, go1, so1, x, cot)
    back4 = shared(sums)
    dt2, e3, sums, n4 = temporal_back(
        sz, core, (dpre,), t2m, t2o, ar4, back4, go1, so1, s2, ar3, gm1, sm1, two
    )
    back3 = shared(sums)
    other, own, sums, n3, ds2 = middle_back(
        sz, core, e3, s2, ar3, back3, gm1, two, t1m, t1o, ar2, go0, so0, nb * frames
    )
    back2 = lax.all_to_all(sums, ("batch", "tm"), 0, 0, tiled=True)

    def beside_d1(sent):
        away, dt, d, _ = after(ds2, dt2, dpre, sent)
        away = swap(away, "batch", 1)
        tb_grad, tb_send = temporal_kernel_grad(sz, place, dt, a2, nblk)
        d, tb_send = after(d, tb_send)
        return (back2, away, tb_grad, tb_send, *own_output(sz, place, t2m, t2o, ar4, go1, so1, x, d))

    d1m, d1o, back2, ds2_far, tb_grad, tb_send, own_out, own_dpre = sum_tm(own, other, beside_d1)
    tb_far = swap(tb_send, "batch", 1)
    out_s, out_l = from_rows(own_out)
    dt1, e1, sums, n2 = temporal_back(
        sz, core, (d1m, d1o), t1m, t1o, ar2, back2, go0, so0, s1, ar1, gm0, sm0, one
    )
    ta_grad, ta_send = temporal_kernel_grad(sz, place, dt1, a1, nblk)
    ta_got = swap(ta_send, "batch", 1)
    dk_two = kernel_grads(sz, (bt, bt_far), (ds2, ds2_far), (tb_grad, tb_far))
    sum_two = lax.psum_scatter(
        owners(dk_two, nb // 2, frames), "batch", scatter_dimension=0, axis_index_groups=parities
    )
    sums, ta_grad, _ = after(sums, ta_grad, dk_two)
    back1 = shared(sums)
    back1, ta_got = after(back1, ta_got)
    ds1, n1 = norm_back(sz, e1, s1, ar1, back1, gm0)
    ds1_got = swap(ds1, "batch", 1)
    other, own = input_back(sz, place, ds1, one)
    ds1_got, ta_got, other, own = after(ds1_got, ta_got, other, own)
    dk_one = kernel_grads(sz, (xt, xt_far), (ds1, ds1_got), (ta_grad, ta_got))
    moved = lax.all_to_all(
        owners(dk_one, nb // 2, frames).reshape((nb // 2 * frames, dk_one.shape[1], -1, 128)),
        ("batch", "tm"), 0, 0, tiled=True,
        axis_index_groups=[[i * frames + j for i in g for j in range(frames)] for g in parities],
    )
    sum_two, own, _ = after(sum_two, own, dk_one)
    grad_s, grad_l = from_rows(own_dpre + scatter_tm(own, other))
    grad_sb, grad_tb = unpack(spread_tm(sum_two)[None])

    n13 = jnp.stack([n1, n3], axis=1)
    n13 = pair(n13, swap(n13, "tm", 2), t // 2)
    n13 = jnp.swapaxes(pair(n13, swap(n13, "tm", 1), t % 2), 0, 1).reshape((frames, 4, 384))
    moved, grad_sb, grad_tb, n13 = after(moved, grad_sb, grad_tb, n13)
    grad_sa, grad_ta = unpack(moved.reshape((nb // 2, frames) + moved.shape[1:]))
    mids = all_channels(n13).reshape(2, 2, -1)
    return (
        out_s, out_l, grad_s, grad_l, grad_sa, grad_ta, grad_sb, grad_tb,
        mids[0], mids[1], jnp.stack([n2[0], n4[0]]), jnp.stack([n2[1], n4[1]]),
    )


def solution(mesh):
    act = P("batch", "tm", None, None, None)
    rows = P(None, ("batch", "tm"), None)
    cols = P(None, None, ("batch", "tm"))
    return jax.shard_map(
        body,
        mesh=mesh,
        in_specs=(act, act, rows, cols, rows, cols, P(), P(), P(), P(), act, act),
        out_specs=(act, act, act, act, rows, cols, rows, cols, P(), P(), P(), P()),
        check_vma=False,
    )
```
